128 devices in a mesh: cp: 8 (over z_lo, y), dp: 16 (over z_hi, x, core).
Axes of the slice: x: 4, y: 4, z: 4 (z_hi: 2, z_lo: 2; z = z_hi * 2 + z_lo), core: 2. Of those that a mesh axis runs over, the one named last changes fastest.
Arguments:
- hidden_in: bfloat16 [16, 1024, 4096], P('dp', 'cp'), may hold values from -6 to 6
- out_grad: bfloat16 [16, 1024, 4096], P('dp', 'cp'), may hold values from -6 to 6
- queries: bfloat16 [16, 1024, 4096], P('dp', 'cp'), may hold values from -5 to 5
- keys: bfloat16 [16, 1024, 256], P('dp', 'cp'), may hold values from -5 to 5
- values: bfloat16 [16, 1024, 256], P('dp', 'cp'), may hold values from -6 to 6
- out_proj: bfloat16 [4096, 4096], P('cp', 'dp'), may hold values from -0.09375 to 0.09375
- expert_ids: int32 [16, 1024, 2], P('dp', 'cp'), may hold values from 0 to 63, all different within a row; in each aligned block of 128 rows (0 to 127, 128 to 255, ..., all dimensions but the last counted through in order) at most 5 rows name the same one
- gate_probs: float32 [16, 1024, 2], P('dp', 'cp'), may hold values from 0.2 to 1
- w_gate: bfloat16 [128, 4096, 768], P(('cp', 'dp')), may hold values from -0.09375 to 0.09375
- w_up: bfloat16 [128, 4096, 768], P(('cp', 'dp')), may hold values from -0.09375 to 0.09375
- w_down: bfloat16 [128, 768, 4096], P(('cp', 'dp')), may hold values from -0.15625 to 0.15625
Outputs:
- resid_grad: bfloat16 [16, 1024, 4096], P('dp', 'cp')
- query_grad: bfloat16 [16, 1024, 4096], P('dp', 'cp')
- key_grad: bfloat16 [16, 1024, 256], P('dp', 'cp')
- value_grad: bfloat16 [16, 1024, 256], P('dp', 'cp')
The draws below stay inside these ranges and needn't reach their ends.
Inputs may be any that keep to these rules, and one draw needn't show every extreme that they name: `expert_ids`: each token names 2 different experts; among the 128 tokens of one device (aligned blocks of the sequence) no expert is named more than 5 times, a bound that some block reaches.
All inputs are finite; a program needn't handle non-finite values.
Results may differ from the reference program's by a relative error of at most 0.028.
Values may be sent and summed in bfloat16 or wider, within the bound.
No kernel may reach another device: no remote copies, remote signals or barrier semaphores. Data moves between devices by JAX's collectives and lax.ppermute only.
A program may use at most 192 MiB of HBM per device.

```python
import math
import jax
import jax.numpy as jnp
import numpy as np
from jax import lax

D = 4096
FF = 1536
HALF = 768
QUERY_HEADS = 32
KEY_VALUE_HEADS = 2
HEAD_SIZE = 128
TOPK = 2
TOK_DEV = 128
SEQUENCE_TOKENS = 1024
SEQUENCE_COUNT = 16
EXPERTS = 64
MOST = 5
CAP = 640


def draw_queries(key, part):
    key = jax.random.fold_in(key, 7)
    return jax.random.truncated_normal(key, -5.0, 5.0, (SEQUENCE_COUNT, SEQUENCE_TOKENS, QUERY_HEADS * HEAD_SIZE), jnp.float32).astype(jnp.bfloat16)


def draw_keys(key, part):
    key = jax.random.fold_in(key, 9)
    return jax.random.truncated_normal(key, -5.0, 5.0, (SEQUENCE_COUNT, SEQUENCE_TOKENS, KEY_VALUE_HEADS * HEAD_SIZE), jnp.float32).astype(jnp.bfloat16)


def levels(rng, dims, cuts, least, top_value):
    def one(axis_at, shards_of):
        heights = jax.random.uniform(jax.random.fold_in(jax.random.fold_in(rng, 6), axis_at), (shards_of,), jnp.float32, least / len(cuts), top_value / len(cuts))
        return jnp.repeat(jnp.exp(heights), dims[axis_at] // shards_of).reshape((-1,) + (1,) * (len(dims) - axis_at - 1))

    gain = one(*cuts[0])
    for cut in cuts[1:]:
        gain = gain * one(*cut)
    return gain


def routed_block(own_key, own, number, rows, amount, top, reach, lean):
    order = jax.random.permutation(own_key, amount)
    heavy_load, usual = load_shares(amount, rows * top, reach, lean, True), load_shares(amount, rows * top, reach, lean, False)
    places = jnp.arange(amount)

    def named(lengths, offset_by):
        used = int((lengths > 0).sum())
        fixed = max(1, used // 4)
        passed = fixed + (places - fixed + offset_by * (used - fixed)) % max(1, amount - fixed)
        return jnp.zeros((amount,), jnp.int32).at[order[jnp.where(places < fixed, places, passed)]].set(jnp.asarray(lengths, jnp.int32))

    lengths = jnp.where(number % 4 == 0, named(heavy_load, number // 4), named(usual, number - number // 4 - 1))
    mixed = jax.random.permutation(jax.random.fold_in(own, 3), amount)
    source_of, receiver = mixed[0:amount // 2 * 2:2], mixed[1:amount // 2 * 2:2]
    room = jnp.minimum(lengths[source_of] - 1, reach - lengths[receiver]) // 2
    room = jnp.where((source_of == order[0]) | (receiver == order[0]) | (lengths[receiver] == 0), 0, jnp.maximum(room, 0))
    passed = jax.random.randint(jax.random.fold_in(own, 4), (amount // 2,), 0, 1 << 20) % (room + 1)
    lengths = lengths.at[source_of].add(-passed).at[receiver].add(passed)
    members = jnp.searchsorted(jnp.cumsum(lengths), jnp.arange(rows * top), side="right").astype(jnp.int32)
    listing = members.reshape(top, rows).T
    listing = listing[jax.random.permutation(jax.random.fold_in(own, 1), rows)]
    offset_by = jax.random.randint(jax.random.fold_in(own, 2), (rows, 1), 0, top)
    return jnp.take_along_axis(listing, (jnp.arange(top)[None, :] + offset_by) % top, axis=1)


def load_shares(count, total, most, lean, full):
    portions = [(1 << 20) // math.isqrt(grade ** lean) + 1 for grade in range(1, count + 1)]
    largest = most if full else min(most, max(-(-total // count), total * portions[0] // sum(portions)))
    least = 1 if total - largest >= count - 1 else 0
    counts, spare = [largest] + [least] * (count - 1), total - largest - least * (count - 1)
    while spare > 0:
        candidates = [i for i in range(1, count) if counts[i] < largest] or [i for i in range(1, count) if counts[i] < most]
        mass, remaining = sum([portions[i] for i in candidates]), spare
        for i in candidates:
            addition = min(most - counts[i], max(1, remaining * portions[i] // mass), spare)
            counts[i] = counts[i] + addition
            spare = spare - addition
    return np.array(counts)


def noise(key, dims, width, most, pieces=(), held_as=jnp.bfloat16):
    values = jax.random.normal(key, dims, jnp.float32) * width
    if len(pieces) > 0:
        values = levels(key, dims, pieces, -0.22, 0.18) * values
    return jnp.clip(values, min=-most, max=most).astype(held_as)


def setup_inputs(seed: int = 0) -> dict:
    key_of = jax.random.split(jax.random.key(seed), 12)
    hidden_in = noise(key_of[0], (SEQUENCE_COUNT, SEQUENCE_TOKENS, D), 1.0, 6.0, ((0, 16), (1, 8)))
    out_grad = noise(key_of[1], (SEQUENCE_COUNT, SEQUENCE_TOKENS, D), 1.0, 6.0, ((0, 16), (1, 8)))
    queries = draw_queries(jax.random.fold_in(key_of[11], 71), 0)
    keys = draw_keys(jax.random.fold_in(key_of[11], 71), 0)
    values = noise(key_of[4], (SEQUENCE_COUNT, SEQUENCE_TOKENS, KEY_VALUE_HEADS * HEAD_SIZE), 1.0, 6.0, ((0, 16), (1, 8)))
    out_proj = noise(key_of[5], (QUERY_HEADS * HEAD_SIZE, D), (QUERY_HEADS * HEAD_SIZE) ** -0.5, 0.09375, ((0, 8), (1, 16)))
    expert_ids_keys = jax.random.split(jax.random.fold_in(key_of[6], 1), SEQUENCE_COUNT * SEQUENCE_TOKENS // TOK_DEV)
    expert_ids_turns = jax.random.permutation(jax.random.fold_in(key_of[6], 3), SEQUENCE_COUNT * SEQUENCE_TOKENS // TOK_DEV)
    expert_ids = jax.vmap(lambda own, number: routed_block(jax.random.fold_in(key_of[6], 2), own, number, TOK_DEV, EXPERTS, TOPK, MOST, 2))(expert_ids_keys, expert_ids_turns).reshape((SEQUENCE_COUNT, SEQUENCE_TOKENS, TOPK))
    gate_probs = jnp.clip(0.2 + 0.8 * jax.random.uniform(key_of[7], (SEQUENCE_COUNT, SEQUENCE_TOKENS, TOPK), jnp.float32) ** levels(key_of[7], (SEQUENCE_COUNT, SEQUENCE_TOKENS, TOPK), ((0, 16), (1, 8)), -0.2, 0.2), 0.2, 1.0)
    w_gate = noise(key_of[8], (2 * EXPERTS, D, HALF), D ** -0.5, 0.09375, ((0, 128),))
    w_up = noise(key_of[9], (2 * EXPERTS, D, HALF), D ** -0.5, 0.09375, ((0, 128),))
    w_down = noise(key_of[10], (2 * EXPERTS, HALF, D), FF ** -0.5, 0.15625, ((0, 128),))
    return {"hidden_in": hidden_in, "out_grad": out_grad, "queries": queries, "keys": keys, "values": values, "out_proj": out_proj, "expert_ids": expert_ids, "gate_probs": gate_probs, "w_gate": w_gate, "w_up": w_up, "w_down": w_down}


def expert_back(rows_in, grads_in, gate_mat, up_mat, down_mat):
    pre_gate = jnp.dot(rows_in, gate_mat, preferred_element_type=jnp.float32)
    pre_up = jnp.dot(rows_in, up_mat, preferred_element_type=jnp.float32)
    upstream = lax.dot_general(grads_in, down_mat, (((1,), (1,)), ((), ())), preferred_element_type=jnp.float32)
    sigmoid_gate = jax.nn.sigmoid(pre_gate)
    d_gate = (upstream * pre_up * sigmoid_gate * (1.0 + pre_gate * (1.0 - sigmoid_gate))).astype(jnp.bfloat16)
    d_up = (upstream * pre_gate * sigmoid_gate).astype(jnp.bfloat16)
    back_gate = lax.dot_general(d_gate, gate_mat, (((1,), (1,)), ((), ())), preferred_element_type=jnp.float32)
    back_up = lax.dot_general(d_up, up_mat, (((1,), (1,)), ((), ())), preferred_element_type=jnp.float32)
    return back_gate + back_up


def reference(hidden_in, out_grad, queries, keys, values, out_proj, expert_ids, gate_probs, w_gate, w_up, w_down):
    experts = w_gate.shape[0] // 2
    route_count = SEQUENCE_COUNT * SEQUENCE_TOKENS * TOPK
    flat_ids = expert_ids.reshape(route_count).astype(jnp.int32)
    flat_probs = gate_probs.reshape(route_count)
    rows_all = hidden_in.reshape(SEQUENCE_COUNT * SEQUENCE_TOKENS, D)
    grads_all = out_grad.reshape(SEQUENCE_COUNT * SEQUENCE_TOKENS, D)
    order = jnp.arange(route_count, dtype=jnp.int32)

    def one_expert(total, expert):
        score = (jnp.where(flat_ids == expert, route_count, 0) - order).astype(jnp.int32)
        unused, picked = lax.top_k(score, CAP)
        picked = picked.astype(jnp.int32)
        valid = flat_ids[picked] == expert
        token_index = (picked // TOPK).astype(jnp.int32)
        gate_mat = jnp.concatenate([w_gate[2 * expert], w_gate[2 * expert + 1]], axis=1)
        up_mat = jnp.concatenate([w_up[2 * expert], w_up[2 * expert + 1]], axis=1)
        down_mat = jnp.concatenate([w_down[2 * expert], w_down[2 * expert + 1]], axis=0)
        back = expert_back(rows_all[token_index], grads_all[token_index], gate_mat, up_mat, down_mat)
        weight = jnp.where(valid, flat_probs[picked], jnp.zeros_like(flat_probs[picked]))
        return total.at[token_index].add(back * weight[:, None]), None

    moe_total, unused_out = lax.scan(one_expert, jnp.zeros((SEQUENCE_COUNT * SEQUENCE_TOKENS, D), jnp.float32), jnp.arange(experts, dtype=jnp.int32))
    resid = (grads_all.astype(jnp.float32) + moe_total).astype(jnp.bfloat16)
    ctx_grad = jnp.dot(resid, out_proj.T, preferred_element_type=jnp.float32).astype(jnp.bfloat16)
    ctx_grad = ctx_grad.reshape(SEQUENCE_COUNT, SEQUENCE_TOKENS, QUERY_HEADS * HEAD_SIZE)
    query_group_count = QUERY_HEADS // KEY_VALUE_HEADS
    scale = HEAD_SIZE ** -0.5

    def one_sequence(inputs):
        query_seq, key_sequence, value_sequence, ctx_seq = inputs
        query_f = query_seq.reshape(SEQUENCE_TOKENS, QUERY_HEADS, HEAD_SIZE).astype(jnp.float32)
        key_float_rows = jnp.repeat(key_sequence.reshape(SEQUENCE_TOKENS, KEY_VALUE_HEADS, HEAD_SIZE), query_group_count, axis=1).astype(jnp.float32)
        value_float_rows = jnp.repeat(value_sequence.reshape(SEQUENCE_TOKENS, KEY_VALUE_HEADS, HEAD_SIZE), query_group_count, axis=1).astype(jnp.float32)
        ctx_f = ctx_seq.reshape(SEQUENCE_TOKENS, QUERY_HEADS, HEAD_SIZE).astype(jnp.float32)
        scores = jnp.einsum('qhd,khd->hqk', query_f, key_float_rows) * scale
        causal = jnp.arange(SEQUENCE_TOKENS)[None, :] <= jnp.arange(SEQUENCE_TOKENS)[:, None]
        scores = jnp.where(causal[None], scores, -1e30)
        highest = jnp.max(scores, axis=-1, keepdims=True)
        probs = jnp.exp(scores - highest)
        probs = probs / jnp.sum(probs, axis=-1, keepdims=True)
        probs_low = probs.astype(jnp.bfloat16)
        dprobs = jnp.einsum('qhd,khd->hqk', ctx_f, value_float_rows)
        delta = jnp.sum(probs * dprobs, axis=-1, keepdims=True)
        dscores = (probs * (dprobs - delta)).astype(jnp.bfloat16).astype(jnp.float32)
        query_out = (jnp.einsum('hqk,khd->qhd', dscores, key_float_rows) * scale).astype(jnp.bfloat16).reshape(SEQUENCE_TOKENS, QUERY_HEADS * HEAD_SIZE)
        key_gradient_out = jnp.einsum('hqk,qhd->khd', dscores, query_f) * scale
        key_gradient_out = jnp.sum(key_gradient_out.reshape(SEQUENCE_TOKENS, KEY_VALUE_HEADS, query_group_count, HEAD_SIZE), axis=2).astype(jnp.bfloat16).reshape(SEQUENCE_TOKENS, KEY_VALUE_HEADS * HEAD_SIZE)
        value_gradient_out = jnp.einsum('hqk,qhd->khd', probs_low.astype(jnp.float32), ctx_f)
        value_gradient_out = jnp.sum(value_gradient_out.reshape(SEQUENCE_TOKENS, KEY_VALUE_HEADS, query_group_count, HEAD_SIZE), axis=2).astype(jnp.bfloat16).reshape(SEQUENCE_TOKENS, KEY_VALUE_HEADS * HEAD_SIZE)
        return query_out, key_gradient_out, value_gradient_out

    query_grad, key_grad, value_grad = lax.map(one_sequence, (queries, keys, values, ctx_grad))
    return resid.reshape(SEQUENCE_COUNT, SEQUENCE_TOKENS, D), query_grad, key_grad, value_grad
```

```python
import jax
import jax.numpy as jnp
from jax import lax
from jax.experimental import pallas as pl
from jax.experimental.pallas import tpu as pltpu
from jax.sharding import Mesh
from jax.sharding import PartitionSpec as P

HEAD_SIZE = 128
GROUPS = 2
CHIPS = ("zlo", "y", "zhi", "x")
SEQ = ("zlo", "y")
HIDDEN_TILE = 256
NT = (((1,), (1,)), ((), ()))
TN = (((0,), (0,)), ((), ()))
F32 = jnp.float32
BF16 = jnp.bfloat16


def expert_kernel(rows, grads, g0, u0, d0, g1, u1, d1, out, total):
    step = pl.program_id(0)
    half_steps = pl.num_programs(0) // 2
    width = rows.shape[1]
    tile = 512

    @pl.when(step == 0)
    def _():
        total[...] = jnp.zeros_like(total)

    def part(gate, up, down):
        zero = jnp.zeros((rows.shape[0], HIDDEN_TILE), F32)

        def add(i, carry):
            pre_gate, pre_up, upstream = carry
            at = pl.ds(pl.multiple_of(i * tile, tile), tile)
            row_block = rows[:, at]
            pre_gate = pre_gate + jnp.dot(row_block, gate[0, at, :], preferred_element_type=F32)
            pre_up = pre_up + jnp.dot(row_block, up[0, at, :], preferred_element_type=F32)
            upstream = upstream + lax.dot_general(
                grads[:, at], down[0, :, at], NT, preferred_element_type=F32
            )
            return pre_gate, pre_up, upstream

        pre_gate, pre_up, upstream = lax.fori_loop(0, width // tile, add, (zero, zero, zero))
        sig = jax.nn.sigmoid(pre_gate)
        d_gate = (upstream * pre_up * sig * (1.0 + pre_gate * (1.0 - sig))).astype(BF16)
        d_up = (upstream * pre_gate * sig).astype(BF16)

        @pl.loop(0, width // tile)
        def _(i):
            at = pl.ds(pl.multiple_of(i * tile, tile), tile)
            total[:, at] += lax.dot_general(
                d_gate, gate[0, at, :], NT, preferred_element_type=F32
            ) + lax.dot_general(d_up, up[0, at, :], NT, preferred_element_type=F32)

    @pl.when(step < half_steps)
    def _():
        part(g0, u0, d0)

    @pl.when(step >= half_steps)
    def _():
        part(g1, u1, d1)

    @pl.when(step == 2 * half_steps - 1)
    def _():
        out[...] = total[...].astype(BF16)


def expert_back(rows, grads, own, other):
    count, width = rows.shape
    half = own[0].shape[2]
    steps = half // HIDDEN_TILE

    def own_at(i):
        return jnp.minimum(i, steps - 1)

    def other_at(i):
        return jnp.maximum(i - steps, 0)

    in_specs = [
        pl.BlockSpec((count, width), lambda i: (0, 0)),
        pl.BlockSpec((count, width), lambda i: (0, 0)),
    ]
    for at in (own_at, other_at):
        in_specs += [
            pl.BlockSpec((1, width, HIDDEN_TILE), lambda i, at=at: (0, 0, at(i))),
            pl.BlockSpec((1, width, HIDDEN_TILE), lambda i, at=at: (0, 0, at(i))),
            pl.BlockSpec((1, HIDDEN_TILE, width), lambda i, at=at: (0, at(i), 0)),
        ]
    return pl.pallas_call(
        expert_kernel,
        grid=(2 * steps,),
        in_specs=in_specs,
        out_specs=pl.BlockSpec((count, width), lambda i: (0, 0)),
        out_shape=jax.ShapeDtypeStruct((count, width), BF16),
        scratch_shapes=[pltpu.VMEM((count, width), F32)],
        compiler_params=pltpu.CompilerParams(vmem_limit_bytes=56 * 1024 * 1024),
        cost_estimate=pl.CostEstimate(
            flops=20 * count * width * half, bytes_accessed=12 * width * half, transcendentals=0
        ),
        name="expert_back",
    )(rows, grads, *own, *other)


def stack_heads(block):
    heads = block.shape[1] // HEAD_SIZE
    return jnp.concatenate(
        [block[:, h * HEAD_SIZE : (h + 1) * HEAD_SIZE] for h in range(heads)], axis=0
    )


def softmax_kernel(first_row, query, key, probs):
    scale = HEAD_SIZE ** (-0.5)
    tokens = query.shape[0]
    scores = (
        lax.dot_general(stack_heads(query[...]), key[...], NT, preferred_element_type=F32) * scale
    )
    row = lax.broadcasted_iota(jnp.int32, scores.shape, 0) % tokens + first_row[0]
    col = lax.broadcasted_iota(jnp.int32, scores.shape, 1)
    scores = jnp.where(col <= row, scores, -1e30)
    weights = jnp.exp(scores - jnp.max(scores, axis=1, keepdims=True))
    probs[...] = (weights / jnp.sum(weights, axis=1, keepdims=True)).astype(BF16)


def softmax_probs(first_row, queries, kv, block_heads):
    tokens, width = queries.shape
    length = kv.shape[0]
    rows = block_heads * tokens
    steps = width // (block_heads * HEAD_SIZE)
    return pl.pallas_call(
        softmax_kernel,
        grid=(steps,),
        in_specs=[
            pl.BlockSpec(memory_space=pltpu.SMEM),
            pl.BlockSpec((tokens, block_heads * HEAD_SIZE), lambda i: (0, i)),
            pl.BlockSpec((length, HEAD_SIZE), lambda i: (0, i * GROUPS // steps)),
        ],
        out_specs=pl.BlockSpec((rows, length), lambda i: (i, 0)),
        out_shape=jax.ShapeDtypeStruct((steps * rows, length), BF16),
        compiler_params=pltpu.CompilerParams(vmem_limit_bytes=48 * 1024 * 1024),
        cost_estimate=pl.CostEstimate(
            flops=20 * steps * rows * length * HEAD_SIZE,
            bytes_accessed=2 * steps * rows * length,
            transcendentals=steps * rows * length,
        ),
        name="softmax_probs",
    )(first_row, queries, kv)


def attention_kernel(core, resid, own, other, query, probs, key, value, dquery, dkv, dkey, dvalue):
    step = pl.program_id(0)
    scale = HEAD_SIZE ** (-0.5)
    tokens = resid.shape[0]
    pieces, block_cols, depth = own.shape[1:]

    @pl.when(step == 0)
    def _():
        dkey[...] = jnp.zeros_like(dkey)
        dvalue[...] = jnp.zeros_like(dvalue)

    ctx = jnp.zeros((tokens, block_cols), F32)
    for side, shard in ((core[0], own), (1 - core[0], other)):
        for piece in range(pieces):
            at = pl.ds(pl.multiple_of((2 * piece + side) * depth, depth), depth)
            ctx = ctx + lax.dot_general(
                resid[:, at], shard[0, piece], NT, preferred_element_type=F32
            )
    ctx = stack_heads(ctx.astype(BF16))
    query_rows = stack_heads(query[...])
    low = probs[...]
    weights = low.astype(F32)
    dprobs = lax.dot_general(ctx, value[...], NT, preferred_element_type=F32)
    delta = jnp.sum(weights * dprobs, axis=1, keepdims=True)
    dscores = (weights * (dprobs - delta)).astype(BF16)
    dq = jnp.dot(dscores, key[...], preferred_element_type=F32) * scale
    for h in range(block_cols // HEAD_SIZE):
        dquery[:, h * HEAD_SIZE : (h + 1) * HEAD_SIZE] = dq[h * tokens : (h + 1) * tokens].astype(
            BF16
        )
    dkey[...] += lax.dot_general(query_rows, dscores, TN, preferred_element_type=F32)
    dvalue[...] += lax.dot_general(ctx, low, TN, preferred_element_type=F32)

    @pl.when(step == pl.num_programs(0) - 1)
    def _():
        dkv[:, :HEAD_SIZE] = jnp.transpose(dkey[...] * scale).astype(BF16)
        dkv[:, HEAD_SIZE:] = jnp.transpose(dvalue[...]).astype(BF16)


def attention_back(group, core, resid, own, other, queries, probs, kv):
    tokens, width = resid.shape
    blocks, pieces, block_cols, depth = own.shape
    length = kv.shape[0]
    steps = blocks // GROUPS
    first = group * steps
    rows = tokens * block_cols // HEAD_SIZE
    return pl.pallas_call(
        attention_kernel,
        grid=(steps,),
        in_specs=[
            pl.BlockSpec(memory_space=pltpu.SMEM),
            pl.BlockSpec((tokens, width), lambda i: (0, 0)),
            pl.BlockSpec((1, pieces, block_cols, depth), lambda i: (first + i, 0, 0, 0)),
            pl.BlockSpec((1, pieces, block_cols, depth), lambda i: (first + i, 0, 0, 0)),
            pl.BlockSpec((tokens, block_cols), lambda i: (0, first + i)),
            pl.BlockSpec((rows, length), lambda i: (first + i, 0)),
            pl.BlockSpec((length, HEAD_SIZE), lambda i: (0, group)),
            pl.BlockSpec((length, HEAD_SIZE), lambda i: (0, GROUPS + group)),
        ],
        out_specs=[
            pl.BlockSpec((tokens, block_cols), lambda i: (0, i)),
            pl.BlockSpec((length, 2 * HEAD_SIZE), lambda i: (0, 0)),
        ],
        out_shape=[
            jax.ShapeDtypeStruct((tokens, steps * block_cols), BF16),
            jax.ShapeDtypeStruct((length, 2 * HEAD_SIZE), BF16),
        ],
        scratch_shapes=[pltpu.VMEM((HEAD_SIZE, length), F32)] * 2,
        compiler_params=pltpu.CompilerParams(vmem_limit_bytes=56 * 1024 * 1024),
        cost_estimate=pl.CostEstimate(
            flops=2 * steps * rows * (5 * length * HEAD_SIZE + width * HEAD_SIZE),
            bytes_accessed=steps * (2 * width * block_cols + 2 * rows * length),
            transcendentals=0,
        ),
        name="attention_back",
    )(core, resid, own, other, queries, probs, kv, kv)


def to_chips(rows, chips):
    width = rows.shape[1]
    sent = rows.reshape(chips, -1, width)
    return lax.all_to_all(sent, CHIPS, split_axis=0, concat_axis=0, tiled=True).reshape(-1, width)


def other_core(block):
    return lax.ppermute(block, "core", [(0, 1), (1, 0)])


def body(
    hidden_in,
    out_grad,
    queries,
    keys,
    values,
    out_proj,
    expert_ids,
    gate_probs,
    w_gate,
    w_up,
    w_down,
):
    tokens, width = hidden_in.shape[1:]
    top_count = expert_ids.shape[2]
    chips = lax.axis_size(CHIPS)
    experts = chips
    cp_count = lax.axis_size(SEQ)
    capacity = 5
    slots = experts * capacity
    core = lax.axis_index("core").astype(jnp.int32).reshape(1)
    first_row = (lax.axis_index(SEQ) * tokens).astype(jnp.int32).reshape(1)
    own = (w_gate, w_up, w_down)
    other = tuple(other_core(w) for w in own)
    kv = lax.all_gather(jnp.concatenate([keys[0], values[0]], axis=1), SEQ, axis=0, tiled=True)
    proj_own = lax.all_gather(out_proj, CHIPS, axis=0, tiled=False)
    proj_own = proj_own.reshape(cp_count, chips // cp_count, *out_proj.shape)
    proj_other = other_core(proj_own)

    flat_ids = expert_ids.reshape(tokens * top_count)
    hot = (flat_ids[:, None] == jnp.arange(experts, dtype=jnp.int32)[None, :]).astype(jnp.int32)
    earlier = jnp.cumsum(hot, axis=0) - hot
    slot_index = flat_ids * capacity + jnp.sum(earlier * hot, axis=1)
    slot_hot = slot_index.reshape(tokens, top_count, 1) == jnp.arange(slots, dtype=jnp.int32)
    picking = jnp.sum(slot_hot.astype(BF16), axis=1).T
    mixing = jnp.sum(jnp.where(slot_hot, gate_probs[0][:, :, None], 0.0), axis=1)
    mixing_high = mixing.astype(BF16)
    mixing_low = (mixing - mixing_high.astype(F32)).astype(BF16)
    mixing_both = jnp.concatenate([mixing_high, mixing_low], axis=0)

    rows = jnp.dot(picking, hidden_in[0], preferred_element_type=F32).astype(BF16)
    grads = jnp.dot(picking, out_grad[0], preferred_element_type=F32).astype(BF16)
    rows = to_chips(rows, chips)
    grads = to_chips(grads, chips)
    probs = softmax_probs(first_row, queries[0], kv, out_proj.shape[0] // HEAD_SIZE)
    back = expert_back(rows, grads, own, other)
    result = to_chips(back, chips)
    mixed = jnp.dot(mixing_both, result, preferred_element_type=F32)
    resid = (out_grad[0].astype(F32) + (mixed[:tokens] + mixed[tokens:])).astype(BF16)

    query_parts = []
    key_parts = []
    value_parts = []
    for group in range(GROUPS):
        dquery, dkv = attention_back(
            group, core, resid, proj_own, proj_other, queries[0], probs, kv
        )
        parts = lax.all_to_all(
            dkv.reshape(cp_count, tokens, 2 * HEAD_SIZE), SEQ, split_axis=0, concat_axis=0, tiled=True
        )
        dkv_sum = jnp.sum(parts.astype(F32), axis=0).astype(BF16)
        query_parts.append(dquery)
        key_parts.append(dkv_sum[:, :HEAD_SIZE])
        value_parts.append(dkv_sum[:, HEAD_SIZE:])
    return (
        resid[None],
        jnp.concatenate(query_parts, axis=1)[None],
        jnp.concatenate(key_parts, axis=1)[None],
        jnp.concatenate(value_parts, axis=1)[None],
    )


def solution(mesh):
    fine = Mesh(mesh.devices.reshape(2, 4, 2, 4, 2), ("zlo", "y", "zhi", "x", "core"))
    dp = ("zhi", "x", "core")
    token_spec = P(dp, SEQ, None)
    weight_spec = P((*SEQ, *dp), None, None)
    return jax.shard_map(
        body,
        mesh=fine,
        in_specs=(token_spec,) * 5
        + (P(SEQ, dp), token_spec, token_spec, weight_spec, weight_spec, weight_spec),
        out_specs=(token_spec,) * 4,
        check_vma=False,
    )
```

```python
import functools

import jax
import jax.numpy as jnp
from jax import lax
from jax.experimental import pallas as pl
from jax.experimental.pallas import tpu as pltpu
from jax.sharding import Mesh
from jax.sharding import PartitionSpec as P

HEAD_SIZE = 128
GROUPS = 2
CHIPS = ("zlo", "y", "zhi", "x")
SEQ = ("zlo", "y")
HIDDEN_TILE = 256
NT = (((1,), (1,)), ((), ()))
TN = (((0,), (0,)), ((), ()))
F32 = jnp.float32
BF16 = jnp.bfloat16


def expert_kernel(rows, grads, g0, u0, d0, g1, u1, d1, out, gate, up, down, d_gate, d_up, sems):
    halves, width, half = gate.shape
    tile = 512
    loads = []
    for h, (g, u, d) in enumerate(((g0, u0, d0), (g1, u1, d1))):
        for at in range(0, half, HIDDEN_TILE):
            part = slice(at, at + HIDDEN_TILE)
            copies = [
                pltpu.make_async_copy(g.at[0, :, part], gate.at[h, :, part], sems.at[len(loads), 0]),
                pltpu.make_async_copy(u.at[0, :, part], up.at[h, :, part], sems.at[len(loads), 1]),
                pltpu.make_async_copy(d.at[0, part, :], down.at[h, part, :], sems.at[len(loads), 2]),
            ]
            for copy in copies:
                copy.start()
            loads.append((h, part, copies))
    for h, part, copies in loads:
        for copy in copies:
            copy.wait()
        pre_gate = jnp.dot(rows[...], gate[h, :, part], preferred_element_type=F32)
        pre_up = jnp.dot(rows[...], up[h, :, part], preferred_element_type=F32)
        upstream = lax.dot_general(grads[...], down[h, part, :], NT, preferred_element_type=F32)
        sig = jax.nn.sigmoid(pre_gate)
        d_gate[h, :, part] = (upstream * pre_up * sig * (1.0 + pre_gate * (1.0 - sig))).astype(BF16)
        d_up[h, :, part] = (upstream * pre_gate * sig).astype(BF16)

    @pl.loop(0, width // tile)
    def _(i):
        at = pl.ds(pl.multiple_of(i * tile, tile), tile)
        total = lax.dot_general(d_gate[0], gate[0, at, :], NT, preferred_element_type=F32)
        total += lax.dot_general(d_up[0], up[0, at, :], NT, preferred_element_type=F32)
        for h in range(1, halves):
            total += lax.dot_general(d_gate[h], gate[h, at, :], NT, preferred_element_type=F32)
            total += lax.dot_general(d_up[h], up[h, at, :], NT, preferred_element_type=F32)
        out[:, at] = total.astype(BF16)


def expert_back(rows, grads, own, other):
    count, width = rows.shape
    half = own[0].shape[2]
    held = pl.BlockSpec(memory_space=pltpu.VMEM)
    far = pl.BlockSpec(memory_space=pl.ANY)
    return pl.pallas_call(
        expert_kernel,
        in_specs=[held, held] + [far] * 6,
        out_specs=held,
        out_shape=jax.ShapeDtypeStruct((count, width), BF16),
        scratch_shapes=[
            pltpu.VMEM((2, width, half), BF16),
            pltpu.VMEM((2, width, half), BF16),
            pltpu.VMEM((2, half, width), BF16),
            pltpu.VMEM((2, count, half), BF16),
            pltpu.VMEM((2, count, half), BF16),
            pltpu.SemaphoreType.DMA((2 * half // HIDDEN_TILE, 3)),
        ],
        compiler_params=pltpu.CompilerParams(vmem_limit_bytes=60 * 1024 * 1024),
        cost_estimate=pl.CostEstimate(
            flops=20 * count * width * half, bytes_accessed=12 * width * half, transcendentals=0
        ),
        name="expert_back",
    )(rows, grads, *own, *other)


def stack_heads(block):
    heads = block.shape[1] // HEAD_SIZE
    return jnp.concatenate(
        [block[:, h * HEAD_SIZE : (h + 1) * HEAD_SIZE] for h in range(heads)], axis=0
    )


def softmax_kernel(first_row, query, key, probs):
    scale = HEAD_SIZE ** (-0.5)
    tokens = query.shape[0]
    scores = jnp.dot(stack_heads(query[...]), key[...], preferred_element_type=F32) * scale
    row = lax.broadcasted_iota(jnp.int32, scores.shape, 0) % tokens + first_row[0]
    col = lax.broadcasted_iota(jnp.int32, scores.shape, 1)
    scores = jnp.where(col <= row, scores, -1e30)
    weights = jnp.exp(scores - jnp.max(scores, axis=1, keepdims=True))
    probs[...] = (weights / jnp.sum(weights, axis=1, keepdims=True)).astype(BF16)


def softmax_probs(first_row, queries, key, block_heads):
    tokens, width = queries.shape
    length = key.shape[1]
    rows = block_heads * tokens
    steps = width // (block_heads * HEAD_SIZE)
    return pl.pallas_call(
        softmax_kernel,
        grid=(steps,),
        in_specs=[
            pl.BlockSpec(memory_space=pltpu.SMEM),
            pl.BlockSpec((tokens, block_heads * HEAD_SIZE), lambda i: (0, i)),
            pl.BlockSpec((HEAD_SIZE, length), lambda i: (0, 0)),
        ],
        out_specs=pl.BlockSpec((rows, length), lambda i: (i, 0)),
        out_shape=jax.ShapeDtypeStruct((steps * rows, length), BF16),
        compiler_params=pltpu.CompilerParams(vmem_limit_bytes=48 * 1024 * 1024),
        cost_estimate=pl.CostEstimate(
            flops=20 * steps * rows * length * HEAD_SIZE,
            bytes_accessed=2 * steps * rows * length,
            transcendentals=steps * rows * length,
        ),
        name="softmax_probs",
    )(first_row, queries, key)


def attention_kernel(last, place, resid, a_own, b_own, a_other, b_other, query, probs, key, value_t, *refs):
    if last:
        dkey_in, dvalue_in, dquery, dkv, dkey, dvalue = refs
    else:
        dquery, dkey, dvalue = refs
    core, x_at, zhi_at = place[0], place[1], place[2]
    step = pl.program_id(0)
    scale = HEAD_SIZE ** (-0.5)
    tokens = resid.shape[0]
    x_count, zhi_count, depth = b_own.shape[0], b_own.shape[2], b_own.shape[3]

    @pl.when(step == 0)
    def _():
        if last:
            dkey[...] = dkey_in[...]
            dvalue[...] = dvalue_in[...]
        else:
            dkey[...] = jnp.zeros_like(dkey)
            dvalue[...] = jnp.zeros_like(dvalue)

    first = jnp.zeros((tokens, a_own.shape[4]), F32)
    second = jnp.zeros((tokens, b_own.shape[4]), F32)
    for side, a_part, b_part in ((core, a_own, b_own), (1 - core, a_other, b_other)):
        for r_x in range(x_count):
            for r_z in range(zhi_count):
                x_from = lax.rem(x_at + x_count - r_x, x_count)
                z_from = lax.rem(zhi_at + zhi_count - r_z, zhi_count)
                piece = (z_from * x_count + x_from) * 2 + side
                columns = resid[:, pl.ds(pl.multiple_of(piece * depth, depth), depth)]
                first += jnp.dot(columns, a_part[0, r_x, r_z], preferred_element_type=F32)
                second += jnp.dot(columns, b_part[r_x, 0, r_z], preferred_element_type=F32)
    ctx = jnp.concatenate(
        [stack_heads(first.astype(BF16)), stack_heads(second.astype(BF16))], axis=0
    )
    query_rows = stack_heads(query[...])
    low = probs[...]
    weights = low.astype(F32)
    dprobs = jnp.dot(ctx, value_t[...], preferred_element_type=F32)
    delta = jnp.sum(weights * dprobs, axis=1, keepdims=True)
    dscores = (weights * (dprobs - delta)).astype(BF16)
    dq = jnp.dot(dscores, key[...], preferred_element_type=F32) * scale
    for h in range(query.shape[1] // HEAD_SIZE):
        dquery[:, h * HEAD_SIZE : (h + 1) * HEAD_SIZE] = dq[h * tokens : (h + 1) * tokens].astype(
            BF16
        )
    dkey[...] += lax.dot_general(query_rows, dscores, TN, preferred_element_type=F32)
    dvalue[...] += lax.dot_general(ctx, low, TN, preferred_element_type=F32)

    if last:

        @pl.when(step == pl.num_programs(0) - 1)
        def _():
            dkv[:, :HEAD_SIZE] = jnp.transpose(dkey[...] * scale).astype(BF16)
            dkv[:, HEAD_SIZE:] = jnp.transpose(dvalue[...]).astype(BF16)


def attention_back(place, resid, proj, queries, probs, key, value_t, carried):
    tokens, width = resid.shape
    y_count, x_count, zhi_count, depth, cols = proj[0].shape
    length = key.shape[0]
    block_cols = 2 * cols
    rows = tokens * block_cols // HEAD_SIZE
    last = carried is not None

    def y_of(i, place):
        return lax.rem(place[3] + y_count - i, y_count)

    def whole(*shape):
        return pl.BlockSpec(shape, lambda i, place: (0,) * len(shape))

    a_spec = pl.BlockSpec((1, x_count, zhi_count, depth, cols), lambda i, place: (i, 0, 0, 0, 0))
    b_spec = pl.BlockSpec((x_count, 1, zhi_count, depth, cols), lambda i, place: (0, i, 0, 0, 0))
    block = pl.BlockSpec((tokens, block_cols), lambda i, place: (0, y_of(i, place)))
    in_specs = [
        whole(tokens, width),
        a_spec,
        b_spec,
        a_spec,
        b_spec,
        block,
        pl.BlockSpec((rows, length), lambda i, place: (y_of(i, place), 0)),
        whole(length, HEAD_SIZE),
        whole(HEAD_SIZE, length),
    ]
    sums = jax.ShapeDtypeStruct((HEAD_SIZE, length), F32)
    dquery = jax.ShapeDtypeStruct((tokens, y_count * block_cols), BF16)
    if last:
        in_specs += [whole(HEAD_SIZE, length)] * 2
        out_specs = [block, whole(length, 2 * HEAD_SIZE)]
        out_shape = [dquery, jax.ShapeDtypeStruct((length, 2 * HEAD_SIZE), BF16)]
        scratch = [pltpu.VMEM((HEAD_SIZE, length), F32)] * 2
    else:
        out_specs = [block] + [whole(HEAD_SIZE, length)] * 2
        out_shape = [dquery, sums, sums]
        scratch = []
    return pl.pallas_call(
        functools.partial(attention_kernel, last),
        grid_spec=pltpu.PrefetchScalarGridSpec(
            num_scalar_prefetch=1,
            grid=(y_count,),
            in_specs=in_specs,
            out_specs=out_specs,
            scratch_shapes=scratch,
        ),
        out_shape=out_shape,
        compiler_params=pltpu.CompilerParams(vmem_limit_bytes=56 * 1024 * 1024),
        cost_estimate=pl.CostEstimate(
            flops=2 * y_count * rows * (5 * length * HEAD_SIZE + width * HEAD_SIZE),
            bytes_accessed=y_count * (2 * width * block_cols + 2 * rows * length),
            transcendentals=0,
        ),
        name="attention_back",
    )(place, resid, *proj, queries, probs, key, value_t, *(carried or ()))


def to_chips(rows, chips):
    width = rows.shape[1]
    sent = rows.reshape(chips, -1, width)
    return lax.all_to_all(sent, CHIPS, split_axis=0, concat_axis=0, tiled=True).reshape(-1, width)


def swapped(block, axis):
    return lax.ppermute(block, axis, [(0, 1), (1, 0)])


def shifted(block, axis, by):
    count = lax.axis_size(axis)
    return lax.ppermute(block, axis, [(i, (i + by) % count) for i in range(count)])


def gathered(block, axis):
    return jnp.stack([block] + [shifted(block, axis, k) for k in range(1, lax.axis_size(axis))])


def body(
    hidden_in,
    out_grad,
    queries,
    keys,
    values,
    out_proj,
    expert_ids,
    gate_probs,
    w_gate,
    w_up,
    w_down,
):
    tokens, width = hidden_in.shape[1:]
    top_count = expert_ids.shape[2]
    chips = lax.axis_size(CHIPS)
    experts = chips
    cp_count = lax.axis_size(SEQ)
    capacity = 5
    slots = experts * capacity
    zlo = lax.axis_index("zlo")
    y_at = lax.axis_index("y")
    y_count = lax.axis_size("y")
    place = jnp.stack([lax.axis_index(a) for a in ("core", "x", "zhi", "y")]).astype(jnp.int32)

    flat_ids = expert_ids.reshape(tokens * top_count)
    hot = (flat_ids[:, None] == jnp.arange(experts, dtype=jnp.int32)[None, :]).astype(jnp.int32)
    earlier = jnp.cumsum(hot, axis=0) - hot
    slot_index = flat_ids * capacity + jnp.sum(earlier * hot, axis=1)
    slot_hot = slot_index.reshape(tokens, top_count, 1) == jnp.arange(slots, dtype=jnp.int32)
    picking = jnp.sum(slot_hot.astype(BF16), axis=1).T
    mixing = jnp.sum(jnp.where(slot_hot, gate_probs[0][:, :, None], 0.0), axis=1)
    mixing_high = mixing.astype(BF16)
    mixing_low = (mixing - mixing_high.astype(F32)).astype(BF16)
    mixing_both = jnp.concatenate([mixing_high, mixing_low], axis=0)

    rows = jnp.dot(picking, hidden_in[0], preferred_element_type=F32).astype(BF16)
    grads = jnp.dot(picking, out_grad[0], preferred_element_type=F32).astype(BF16)
    rows = to_chips(rows, chips)
    grads = to_chips(grads, chips)

    own = (w_gate, w_up, w_down)
    other = tuple(swapped(w, "core") for w in own)

    kv = lax.all_gather(jnp.concatenate([keys[0], values[0]], axis=1), SEQ, axis=0, tiled=True)
    key = lax.dynamic_slice_in_dim(kv, zlo * HEAD_SIZE, HEAD_SIZE, 1)
    value = lax.dynamic_slice_in_dim(kv, (GROUPS + zlo) * HEAD_SIZE, HEAD_SIZE, 1)
    key_t, value_t = key.T, value.T
    group_width = width // GROUPS
    own_query = lax.dynamic_slice_in_dim(queries[0], zlo * group_width, group_width, 1)
    near_query = swapped(
        lax.dynamic_slice_in_dim(queries[0], (1 - zlo) * group_width, group_width, 1), "zlo"
    )
    block_heads = out_proj.shape[0] // HEAD_SIZE
    own_row = ((zlo * y_count + y_at) * tokens).astype(jnp.int32).reshape(1)
    near_row = (((1 - zlo) * y_count + y_at) * tokens).astype(jnp.int32).reshape(1)
    own_probs = softmax_probs(own_row, own_query, key_t, block_heads)
    near_probs = softmax_probs(near_row, near_query, key_t, block_heads)

    proj_t = out_proj.T
    cols = proj_t.shape[1] // 2
    proj_a = gathered(gathered(gathered(proj_t[:, :cols], "zhi"), "x"), "y")
    proj_b = gathered(gathered(gathered(proj_t[:, cols:], "zhi"), "y"), "x")
    proj = (proj_a, proj_b, swapped(proj_a, "core"), swapped(proj_b, "core"))

    back = expert_back(rows, grads, own, other)
    result = to_chips(back, chips)
    mixed = jnp.dot(mixing_both, result, preferred_element_type=F32)
    resid = (out_grad[0].astype(F32) + (mixed[:tokens] + mixed[tokens:])).astype(BF16)
    near_resid = swapped(resid, "zlo")

    dquery, dkey, dvalue = attention_back(
        place, resid, proj, own_query, own_probs, key, value_t, None
    )
    near_dquery, dkv = attention_back(
        place, near_resid, proj, near_query, near_probs, key, value_t, (dkey, dvalue)
    )
    far_dquery = swapped(near_dquery, "zlo")
    dquery = jnp.where(
        zlo == 0,
        jnp.concatenate([dquery, far_dquery], axis=1),
        jnp.concatenate([far_dquery, dquery], axis=1),
    )
    parts = lax.all_to_all(
        dkv.reshape(cp_count, tokens, 2 * HEAD_SIZE), SEQ, split_axis=0, concat_axis=0, tiled=True
    )
    parts = parts.reshape(GROUPS, y_count, tokens, 2 * HEAD_SIZE)
    sums = jnp.sum(parts.astype(F32), axis=1).astype(BF16)
    dkey = jnp.concatenate([sums[g, :, :HEAD_SIZE] for g in range(GROUPS)], axis=1)
    dvalue = jnp.concatenate([sums[g, :, HEAD_SIZE:] for g in range(GROUPS)], axis=1)
    return resid[None], dquery[None], dkey[None], dvalue[None]


def solution(mesh):
    fine = Mesh(mesh.devices.reshape(2, 4, 2, 4, 2), ("zlo", "y", "zhi", "x", "core"))
    dp = ("zhi", "x", "core")
    token_spec = P(dp, SEQ, None)
    weight_spec = P((*SEQ, *dp), None, None)
    return jax.shard_map(
        body,
        mesh=fine,
        in_specs=(token_spec,) * 5
        + (P(SEQ, dp), token_spec, token_spec, weight_spec, weight_spec, weight_spec),
        out_specs=(token_spec,) * 4,
        check_vma=False,
    )
```

```python
import functools

import jax
import jax.numpy as jnp
import numpy as np
from jax import lax
from jax.experimental import pallas as pl
from jax.experimental.pallas import tpu as pltpu
from jax.sharding import Mesh
from jax.sharding import PartitionSpec as P

HEAD_SIZE = 128
GROUPS = 2
CAPACITY = 5
SEQ = ("zlo", "y")
RINGS = {"x": ("x", (0, 1, 2, 3)), "y": ("y", (0, 1, 2, 3)), "z": (("zlo", "zhi"), (0, 2, 1, 3))}
RING = 4
ORDERS = (("x", "y", "z"), ("y", "z", "x"), ("z", "x", "y"))
SLOTS = RING**3 * CAPACITY
CHUNK = SLOTS // RING
LANES = 128
HIDDEN_TILE = 256
NT = (((1,), (1,)), ((), ()))
TN = (((0,), (0,)), ((), ()))
F32 = jnp.float32
BF16 = jnp.bfloat16


def bounds_of(width):
    tiles = width // LANES
    edges = [-(-tiles * p // len(ORDERS)) * LANES for p in range(len(ORDERS) + 1)]
    return tuple(zip(edges[:-1], edges[1:]))


def reorder(axes):
    index = np.arange(SLOTS).reshape(RING, RING, RING, CAPACITY)
    moved = index.transpose(*axes, 3).reshape(SLOTS)
    return jnp.asarray(np.eye(SLOTS, dtype=np.float32)[moved], BF16)


def ring(block, axis, by):
    if by % RING == 0:
        return block
    name, number = RINGS[axis]
    return lax.ppermute(block, name, [(number[i], number[(i + by) % RING]) for i in range(RING)])


def route_rows(place, ids):
    tokens, experts = ids.shape[0], RING**3
    lane = lax.broadcasted_iota(jnp.int32, (tokens, experts), 1)
    chosen = [ids[:, k : k + 1] for k in range(ids.shape[1])]
    hots = [jnp.where(lane == e, 1.0, 0.0) for e in chosen]
    before = jnp.where(
        lax.broadcasted_iota(jnp.int32, (tokens, tokens), 1)
        < lax.broadcasted_iota(jnp.int32, (tokens, tokens), 0),
        1.0,
        0.0,
    ).astype(BF16)
    earlier = jnp.dot(before, sum(hots).astype(BF16), preferred_element_type=F32)
    rows = []
    for e, hot in zip(chosen, hots):
        slot = jnp.sum(earlier * hot, axis=1, keepdims=True).astype(jnp.int32)
        z = ((e >> 2) & 1) * 2 + (e >> 5)
        offset = {
            "x": ((e & 3) - place[1]) & 3,
            "y": (((e >> 3) & 3) - place[3]) & 3,
            "z": (z - place[4]) & 3,
        }
        rows.append(
            [
                ((offset[a] * RING + offset[b]) * RING + offset[c]) * CAPACITY + slot
                for a, b, c in ORDERS
            ]
        )
    return rows


def pick_kernel(bounds, place, ids, hidden, grads, *outs):
    rows = route_rows(place, ids)
    lane = lax.broadcasted_iota(jnp.int32, (ids.shape[0], SLOTS), 1)
    for p, (low, high) in enumerate(bounds):
        picking = sum(jnp.where(lane == route[p], 1.0, 0.0) for route in rows).astype(BF16)
        for side, source in enumerate((hidden, grads)):
            picked = lax.dot_general(
                picking, source[:, low:high], TN, preferred_element_type=F32
            ).astype(BF16)
            at = slice(side * (high - low), (side + 1) * (high - low))
            for k in range(RING):
                outs[p * RING + k][:, at] = picked[k * CHUNK : (k + 1) * CHUNK]


def pick(place, ids, hidden, grads):
    bounds = bounds_of(hidden.shape[1])
    held = pl.BlockSpec(memory_space=pltpu.VMEM)
    outs = pl.pallas_call(
        functools.partial(pick_kernel, bounds),
        in_specs=[pl.BlockSpec(memory_space=pltpu.SMEM)] + [held] * 3,
        out_specs=[held] * (RING * len(bounds)),
        out_shape=[
            jax.ShapeDtypeStruct((CHUNK, 2 * (high - low)), BF16)
            for low, high in bounds
            for _ in range(RING)
        ],
        compiler_params=pltpu.CompilerParams(vmem_limit_bytes=48 * 1024 * 1024),
        name="pick",
    )(place, ids, hidden, grads)
    return [outs[p * RING : (p + 1) * RING] for p in range(len(bounds))]


def mix_kernel(p, low, high, place, ids, probs, grads, *refs):
    out = refs[-1]
    lane = lax.broadcasted_iota(jnp.int32, (ids.shape[0], SLOTS), 1)
    mixing = sum(
        jnp.where(lane == route[p], probs[:, k : k + 1], 0.0)
        for k, route in enumerate(route_rows(place, ids))
    )
    mixing_high = mixing.astype(BF16)
    mixing_low = (mixing - mixing_high.astype(F32)).astype(BF16)
    rows = jnp.concatenate([ref[...] for ref in refs[:-1]], axis=0)
    mixed = jnp.dot(mixing_high, rows, preferred_element_type=F32)
    mixed += jnp.dot(mixing_low, rows, preferred_element_type=F32)
    out[...] = (grads[:, low:high].astype(F32) + mixed).astype(BF16)


def mix(p, place, ids, probs, grads, parts):
    low, high = bounds_of(grads.shape[1])[p]
    held = pl.BlockSpec(memory_space=pltpu.VMEM)
    return pl.pallas_call(
        functools.partial(mix_kernel, p, low, high),
        in_specs=[pl.BlockSpec(memory_space=pltpu.SMEM)] + [held] * 7,
        out_specs=held,
        out_shape=jax.ShapeDtypeStruct((grads.shape[0], high - low), BF16),
        compiler_params=pltpu.CompilerParams(vmem_limit_bytes=48 * 1024 * 1024),
        name="mix",
    )(place, ids, probs, grads, *parts)


def regroup_kernel(count, order, *refs):
    parts, outs = refs[:RING], refs[len(refs) - count - RING : len(refs) - count]
    rows = jnp.concatenate([part[...] for part in parts], axis=0)
    moved = jnp.dot(order[...], rows, preferred_element_type=F32).astype(BF16)
    for k, out in enumerate(outs):
        out[...] = moved[k * CHUNK : (k + 1) * CHUNK]


def regroup(order, parts, carried=()):
    held = pl.BlockSpec(memory_space=pltpu.VMEM)
    far = pl.BlockSpec(memory_space=pl.ANY)
    count = len(carried)
    outs = pl.pallas_call(
        functools.partial(regroup_kernel, count),
        in_specs=[held] * (1 + RING) + [far] * count,
        out_specs=[held] * RING + [far] * count,
        out_shape=[jax.ShapeDtypeStruct(a.shape, a.dtype) for a in (*parts, *carried)],
        input_output_aliases={1 + RING + i: RING + i for i in range(count)},
        compiler_params=pltpu.CompilerParams(vmem_limit_bytes=48 * 1024 * 1024),
        name="regroup",
    )(order, *parts, *carried)
    return (outs[:RING], outs[RING:]) if count else outs


def expert_kernel(bounds, turn, back_turn, g0, u0, d0, g1, u1, d1, *refs):
    count = RING * len(bounds)
    parts, outs = refs[:count], refs[count : 2 * count]
    rows, grads, gate, up, down, d_gate, d_up, sems = refs[2 * count :]
    halves, width, half = gate.shape
    tile = 512
    loads = []
    for h, (g, u, d) in enumerate(((g0, u0, d0), (g1, u1, d1))):
        for at in range(0, half, HIDDEN_TILE):
            part = slice(at, at + HIDDEN_TILE)
            copies = [
                pltpu.make_async_copy(g.at[0, :, part], gate.at[h, :, part], sems.at[len(loads), 0]),
                pltpu.make_async_copy(u.at[0, :, part], up.at[h, :, part], sems.at[len(loads), 1]),
                pltpu.make_async_copy(d.at[0, part, :], down.at[h, part, :], sems.at[len(loads), 2]),
            ]
            for copy in copies:
                copy.start()
            loads.append((h, part, copies))
    for p, (low, high) in enumerate(bounds):
        came = jnp.concatenate([ref[...] for ref in parts[p * RING : (p + 1) * RING]], axis=0)
        if p > 0:
            order = (turn if p == 1 else back_turn)[...]
            came = jnp.dot(order, came, preferred_element_type=F32).astype(BF16)
        rows[:, low:high] = came[:, : high - low]
        grads[:, low:high] = came[:, high - low :]
    for h, part, copies in loads:
        for copy in copies:
            copy.wait()
        pre_gate = jnp.dot(rows[...], gate[h, :, part], preferred_element_type=F32)
        pre_up = jnp.dot(rows[...], up[h, :, part], preferred_element_type=F32)
        upstream = lax.dot_general(grads[...], down[h, part, :], NT, preferred_element_type=F32)
        sig = jax.nn.sigmoid(pre_gate)
        d_gate[h, :, part] = (upstream * pre_up * sig * (1.0 + pre_gate * (1.0 - sig))).astype(BF16)
        d_up[h, :, part] = (upstream * pre_gate * sig).astype(BF16)

    @pl.loop(0, width // tile)
    def _(i):
        at = pl.ds(pl.multiple_of(i * tile, tile), tile)
        total = lax.dot_general(d_gate[0], gate[0, at, :], NT, preferred_element_type=F32)
        total += lax.dot_general(d_up[0], up[0, at, :], NT, preferred_element_type=F32)
        for h in range(1, halves):
            total += lax.dot_general(d_gate[h], gate[h, at, :], NT, preferred_element_type=F32)
            total += lax.dot_general(d_up[h], up[h, at, :], NT, preferred_element_type=F32)
        rows[:, at] = total.astype(BF16)

    for p, (low, high) in enumerate(bounds):
        back = rows[:, low:high]
        if p > 0:
            order = (back_turn if p == 1 else turn)[...]
            back = jnp.dot(order, back, preferred_element_type=F32).astype(BF16)
        for k in range(RING):
            outs[p * RING + k][...] = back[k * CHUNK : (k + 1) * CHUNK]


def expert_back(parts, own, other):
    width, half = own[0].shape[1:]
    bounds = bounds_of(width)
    held = pl.BlockSpec(memory_space=pltpu.VMEM)
    far = pl.BlockSpec(memory_space=pl.ANY)
    count = RING * len(bounds)
    outs = pl.pallas_call(
        functools.partial(expert_kernel, bounds),
        in_specs=[held] * 2 + [far] * 6 + [held] * count,
        out_specs=[held] * count,
        out_shape=[
            jax.ShapeDtypeStruct((CHUNK, high - low), BF16)
            for low, high in bounds
            for _ in range(RING)
        ],
        scratch_shapes=[
            pltpu.VMEM((SLOTS, width), BF16),
            pltpu.VMEM((SLOTS, width), BF16),
            pltpu.VMEM((2, width, half), BF16),
            pltpu.VMEM((2, width, half), BF16),
            pltpu.VMEM((2, half, width), BF16),
            pltpu.VMEM((2, SLOTS, half), BF16),
            pltpu.VMEM((2, SLOTS, half), BF16),
            pltpu.SemaphoreType.DMA((2 * half // HIDDEN_TILE, 3)),
        ],
        compiler_params=pltpu.CompilerParams(vmem_limit_bytes=60 * 1024 * 1024),
        cost_estimate=pl.CostEstimate(
            flops=20 * SLOTS * width * half, bytes_accessed=12 * width * half, transcendentals=0
        ),
        name="expert_back",
    )(reorder((2, 0, 1)), reorder((1, 2, 0)), *own, *other, *[a for part in parts for a in part])
    return [outs[p * RING : (p + 1) * RING] for p in range(len(bounds))]


def stack_heads(block):
    heads = block.shape[1] // HEAD_SIZE
    return jnp.concatenate(
        [block[:, h * HEAD_SIZE : (h + 1) * HEAD_SIZE] for h in range(heads)], axis=0
    )


def softmax_kernel(first_row, query, key, probs):
    scale = HEAD_SIZE ** (-0.5)
    tokens = query.shape[0]
    scores = jnp.dot(stack_heads(query[...]), key[...], preferred_element_type=F32) * scale
    row = lax.broadcasted_iota(jnp.int32, scores.shape, 0) % tokens + first_row[0]
    col = lax.broadcasted_iota(jnp.int32, scores.shape, 1)
    scores = jnp.where(col <= row, scores, -1e30)
    weights = jnp.exp(scores - jnp.max(scores, axis=1, keepdims=True))
    probs[...] = (weights / jnp.sum(weights, axis=1, keepdims=True)).astype(BF16)


def softmax_probs(first_row, queries, key, block_heads):
    tokens, width = queries.shape
    length = key.shape[1]
    rows = block_heads * tokens
    steps = width // (block_heads * HEAD_SIZE)
    return pl.pallas_call(
        softmax_kernel,
        grid=(steps,),
        in_specs=[
            pl.BlockSpec(memory_space=pltpu.SMEM),
            pl.BlockSpec((tokens, block_heads * HEAD_SIZE), lambda i: (0, i)),
            pl.BlockSpec((HEAD_SIZE, length), lambda i: (0, 0)),
        ],
        out_specs=pl.BlockSpec((rows, length), lambda i: (i, 0)),
        out_shape=jax.ShapeDtypeStruct((steps * rows, length), BF16),
        compiler_params=pltpu.CompilerParams(vmem_limit_bytes=48 * 1024 * 1024),
        cost_estimate=pl.CostEstimate(
            flops=20 * steps * rows * length * HEAD_SIZE,
            bytes_accessed=2 * steps * rows * length,
            transcendentals=steps * rows * length,
        ),
        name="softmax_probs",
    )(first_row, queries, key)


def attention_kernel(
    last, bounds, place, a_own, b_own, a_other, b_other, query, probs, key, value_t, *refs
):
    pieces, refs = refs[: len(bounds)], refs[len(bounds) :]
    if last:
        dkey_in, dvalue_in, dquery, dkv, dkey, dvalue, resid = refs
    else:
        dquery, dkey, dvalue, resid = refs
    core, x_at, zhi_at = place[0], place[1], place[2]
    step = pl.program_id(0)
    scale = HEAD_SIZE ** (-0.5)
    tokens = query.shape[0]
    x_count, zhi_count, depth = b_own.shape[0], b_own.shape[2], b_own.shape[3]

    @pl.when(step == 0)
    def _():
        for (low, high), ref in zip(bounds, pieces):
            resid[:, low:high] = ref[...]
        if last:
            dkey[...] = dkey_in[...]
            dvalue[...] = dvalue_in[...]
        else:
            dkey[...] = jnp.zeros_like(dkey)
            dvalue[...] = jnp.zeros_like(dvalue)

    first = jnp.zeros((tokens, a_own.shape[4]), F32)
    second = jnp.zeros((tokens, b_own.shape[4]), F32)
    for side, a_part, b_part in ((core, a_own, b_own), (1 - core, a_other, b_other)):
        for r_x in range(x_count):
            for r_z in range(zhi_count):
                x_from = lax.rem(x_at + x_count - r_x, x_count)
                z_from = lax.rem(zhi_at + zhi_count - r_z, zhi_count)
                piece = (z_from * x_count + x_from) * 2 + side
                columns = resid[:, pl.ds(pl.multiple_of(piece * depth, depth), depth)]
                first += jnp.dot(columns, a_part[0, r_x, r_z], preferred_element_type=F32)
                second += jnp.dot(columns, b_part[r_x, 0, r_z], preferred_element_type=F32)
    ctx = jnp.concatenate(
        [stack_heads(first.astype(BF16)), stack_heads(second.astype(BF16))], axis=0
    )
    query_rows = stack_heads(query[...])
    low = probs[...]
    weights = low.astype(F32)
    dprobs = jnp.dot(ctx, value_t[...], preferred_element_type=F32)
    delta = jnp.sum(weights * dprobs, axis=1, keepdims=True)
    dscores = (weights * (dprobs - delta)).astype(BF16)
    dq = jnp.dot(dscores, key[...], preferred_element_type=F32) * scale
    for h in range(query.shape[1] // HEAD_SIZE):
        dquery[:, h * HEAD_SIZE : (h + 1) * HEAD_SIZE] = dq[h * tokens : (h + 1) * tokens].astype(
            BF16
        )
    dkey[...] += lax.dot_general(query_rows, dscores, TN, preferred_element_type=F32)
    dvalue[...] += lax.dot_general(ctx, low, TN, preferred_element_type=F32)

    if last:

        @pl.when(step == pl.num_programs(0) - 1)
        def _():
            dkv[:, :HEAD_SIZE] = jnp.transpose(dkey[...] * scale).astype(BF16)
            dkv[:, HEAD_SIZE:] = jnp.transpose(dvalue[...]).astype(BF16)


def attention_back(place, resid, proj, queries, probs, key, value_t, carried):
    tokens = queries.shape[0]
    width = sum(piece.shape[1] for piece in resid)
    y_count, x_count, zhi_count, depth, cols = proj[0].shape
    length = key.shape[0]
    block_cols = 2 * cols
    rows = tokens * block_cols // HEAD_SIZE
    last = carried is not None

    def y_of(i, place):
        return lax.rem(place[3] + y_count - i, y_count)

    def whole(*shape):
        return pl.BlockSpec(shape, lambda i, place: (0,) * len(shape))

    a_spec = pl.BlockSpec((1, x_count, zhi_count, depth, cols), lambda i, place: (i, 0, 0, 0, 0))
    b_spec = pl.BlockSpec((x_count, 1, zhi_count, depth, cols), lambda i, place: (0, i, 0, 0, 0))
    block = pl.BlockSpec((tokens, block_cols), lambda i, place: (0, y_of(i, place)))
    in_specs = [
        a_spec,
        b_spec,
        a_spec,
        b_spec,
        block,
        pl.BlockSpec((rows, length), lambda i, place: (y_of(i, place), 0)),
        whole(length, HEAD_SIZE),
        whole(HEAD_SIZE, length),
    ] + [whole(*piece.shape) for piece in resid]
    sums = jax.ShapeDtypeStruct((HEAD_SIZE, length), F32)
    dquery = jax.ShapeDtypeStruct((tokens, y_count * block_cols), BF16)
    if last:
        in_specs += [whole(HEAD_SIZE, length)] * 2
        out_specs = [block, whole(length, 2 * HEAD_SIZE)]
        out_shape = [dquery, jax.ShapeDtypeStruct((length, 2 * HEAD_SIZE), BF16)]
        scratch = [pltpu.VMEM((HEAD_SIZE, length), F32)] * 2 + [pltpu.VMEM((tokens, width), BF16)]
    else:
        out_specs = [block] + [whole(HEAD_SIZE, length)] * 2 + [whole(tokens, width)]
        out_shape = [dquery, sums, sums, jax.ShapeDtypeStruct((tokens, width), BF16)]
        scratch = []
    return pl.pallas_call(
        functools.partial(attention_kernel, last, bounds_of(width)),
        grid_spec=pltpu.PrefetchScalarGridSpec(
            num_scalar_prefetch=1,
            grid=(y_count,),
            in_specs=in_specs,
            out_specs=out_specs,
            scratch_shapes=scratch,
        ),
        out_shape=out_shape,
        compiler_params=pltpu.CompilerParams(vmem_limit_bytes=56 * 1024 * 1024),
        cost_estimate=pl.CostEstimate(
            flops=2 * y_count * rows * (5 * length * HEAD_SIZE + width * HEAD_SIZE),
            bytes_accessed=y_count * (2 * width * block_cols + 2 * rows * length),
            transcendentals=0,
        ),
        name="attention_back",
    )(place, *proj, queries, probs, key, value_t, *resid, *(carried or ()))


def swapped(block, axis):
    return lax.ppermute(block, axis, [(0, 1), (1, 0)])


def shifted(block, axis, by):
    count = lax.axis_size(axis)
    return lax.ppermute(block, axis, [(i, (i + by) % count) for i in range(count)])


def gathered(block, axis):
    return jnp.stack([block] + [shifted(block, axis, k) for k in range(1, lax.axis_size(axis))])


def body(
    hidden_in,
    out_grad,
    queries,
    keys,
    values,
    out_proj,
    expert_ids,
    gate_probs,
    w_gate,
    w_up,
    w_down,
):
    tokens, width = hidden_in.shape[1:]
    zlo = lax.axis_index("zlo")
    y_at = lax.axis_index("y")
    zhi_at = lax.axis_index("zhi")
    y_count = lax.axis_size("y")
    place = jnp.stack(
        [lax.axis_index("core"), lax.axis_index("x"), zhi_at, y_at, 2 * zhi_at + zlo]
    ).astype(jnp.int32)
    swap_two, swap_ends = reorder((1, 0, 2)), reorder((2, 1, 0))

    proj_t = out_proj.T
    cols = proj_t.shape[1] // 2
    proj_pair = gathered(proj_t, "zhi")

    parts = pick(place, expert_ids[0], hidden_in[0], out_grad[0])
    for p, order in enumerate(ORDERS):
        here = [ring(block, order[0], k) for k, block in enumerate(parts[p])]
        here = regroup(swap_two, here)
        parts[p] = [ring(block, order[1], k) for k, block in enumerate(here)]
    for p, order in enumerate(ORDERS):
        if p == 0:
            here, (proj_pair,) = regroup(swap_ends, parts[p], (proj_pair,))
        else:
            here = regroup(swap_ends, parts[p])
        parts[p] = [ring(block, order[2], k) for k, block in enumerate(here)]

    own = (w_gate, w_up, w_down)
    other = tuple(swapped(w, "core") for w in own)
    proj_a = gathered(gathered(proj_pair[:, :, :cols], "x"), "y")
    proj_b = gathered(gathered(proj_pair[:, :, cols:], "y"), "x")
    proj = (proj_a, proj_b, swapped(proj_a, "core"), swapped(proj_b, "core"))

    kv = jnp.stack([keys[0], values[0]]).reshape(2, tokens, GROUPS, HEAD_SIZE)
    own_kv = lax.dynamic_index_in_dim(kv, zlo, 2, keepdims=False)
    near_kv = swapped(lax.dynamic_index_in_dim(kv, 1 - zlo, 2, keepdims=False), "zlo")
    all_kv = gathered(
        jnp.where(zlo == 0, jnp.stack([own_kv, near_kv]), jnp.stack([near_kv, own_kv])), "y"
    )
    back_by = jnp.remainder(y_at - jnp.arange(y_count), y_count)
    all_kv = jnp.take(all_kv, back_by, axis=0).transpose(2, 1, 0, 3, 4).reshape(2, -1, HEAD_SIZE)
    key, value = all_kv[0], all_kv[1]
    key_t, value_t = key.T, value.T
    group_width = width // GROUPS
    own_query = lax.dynamic_slice_in_dim(queries[0], zlo * group_width, group_width, 1)
    near_query = swapped(
        lax.dynamic_slice_in_dim(queries[0], (1 - zlo) * group_width, group_width, 1), "zlo"
    )
    block_heads = out_proj.shape[0] // HEAD_SIZE
    own_row = ((zlo * y_count + y_at) * tokens).astype(jnp.int32).reshape(1)
    near_row = (((1 - zlo) * y_count + y_at) * tokens).astype(jnp.int32).reshape(1)
    own_probs = softmax_probs(own_row, own_query, key_t, block_heads)
    near_probs = softmax_probs(near_row, near_query, key_t, block_heads)

    parts = expert_back(parts, own, other)
    resid = []
    near_resid = []
    for p, order in enumerate(ORDERS):
        here = [ring(block, order[2], -k) for k, block in enumerate(parts[p])]
        here = regroup(swap_ends, here)
        here = [ring(block, order[1], -k) for k, block in enumerate(here)]
        here = regroup(swap_two, here)
        here = [ring(block, order[0], -k) for k, block in enumerate(here)]
        piece = mix(p, place, expert_ids[0], gate_probs[0], out_grad[0], here)
        resid.append(piece)
        near_resid.append(swapped(piece, "zlo"))

    dquery, dkey, dvalue, whole_resid = attention_back(
        place, resid, proj, own_query, own_probs, key, value_t, None
    )
    near_dquery, dkv = attention_back(
        place, near_resid, proj, near_query, near_probs, key, value_t, (dkey, dvalue)
    )
    far_dquery = swapped(near_dquery, "zlo")
    dquery = jnp.where(
        zlo == 0,
        jnp.concatenate([dquery, far_dquery], axis=1),
        jnp.concatenate([far_dquery, dquery], axis=1),
    )
    sent = lax.all_to_all(
        dkv.reshape(-1, tokens, 2 * HEAD_SIZE), SEQ, split_axis=0, concat_axis=0, tiled=True
    )
    sent = sent.reshape(GROUPS, y_count, tokens, 2 * HEAD_SIZE)
    sums = jnp.sum(sent.astype(F32), axis=1).astype(BF16)
    dkey = jnp.concatenate([sums[g, :, :HEAD_SIZE] for g in range(GROUPS)], axis=1)
    dvalue = jnp.concatenate([sums[g, :, HEAD_SIZE:] for g in range(GROUPS)], axis=1)
    return whole_resid[None], dquery[None], dkey[None], dvalue[None]


def solution(mesh):
    fine = Mesh(mesh.devices.reshape(2, 4, 2, 4, 2), ("zlo", "y", "zhi", "x", "core"))
    dp = ("zhi", "x", "core")
    token_spec = P(dp, SEQ, None)
    weight_spec = P((*SEQ, *dp), None, None)
    return jax.shard_map(
        body,
        mesh=fine,
        in_specs=(token_spec,) * 5
        + (P(SEQ, dp), token_spec, token_spec, weight_spec, weight_spec, weight_spec),
        out_specs=(token_spec,) * 4,
        check_vma=False,
    )
```

```python
import functools

import jax
import jax.numpy as jnp
import numpy as np
from jax import lax
from jax.experimental import pallas as pl
from jax.experimental.pallas import tpu as pltpu
from jax.sharding import Mesh
from jax.sharding import PartitionSpec as P

HEAD_SIZE = 128
GROUPS = 2
CAPACITY = 5
EXPERTS = 64
SLOTS = EXPERTS * CAPACITY
SEQ = ("zlo", "y")
CHIPS = ("zlo", "y", "zhi", "x")
PLANE = ("y", "zhi", "x")
BLOCK = 512
PIECES = 8
BATCH = PIECES * CAPACITY
HIDDEN_TILE = 256
NT = (((1,), (1,)), ((), ()))
TN = (((0,), (0,)), ((), ()))
F32 = jnp.float32
BF16 = jnp.bfloat16


def chunk_order():
    index = np.arange(PIECES * BATCH).reshape(PIECES, PIECES, CAPACITY)
    moved = index.transpose(1, 0, 2).reshape(-1)
    return jnp.asarray(np.eye(PIECES * BATCH, dtype=np.float32)[moved], BF16)


def reordered(order, rows):
    return jnp.dot(order, rows, preferred_element_type=F32)


def slot_rows(ids):
    tokens = ids.shape[0]
    lane = lax.broadcasted_iota(jnp.int32, (tokens, EXPERTS), 1)
    chosen = [ids[:, k : k + 1] for k in range(ids.shape[1])]
    hots = [jnp.where(lane == e, 1.0, 0.0) for e in chosen]
    before = jnp.where(
        lax.broadcasted_iota(jnp.int32, (tokens, tokens), 1)
        < lax.broadcasted_iota(jnp.int32, (tokens, tokens), 0),
        1.0,
        0.0,
    ).astype(BF16)
    earlier = jnp.dot(before, sum(hots).astype(BF16), preferred_element_type=F32)
    return [
        e * CAPACITY + jnp.sum(earlier * hot, axis=1, keepdims=True).astype(jnp.int32)
        for e, hot in zip(chosen, hots)
    ]


def pick_kernel(order, ids, hidden, grads, out, rows, row_grads):
    lane = lax.broadcasted_iota(jnp.int32, (ids.shape[0], SLOTS), 1)
    picking = sum(jnp.where(lane == row, 1.0, 0.0) for row in slot_rows(ids)).astype(BF16)
    for piece in range(PIECES):
        at = slice(piece * BLOCK, (piece + 1) * BLOCK)
        rows[:, at] = lax.dot_general(picking, hidden[:, at], TN, preferred_element_type=F32)
        row_grads[:, at] = lax.dot_general(picking, grads[:, at], TN, preferred_element_type=F32)
    for g in range(SLOTS // BATCH):
        slots = slice(g * BATCH, (g + 1) * BATCH)
        for side, source in enumerate((rows, row_grads)):
            pieces = [source[slots, p * BLOCK : (p + 1) * BLOCK] for p in range(PIECES)]
            sent = reordered(order[...], jnp.concatenate(pieces, axis=0).astype(BF16))
            out[g * PIECES * BATCH : (g + 1) * PIECES * BATCH, side * BLOCK : (side + 1) * BLOCK] = (
                sent.astype(BF16)
            )


def pick(ids, hidden, grads):
    width = hidden.shape[1]
    held = pl.BlockSpec(memory_space=pltpu.VMEM)
    return pl.pallas_call(
        pick_kernel,
        in_specs=[held] * 4,
        out_specs=held,
        out_shape=jax.ShapeDtypeStruct((EXPERTS * BATCH, 2 * BLOCK), BF16),
        scratch_shapes=[pltpu.VMEM((SLOTS, width), F32)] * 2,
        compiler_params=pltpu.CompilerParams(vmem_limit_bytes=48 * 1024 * 1024),
        name="pick",
    )(chunk_order(), ids, hidden, grads)


def mix_kernel(order, ids, probs, grads, came, out, rows):
    for g in range(SLOTS // BATCH):
        batch = came[g * PIECES * BATCH : (g + 1) * PIECES * BATCH]
        batch = reordered(order[...], batch)
        for p in range(PIECES):
            rows[g * BATCH : (g + 1) * BATCH, p * BLOCK : (p + 1) * BLOCK] = batch[
                p * BATCH : (p + 1) * BATCH
            ]
    lane = lax.broadcasted_iota(jnp.int32, (ids.shape[0], SLOTS), 1)
    mixing = sum(
        jnp.where(lane == row, probs[:, k : k + 1], 0.0) for k, row in enumerate(slot_rows(ids))
    )
    mixing_high = mixing.astype(BF16)
    mixing_low = (mixing - mixing_high.astype(F32)).astype(BF16)
    for p in range(PIECES):
        at = slice(p * BLOCK, (p + 1) * BLOCK)
        block = rows[:, at].astype(BF16)
        mixed = jnp.dot(mixing_high, block, preferred_element_type=F32)
        mixed += jnp.dot(mixing_low, block, preferred_element_type=F32)
        out[:, at] = (grads[:, at].astype(F32) + mixed).astype(BF16)


def mix(ids, probs, grads, came):
    held = pl.BlockSpec(memory_space=pltpu.VMEM)
    return pl.pallas_call(
        mix_kernel,
        in_specs=[held] * 5,
        out_specs=held,
        out_shape=jax.ShapeDtypeStruct(grads.shape, BF16),
        scratch_shapes=[pltpu.VMEM((SLOTS, grads.shape[1]), F32)],
        compiler_params=pltpu.CompilerParams(vmem_limit_bytes=48 * 1024 * 1024),
        name="mix",
    )(chunk_order(), ids, probs, grads, came)


def after_kernel(*refs):
    pass


def after(arrays, event):
    far = pl.BlockSpec(memory_space=pl.ANY)
    count = len(arrays)
    return pl.pallas_call(
        after_kernel,
        in_specs=[far] * (count + 1),
        out_specs=[far] * count,
        out_shape=[jax.ShapeDtypeStruct(a.shape, a.dtype) for a in arrays],
        input_output_aliases={i: i for i in range(count)},
        name="after",
    )(*arrays, event)


def expert_kernel(order, g0, u0, d0, g1, u1, d1, came, *refs):
    carried = (len(refs) - 9) // 2
    out = refs[carried]
    rows, grads, gate, up, down, d_gate, d_up, sems = refs[2 * carried + 1 :]
    halves, width, half = gate.shape
    tile = 512
    loads = []
    for h, (g, u, d) in enumerate(((g0, u0, d0), (g1, u1, d1))):
        for at in range(0, half, HIDDEN_TILE):
            part = slice(at, at + HIDDEN_TILE)
            copies = [
                pltpu.make_async_copy(g.at[0, :, part], gate.at[h, :, part], sems.at[len(loads), 0]),
                pltpu.make_async_copy(u.at[0, :, part], up.at[h, :, part], sems.at[len(loads), 1]),
                pltpu.make_async_copy(d.at[0, part, :], down.at[h, part, :], sems.at[len(loads), 2]),
            ]
            for copy in copies:
                copy.start()
            loads.append((h, part, copies))
    size = PIECES * BATCH
    for g in range(0, SLOTS // BATCH, 2):
        batches = [reordered(order[...], came[(g + i) * size : (g + i + 1) * size]) for i in range(2)]
        slots = slice(g * BATCH, (g + 2) * BATCH)
        for p in range(PIECES):
            pair = [batch[p * BATCH : (p + 1) * BATCH] for batch in batches]
            pair = jnp.concatenate(pair, axis=0).astype(BF16)
            rows[slots, p * BLOCK : (p + 1) * BLOCK] = pair[:, :BLOCK]
            grads[slots, p * BLOCK : (p + 1) * BLOCK] = pair[:, BLOCK:]
    for h, part, copies in loads:
        for copy in copies:
            copy.wait()
        pre_gate = jnp.dot(rows[...], gate[h, :, part], preferred_element_type=F32)
        pre_up = jnp.dot(rows[...], up[h, :, part], preferred_element_type=F32)
        upstream = lax.dot_general(grads[...], down[h, part, :], NT, preferred_element_type=F32)
        sig = jax.nn.sigmoid(pre_gate)
        d_gate[h, :, part] = (upstream * pre_up * sig * (1.0 + pre_gate * (1.0 - sig))).astype(BF16)
        d_up[h, :, part] = (upstream * pre_gate * sig).astype(BF16)

    @pl.loop(0, width // tile)
    def _(i):
        at = pl.ds(pl.multiple_of(i * tile, tile), tile)
        total = lax.dot_general(d_gate[0], gate[0, at, :], NT, preferred_element_type=F32)
        total += lax.dot_general(d_up[0], up[0, at, :], NT, preferred_element_type=F32)
        for h in range(1, halves):
            total += lax.dot_general(d_gate[h], gate[h, at, :], NT, preferred_element_type=F32)
            total += lax.dot_general(d_up[h], up[h, at, :], NT, preferred_element_type=F32)
        rows[:, at] = total.astype(BF16)

    for g in range(0, SLOTS // BATCH, 2):
        slots = slice(g * BATCH, (g + 2) * BATCH)
        pieces = [rows[slots, p * BLOCK : (p + 1) * BLOCK].astype(F32) for p in range(PIECES)]
        for i in range(2):
            batch = [piece[i * BATCH : (i + 1) * BATCH] for piece in pieces]
            batch = jnp.concatenate(batch, axis=0).astype(BF16)
            out[(g + i) * size : (g + i + 1) * size] = reordered(order[...], batch).astype(BF16)


def expert_back(came, own, other, carried):
    width, half = own[0].shape[1:]
    held = pl.BlockSpec(memory_space=pltpu.VMEM)
    far = pl.BlockSpec(memory_space=pl.ANY)
    count = len(carried)
    return pl.pallas_call(
        expert_kernel,
        in_specs=[held] + [far] * 6 + [held] + [far] * count,
        out_specs=[held] + [far] * count,
        out_shape=[jax.ShapeDtypeStruct((EXPERTS * BATCH, BLOCK), BF16)]
        + [jax.ShapeDtypeStruct(a.shape, a.dtype) for a in carried],
        input_output_aliases={8 + i: 1 + i for i in range(count)},
        scratch_shapes=[
            pltpu.VMEM((SLOTS, width), BF16),
            pltpu.VMEM((SLOTS, width), BF16),
            pltpu.VMEM((2, width, half), BF16),
            pltpu.VMEM((2, width, half), BF16),
            pltpu.VMEM((2, half, width), BF16),
            pltpu.VMEM((2, SLOTS, half), BF16),
            pltpu.VMEM((2, SLOTS, half), BF16),
            pltpu.SemaphoreType.DMA((2 * half // HIDDEN_TILE, 3)),
        ],
        compiler_params=pltpu.CompilerParams(vmem_limit_bytes=60 * 1024 * 1024),
        cost_estimate=pl.CostEstimate(
            flops=20 * SLOTS * width * half, bytes_accessed=12 * width * half, transcendentals=0
        ),
        name="expert_back",
    )(chunk_order(), *own, *other, came, *carried)


def stack_heads(block):
    heads = block.shape[1] // HEAD_SIZE
    return jnp.concatenate(
        [block[:, h * HEAD_SIZE : (h + 1) * HEAD_SIZE] for h in range(heads)], axis=0
    )


def softmax_kernel(first_row, query, key, probs):
    scale = HEAD_SIZE ** (-0.5)
    tokens = query.shape[0]
    scores = jnp.dot(stack_heads(query[...]), key[...], preferred_element_type=F32) * scale
    row = lax.broadcasted_iota(jnp.int32, scores.shape, 0) % tokens + first_row[0]
    col = lax.broadcasted_iota(jnp.int32, scores.shape, 1)
    scores = jnp.where(col <= row, scores, -1e30)
    weights = jnp.exp(scores - jnp.max(scores, axis=1, keepdims=True))
    probs[...] = (weights / jnp.sum(weights, axis=1, keepdims=True)).astype(BF16)


def softmax_probs(first_row, queries, key, block_heads):
    tokens, width = queries.shape
    length = key.shape[1]
    rows = block_heads * tokens
    steps = width // (block_heads * HEAD_SIZE)
    return pl.pallas_call(
        softmax_kernel,
        grid=(steps,),
        in_specs=[
            pl.BlockSpec(memory_space=pltpu.SMEM),
            pl.BlockSpec((tokens, block_heads * HEAD_SIZE), lambda i: (0, i)),
            pl.BlockSpec((HEAD_SIZE, length), lambda i: (0, 0)),
        ],
        out_specs=pl.BlockSpec((rows, length), lambda i: (i, 0)),
        out_shape=jax.ShapeDtypeStruct((steps * rows, length), BF16),
        compiler_params=pltpu.CompilerParams(vmem_limit_bytes=48 * 1024 * 1024),
        cost_estimate=pl.CostEstimate(
            flops=20 * steps * rows * length * HEAD_SIZE,
            bytes_accessed=2 * steps * rows * length,
            transcendentals=steps * rows * length,
        ),
        name="softmax_probs",
    )(first_row, queries, key)


def attention_kernel(last, core, resid, own, other, query, probs, key, value_t, *refs):
    if last:
        dkey_in, dvalue_in, dquery, dkv, dkey, dvalue = refs
    else:
        dquery, dkey, dvalue = refs
    step = pl.program_id(0)
    scale = HEAD_SIZE ** (-0.5)
    tokens = query.shape[0]
    pieces, depth, block_cols = own.shape[1:]

    @pl.when(step == 0)
    def _():
        if last:
            dkey[...] = dkey_in[...]
            dvalue[...] = dvalue_in[...]
        else:
            dkey[...] = jnp.zeros_like(dkey)
            dvalue[...] = jnp.zeros_like(dvalue)

    ctx = jnp.zeros((tokens, block_cols), F32)
    for side, shard in ((core[0], own), (1 - core[0], other)):
        for piece in range(pieces):
            at = pl.ds(pl.multiple_of((2 * piece + side) * depth, depth), depth)
            ctx += jnp.dot(resid[:, at], shard[0, piece], preferred_element_type=F32)
    ctx = stack_heads(ctx.astype(BF16))
    query_rows = stack_heads(query[...])
    low = probs[...]
    weights = low.astype(F32)
    dprobs = jnp.dot(ctx, value_t[...], preferred_element_type=F32)
    delta = jnp.sum(weights * dprobs, axis=1, keepdims=True)
    dscores = (weights * (dprobs - delta)).astype(BF16)
    dq = jnp.dot(dscores, key[...], preferred_element_type=F32) * scale
    for h in range(query.shape[1] // HEAD_SIZE):
        dquery[:, h * HEAD_SIZE : (h + 1) * HEAD_SIZE] = dq[h * tokens : (h + 1) * tokens].astype(
            BF16
        )
    dkey[...] += lax.dot_general(query_rows, dscores, TN, preferred_element_type=F32)
    dvalue[...] += lax.dot_general(ctx, low, TN, preferred_element_type=F32)

    if last:

        @pl.when(step == pl.num_programs(0) - 1)
        def _():
            dkv[:, :HEAD_SIZE] = jnp.transpose(dkey[...] * scale).astype(BF16)
            dkv[:, HEAD_SIZE:] = jnp.transpose(dvalue[...]).astype(BF16)


def attention_back(core, resid, own, other, queries, probs, key, value_t, carried):
    tokens, width = resid.shape
    steps, pieces, depth, block_cols = own.shape
    length = key.shape[0]
    rows = tokens * block_cols // HEAD_SIZE
    last = carried is not None

    def whole(*shape):
        return pl.BlockSpec(shape, lambda i: (0,) * len(shape))

    shard = pl.BlockSpec((1, pieces, depth, block_cols), lambda i: (i, 0, 0, 0))
    block = pl.BlockSpec((tokens, block_cols), lambda i: (0, i))
    in_specs = [
        pl.BlockSpec(memory_space=pltpu.SMEM),
        whole(tokens, width),
        shard,
        shard,
        block,
        pl.BlockSpec((rows, length), lambda i: (i, 0)),
        whole(length, HEAD_SIZE),
        whole(HEAD_SIZE, length),
    ]
    sums = jax.ShapeDtypeStruct((HEAD_SIZE, length), F32)
    dquery = jax.ShapeDtypeStruct((tokens, steps * block_cols), BF16)
    if last:
        in_specs += [whole(HEAD_SIZE, length)] * 2
        out_specs = [block, whole(length, 2 * HEAD_SIZE)]
        out_shape = [dquery, jax.ShapeDtypeStruct((length, 2 * HEAD_SIZE), BF16)]
        scratch = [pltpu.VMEM((HEAD_SIZE, length), F32)] * 2
    else:
        out_specs = [block] + [whole(HEAD_SIZE, length)] * 2
        out_shape = [dquery, sums, sums]
        scratch = []
    return pl.pallas_call(
        functools.partial(attention_kernel, last),
        grid=(steps,),
        in_specs=in_specs,
        out_specs=out_specs,
        scratch_shapes=scratch,
        out_shape=out_shape,
        compiler_params=pltpu.CompilerParams(vmem_limit_bytes=56 * 1024 * 1024),
        cost_estimate=pl.CostEstimate(
            flops=2 * steps * rows * (5 * length * HEAD_SIZE + width * HEAD_SIZE),
            bytes_accessed=steps * (2 * width * block_cols + 2 * rows * length),
            transcendentals=0,
        ),
        name="attention_back",
    )(core, resid, own, other, queries, probs, key, value_t, *(carried or ()))


def swapped(block, axis):
    return lax.ppermute(block, axis, [(0, 1), (1, 0)])


def to_chips(chunks):
    sent = chunks.reshape(EXPERTS, BATCH, -1)
    return lax.all_to_all(sent, CHIPS, split_axis=0, concat_axis=0, tiled=True).reshape(
        chunks.shape
    )


def body(
    hidden_in,
    out_grad,
    queries,
    keys,
    values,
    out_proj,
    expert_ids,
    gate_probs,
    w_gate,
    w_up,
    w_down,
):
    tokens, width = hidden_in.shape[1:]
    zlo = lax.axis_index("zlo")
    y_at = lax.axis_index("y")
    y_count = lax.axis_size("y")
    core = lax.axis_index("core").astype(jnp.int32).reshape(1)
    own = (w_gate, w_up, w_down)
    other = tuple(swapped(w, "core") for w in own)

    came = to_chips(pick(expert_ids[0], hidden_in[0], out_grad[0]))

    kv = lax.all_gather(jnp.concatenate([keys[0], values[0]], axis=1), SEQ, axis=0, tiled=True)
    key = lax.dynamic_slice_in_dim(kv, zlo * HEAD_SIZE, HEAD_SIZE, 1)
    value = lax.dynamic_slice_in_dim(kv, (GROUPS + zlo) * HEAD_SIZE, HEAD_SIZE, 1)
    key_t, value_t = key.T, value.T
    group_width = width // GROUPS
    own_query = lax.dynamic_slice_in_dim(queries[0], zlo * group_width, group_width, 1)
    near_query = swapped(
        lax.dynamic_slice_in_dim(queries[0], (1 - zlo) * group_width, group_width, 1), "zlo"
    )
    block_heads = out_proj.shape[0] // HEAD_SIZE
    own_row = ((zlo * y_count + y_at) * tokens).astype(jnp.int32).reshape(1)
    near_row = (((1 - zlo) * y_count + y_at) * tokens).astype(jnp.int32).reshape(1)
    own_probs = softmax_probs(own_row, own_query, key_t, block_heads)
    near_probs = softmax_probs(near_row, near_query, key_t, block_heads)

    back, own_probs, near_probs = expert_back(came, own, other, (own_probs, near_probs))

    proj_own = lax.all_gather(out_proj.T, PLANE, axis=0, tiled=False)
    proj_own = proj_own.reshape(y_count, -1, *proj_own.shape[1:])
    (proj_own,) = after((proj_own,), back)
    proj_other = swapped(proj_own, "core")
    result = to_chips(back)
    resid = mix(expert_ids[0], gate_probs[0], out_grad[0], result)
    near_resid = swapped(resid, "zlo")

    dquery, dkey, dvalue = attention_back(
        core, resid, proj_own, proj_other, own_query, own_probs, key, value_t, None
    )
    near_dquery, dkv = attention_back(
        core,
        near_resid,
        proj_own,
        proj_other,
        near_query,
        near_probs,
        key,
        value_t,
        (dkey, dvalue),
    )
    far_dquery = swapped(near_dquery, "zlo")
    dquery = jnp.where(
        zlo == 0,
        jnp.concatenate([dquery, far_dquery], axis=1),
        jnp.concatenate([far_dquery, dquery], axis=1),
    )
    sent = lax.all_to_all(
        dkv.reshape(-1, tokens, 2 * HEAD_SIZE), SEQ, split_axis=0, concat_axis=0, tiled=True
    )
    sent = sent.reshape(GROUPS, y_count, tokens, 2 * HEAD_SIZE)
    sums = jnp.sum(sent.astype(F32), axis=1).astype(BF16)
    dkey = jnp.concatenate([sums[g, :, :HEAD_SIZE] for g in range(GROUPS)], axis=1)
    dvalue = jnp.concatenate([sums[g, :, HEAD_SIZE:] for g in range(GROUPS)], axis=1)
    return resid[None], dquery[None], dkey[None], dvalue[None]


def solution(mesh):
    fine = Mesh(mesh.devices.reshape(2, 4, 2, 4, 2), ("zlo", "y", "zhi", "x", "core"))
    dp = ("zhi", "x", "core")
    token_spec = P(dp, SEQ, None)
    weight_spec = P((*SEQ, *dp), None, None)
    return jax.shard_map(
        body,
        mesh=fine,
        in_specs=(token_spec,) * 5
        + (P(SEQ, dp), token_spec, token_spec, weight_spec, weight_spec, weight_spec),
        out_specs=(token_spec,) * 4,
        check_vma=False,
    )
```

```python
import functools

import jax
import jax.numpy as jnp
import numpy as np
from jax import lax
from jax.experimental import pallas as pl
from jax.experimental.pallas import tpu as pltpu
from jax.sharding import Mesh
from jax.sharding import PartitionSpec as P

HEAD_SIZE = 128
GROUPS = 2
CAPACITY = 5
EXPERTS = 64
SLOTS = EXPERTS * CAPACITY
SEQ = ("zlo", "y")
CHIPS = ("zlo", "y", "zhi", "x")
PLANE = ("y", "zhi", "x")
BLOCK = 512
PIECES = 8
BATCH = PIECES * CAPACITY
HIDDEN_TILE = 256
VMEM_BYTES = 60 * 1024 * 1024
NT = (((1,), (1,)), ((), ()))
TN = (((0,), (0,)), ((), ()))
F32 = jnp.float32
BF16 = jnp.bfloat16


def chunk_order():
    count = PIECES * BATCH
    row = lax.broadcasted_iota(jnp.int32, (count, 1), 0)
    chip = (row * 1639) >> 16
    rest = row - chip * BATCH
    piece = (rest * 205) >> 10
    moved = piece * BATCH + chip * CAPACITY + rest - piece * CAPACITY
    return jnp.where(
        lax.broadcasted_iota(jnp.int32, (count, count), 1) == moved, 1.0, 0.0
    ).astype(BF16)


def reordered(order, rows):
    return jnp.dot(order, rows, preferred_element_type=F32)


def slot_rows(ids):
    tokens = ids.shape[1]
    expert = lax.broadcasted_iota(jnp.int32, (EXPERTS, tokens), 0)
    chosen = [ids[k : k + 1] for k in range(ids.shape[0])]
    hots = [jnp.where(expert == e, 1.0, 0.0) for e in chosen]
    before = jnp.where(
        lax.broadcasted_iota(jnp.int32, (tokens, tokens), 0)
        < lax.broadcasted_iota(jnp.int32, (tokens, tokens), 1),
        1.0,
        0.0,
    ).astype(BF16)
    earlier = jnp.dot(sum(hots).astype(BF16), before, preferred_element_type=F32)
    return [
        e * CAPACITY + jnp.sum(earlier * hot, axis=0, keepdims=True).astype(jnp.int32)
        for e, hot in zip(chosen, hots)
    ]


def pick_kernel(ids, hidden, grads, out, rows, row_grads):
    slot = lax.broadcasted_iota(jnp.int32, (SLOTS, ids.shape[1]), 0)
    picking = sum(jnp.where(slot == row, 1.0, 0.0) for row in slot_rows(ids)).astype(BF16)
    for piece in range(PIECES):
        at = slice(piece * BLOCK, (piece + 1) * BLOCK)
        rows[:, at] = jnp.dot(picking, hidden[:, at], preferred_element_type=F32)
        row_grads[:, at] = jnp.dot(picking, grads[:, at], preferred_element_type=F32)
    order = chunk_order()
    for g in range(SLOTS // BATCH):
        slots = slice(g * BATCH, (g + 1) * BATCH)
        for side, source in enumerate((rows, row_grads)):
            pieces = [source[slots, p * BLOCK : (p + 1) * BLOCK] for p in range(PIECES)]
            sent = reordered(order, jnp.concatenate(pieces, axis=0).astype(BF16))
            out[g * PIECES * BATCH : (g + 1) * PIECES * BATCH, side * BLOCK : (side + 1) * BLOCK] = (
                sent.astype(BF16)
            )


def pick(ids, hidden, grads):
    width = hidden.shape[1]
    held = pl.BlockSpec(memory_space=pltpu.VMEM)
    return pl.pallas_call(
        pick_kernel,
        in_specs=[held] * 3,
        out_specs=held,
        out_shape=jax.ShapeDtypeStruct((EXPERTS * BATCH, 2 * BLOCK), BF16),
        scratch_shapes=[pltpu.VMEM((SLOTS, width), F32)] * 2,
        compiler_params=pltpu.CompilerParams(vmem_limit_bytes=VMEM_BYTES),
        name="pick",
    )(ids, hidden, grads)


def mix_kernel(ids, probs, grads, came, out, rows):
    order = chunk_order()
    for g in range(SLOTS // BATCH):
        batch = came[g * PIECES * BATCH : (g + 1) * PIECES * BATCH]
        batch = reordered(order, batch)
        for p in range(PIECES):
            rows[g * BATCH : (g + 1) * BATCH, p * BLOCK : (p + 1) * BLOCK] = batch[
                p * BATCH : (p + 1) * BATCH
            ]
    slot = lax.broadcasted_iota(jnp.int32, (SLOTS, ids.shape[1]), 0)
    mixing = sum(
        jnp.where(slot == row, probs[k : k + 1], 0.0) for k, row in enumerate(slot_rows(ids))
    )
    mixing = jnp.transpose(mixing)
    mixing_high = mixing.astype(BF16)
    mixing_low = (mixing - mixing_high.astype(F32)).astype(BF16)
    for p in range(PIECES):
        at = slice(p * BLOCK, (p + 1) * BLOCK)
        block = rows[:, at].astype(BF16)
        mixed = jnp.dot(mixing_high, block, preferred_element_type=F32)
        mixed += jnp.dot(mixing_low, block, preferred_element_type=F32)
        out[:, at] = (grads[:, at].astype(F32) + mixed).astype(BF16)


def mix(ids, probs, grads, came):
    held = pl.BlockSpec(memory_space=pltpu.VMEM)
    return pl.pallas_call(
        mix_kernel,
        in_specs=[held] * 4,
        out_specs=held,
        out_shape=jax.ShapeDtypeStruct(grads.shape, BF16),
        scratch_shapes=[pltpu.VMEM((SLOTS, grads.shape[1]), F32)],
        compiler_params=pltpu.CompilerParams(vmem_limit_bytes=VMEM_BYTES),
        name="mix",
    )(ids, probs, grads, came)


def turn_kernel(block, out):
    out[...] = jnp.transpose(block[...])


def turned(block):
    held = pl.BlockSpec(memory_space=pltpu.VMEM)
    return pl.pallas_call(
        turn_kernel,
        in_specs=[held],
        out_specs=held,
        out_shape=jax.ShapeDtypeStruct(block.shape[::-1], block.dtype),
        compiler_params=pltpu.CompilerParams(vmem_limit_bytes=VMEM_BYTES),
        name="turned",
    )(block)


def expert_kernel(
    g0, u0, d0, g1, u1, d1, sent, out, came, rows, grads, gate, up, down, d_gate, d_up, sems, came_sem
):
    arrival = pltpu.make_async_copy(sent, came, came_sem)
    arrival.start()
    halves, width, half = gate.shape
    tile = 512
    loads = []
    for h, (g, u, d) in enumerate(((g0, u0, d0), (g1, u1, d1))):
        for at in range(0, half, HIDDEN_TILE):
            part = slice(at, at + HIDDEN_TILE)
            copies = [
                pltpu.make_async_copy(g.at[0, :, part], gate.at[h, :, part], sems.at[len(loads), 0]),
                pltpu.make_async_copy(u.at[0, :, part], up.at[h, :, part], sems.at[len(loads), 1]),
                pltpu.make_async_copy(d.at[0, part, :], down.at[h, part, :], sems.at[len(loads), 2]),
            ]
            for copy in copies:
                copy.start()
            loads.append((h, part, copies))
    size = PIECES * BATCH
    order = chunk_order()
    arrival.wait()
    for g in range(0, SLOTS // BATCH, 2):
        batches = [reordered(order, came[(g + i) * size : (g + i + 1) * size]) for i in range(2)]
        slots = slice(g * BATCH, (g + 2) * BATCH)
        for p in range(PIECES):
            pair = [batch[p * BATCH : (p + 1) * BATCH] for batch in batches]
            pair = jnp.concatenate(pair, axis=0).astype(BF16)
            rows[slots, p * BLOCK : (p + 1) * BLOCK] = pair[:, :BLOCK]
            grads[slots, p * BLOCK : (p + 1) * BLOCK] = pair[:, BLOCK:]
    for h, part, copies in loads:
        for copy in copies:
            copy.wait()
        pre_gate = jnp.dot(rows[...], gate[h, :, part], preferred_element_type=F32)
        pre_up = jnp.dot(rows[...], up[h, :, part], preferred_element_type=F32)
        upstream = lax.dot_general(grads[...], down[h, part, :], NT, preferred_element_type=F32)
        sig = jax.nn.sigmoid(pre_gate)
        d_gate[h, :, part] = (upstream * pre_up * sig * (1.0 + pre_gate * (1.0 - sig))).astype(BF16)
        d_up[h, :, part] = (upstream * pre_gate * sig).astype(BF16)

    @pl.loop(0, width // tile)
    def _(i):
        at = pl.ds(pl.multiple_of(i * tile, tile), tile)
        total = lax.dot_general(d_gate[0], gate[0, at, :], NT, preferred_element_type=F32)
        total += lax.dot_general(d_up[0], up[0, at, :], NT, preferred_element_type=F32)
        for h in range(1, halves):
            total += lax.dot_general(d_gate[h], gate[h, at, :], NT, preferred_element_type=F32)
            total += lax.dot_general(d_up[h], up[h, at, :], NT, preferred_element_type=F32)
        rows[:, at] = total.astype(BF16)

    for g in range(0, SLOTS // BATCH, 2):
        slots = slice(g * BATCH, (g + 2) * BATCH)
        pieces = [rows[slots, p * BLOCK : (p + 1) * BLOCK].astype(F32) for p in range(PIECES)]
        for i in range(2):
            batch = [piece[i * BATCH : (i + 1) * BATCH] for piece in pieces]
            batch = jnp.concatenate(batch, axis=0).astype(BF16)
            out[(g + i) * size : (g + i + 1) * size] = reordered(order, batch).astype(BF16)


def expert_back(sent, own, other):
    width, half = own[0].shape[1:]
    far = pl.BlockSpec(memory_space=pl.ANY)
    return pl.pallas_call(
        expert_kernel,
        in_specs=[far] * 7,
        out_specs=pl.BlockSpec(memory_space=pltpu.VMEM),
        out_shape=jax.ShapeDtypeStruct((EXPERTS * BATCH, BLOCK), BF16),
        scratch_shapes=[
            pltpu.VMEM(sent.shape, BF16),
            pltpu.VMEM((SLOTS, width), BF16),
            pltpu.VMEM((SLOTS, width), BF16),
            pltpu.VMEM((2, width, half), BF16),
            pltpu.VMEM((2, width, half), BF16),
            pltpu.VMEM((2, half, width), BF16),
            pltpu.VMEM((2, SLOTS, half), BF16),
            pltpu.VMEM((2, SLOTS, half), BF16),
            pltpu.SemaphoreType.DMA((2 * half // HIDDEN_TILE, 3)),
            pltpu.SemaphoreType.DMA,
        ],
        compiler_params=pltpu.CompilerParams(vmem_limit_bytes=VMEM_BYTES),
        cost_estimate=pl.CostEstimate(
            flops=20 * SLOTS * width * half, bytes_accessed=12 * width * half, transcendentals=0
        ),
        name="expert_back",
    )(*own, *other, sent)


def stack_heads(block):
    heads = block.shape[1] // HEAD_SIZE
    return jnp.concatenate(
        [block[:, h * HEAD_SIZE : (h + 1) * HEAD_SIZE] for h in range(heads)], axis=0
    )


def softmax_kernel(first_row, query, key, probs):
    scale = HEAD_SIZE ** (-0.5)
    tokens = query.shape[0]
    scores = jnp.dot(stack_heads(query[...]), key[...], preferred_element_type=F32) * scale
    row = lax.broadcasted_iota(jnp.int32, scores.shape, 0) % tokens + first_row[0]
    col = lax.broadcasted_iota(jnp.int32, scores.shape, 1)
    scores = jnp.where(col <= row, scores, -1e30)
    weights = jnp.exp(scores - jnp.max(scores, axis=1, keepdims=True))
    probs[...] = (weights / jnp.sum(weights, axis=1, keepdims=True)).astype(BF16)


def softmax_probs(first_row, queries, key, block_heads):
    tokens, width = queries.shape
    length = key.shape[1]
    rows = block_heads * tokens
    steps = width // (block_heads * HEAD_SIZE)
    return pl.pallas_call(
        softmax_kernel,
        grid=(steps,),
        in_specs=[
            pl.BlockSpec(memory_space=pltpu.SMEM),
            pl.BlockSpec((tokens, block_heads * HEAD_SIZE), lambda i: (0, i)),
            pl.BlockSpec((HEAD_SIZE, length), lambda i: (0, 0)),
        ],
        out_specs=pl.BlockSpec((rows, length), lambda i: (i, 0)),
        out_shape=jax.ShapeDtypeStruct((steps * rows, length), BF16),
        compiler_params=pltpu.CompilerParams(vmem_limit_bytes=48 * 1024 * 1024),
        cost_estimate=pl.CostEstimate(
            flops=20 * steps * rows * length * HEAD_SIZE,
            bytes_accessed=2 * steps * rows * length,
            transcendentals=steps * rows * length,
        ),
        name="softmax_probs",
    )(first_row, queries, key)


def attention_kernel(begins, ends, core, resid, own, query, probs, key, value_t, *refs):
    ctx, refs = refs[-1], refs[:-1]
    steps = pl.num_programs(0)
    if not begins:
        dkey_in, dvalue_in = refs[:2]
        refs = refs[2:]
    if ends:
        *others, dquery, dkv, dkey, dvalue = refs
    else:
        *others, dquery, dkey, dvalue = refs
    step = pl.program_id(0)
    scale = HEAD_SIZE ** (-0.5)
    tokens = query.shape[0]
    pieces, depth, block_cols = own.shape[1:]

    @pl.when(step == 0)
    def _():
        if begins:
            dkey[...] = jnp.zeros_like(dkey)
            dvalue[...] = jnp.zeros_like(dvalue)
        else:
            dkey[...] = dkey_in[...]
            dvalue[...] = dvalue_in[...]

    def project(side, shard):
        total = jnp.zeros((tokens, block_cols), F32)
        for piece in range(pieces):
            at = pl.ds(pl.multiple_of((2 * piece + side) * depth, depth), depth)
            total += jnp.dot(resid[:, at], shard[0, piece], preferred_element_type=F32)
        return total

    for j, other in enumerate(others):

        @pl.when(step * len(others) // steps == j)
        def _(other=other):
            ctx[...] = project(1 - core[0], other)

    ctx = stack_heads((ctx[...] + project(core[0], own)).astype(BF16))
    query_rows = stack_heads(query[...])
    low = probs[...]
    weights = low.astype(F32)
    dprobs = jnp.dot(ctx, value_t[...], preferred_element_type=F32)
    delta = jnp.sum(weights * dprobs, axis=1, keepdims=True)
    dscores = (weights * (dprobs - delta)).astype(BF16)
    dq = jnp.dot(dscores, key[...], preferred_element_type=F32) * scale
    for h in range(query.shape[1] // HEAD_SIZE):
        dquery[:, h * HEAD_SIZE : (h + 1) * HEAD_SIZE] = dq[h * tokens : (h + 1) * tokens].astype(
            BF16
        )
    dkey[...] += lax.dot_general(query_rows, dscores, TN, preferred_element_type=F32)
    dvalue[...] += lax.dot_general(ctx, low, TN, preferred_element_type=F32)

    if ends:

        @pl.when(step == steps - 1)
        def _():
            dkv[:, :HEAD_SIZE] = jnp.transpose(dkey[...] * scale).astype(BF16)
            dkv[:, HEAD_SIZE:] = jnp.transpose(dvalue[...]).astype(BF16)


def attention_back(core, resid, own, others, queries, probs, key, value_t, first, carried, ends):
    tokens, width = resid.shape
    pieces, depth, block_cols = own.shape[1:]
    each = others[0].shape[0]
    steps = each * len(others)
    length = key.shape[0]
    rows = tokens * block_cols // HEAD_SIZE

    def whole(*shape):
        return pl.BlockSpec(shape, lambda i: (0,) * len(shape))

    shard = (1, pieces, depth, block_cols)
    in_specs = [
        pl.BlockSpec(memory_space=pltpu.SMEM),
        whole(tokens, width),
        pl.BlockSpec(shard, lambda i: (first + i, 0, 0, 0)),
        pl.BlockSpec((tokens, block_cols), lambda i: (0, first + i)),
        pl.BlockSpec((rows, length), lambda i: (first + i, 0)),
        whole(length, HEAD_SIZE),
        whole(HEAD_SIZE, length),
    ]
    in_specs += [whole(HEAD_SIZE, length)] * len(carried)
    for j in range(len(others)):
        in_specs.append(
            pl.BlockSpec(shard, lambda i, j=j: (jnp.clip(i - j * each, 0, each - 1), 0, 0, 0))
        )
    sums = jax.ShapeDtypeStruct((HEAD_SIZE, length), F32)
    out_specs = [pl.BlockSpec((tokens, block_cols), lambda i: (0, i))]
    out_shape = [jax.ShapeDtypeStruct((tokens, steps * block_cols), BF16)]
    scratch = [pltpu.VMEM((tokens, block_cols), F32)]
    if ends:
        out_specs += [whole(length, 2 * HEAD_SIZE)]
        out_shape += [jax.ShapeDtypeStruct((length, 2 * HEAD_SIZE), BF16)]
        scratch = [pltpu.VMEM((HEAD_SIZE, length), F32)] * 2 + scratch
    else:
        out_specs += [whole(HEAD_SIZE, length)] * 2
        out_shape += [sums, sums]
    return pl.pallas_call(
        functools.partial(attention_kernel, not carried, ends),
        grid=(steps,),
        in_specs=in_specs,
        out_specs=out_specs,
        scratch_shapes=scratch,
        out_shape=out_shape,
        compiler_params=pltpu.CompilerParams(vmem_limit_bytes=VMEM_BYTES),
        cost_estimate=pl.CostEstimate(
            flops=2 * steps * rows * (5 * length * HEAD_SIZE + width * HEAD_SIZE),
            bytes_accessed=steps * (2 * width * block_cols + 2 * rows * length),
            transcendentals=0,
        ),
        name="attention_back",
    )(core, resid, own, queries, probs, key, value_t, *carried, *others)


def swapped(block, axis):
    return lax.ppermute(block, axis, [(0, 1), (1, 0)])


def shifted(block, axis, by):
    count = lax.axis_size(axis)
    return lax.ppermute(block, axis, [(i, (i + by) % count) for i in range(count)])


def to_chips(chunks):
    sent = chunks.reshape(EXPERTS, BATCH, -1)
    return lax.all_to_all(sent, CHIPS, split_axis=0, concat_axis=0, tiled=True).reshape(
        chunks.shape
    )


def body(
    hidden_in,
    out_grad,
    queries,
    keys,
    values,
    out_proj,
    expert_ids,
    gate_probs,
    w_gate,
    w_up,
    w_down,
):
    tokens, width = hidden_in.shape[1:]
    zlo = lax.axis_index("zlo")
    y_at = lax.axis_index("y")
    y_count = lax.axis_size("y")
    core = lax.axis_index("core").astype(jnp.int32).reshape(1)
    own = (w_gate, w_up, w_down)
    other = tuple(swapped(w, "core") for w in own)

    ids = expert_ids[0].T

    kv = jnp.stack([keys[0], values[0]]).reshape(2, tokens, GROUPS, HEAD_SIZE)
    own_kv = lax.dynamic_index_in_dim(kv, zlo, 2, keepdims=False)
    near_kv = swapped(lax.dynamic_index_in_dim(kv, 1 - zlo, 2, keepdims=False), "zlo")
    pair_kv = jnp.where(zlo == 0, jnp.stack([own_kv, near_kv]), jnp.stack([near_kv, own_kv]))

    chunks = pick(ids, hidden_in[0], out_grad[0])
    chunks, pair_kv = lax.optimization_barrier((chunks, pair_kv))
    came = to_chips(chunks)

    all_kv = jnp.stack([pair_kv] + [shifted(pair_kv, "y", k) for k in range(1, y_count)])
    group_width = width // GROUPS
    own_query = lax.dynamic_slice_in_dim(queries[0], zlo * group_width, group_width, 1)
    near_query = swapped(
        lax.dynamic_slice_in_dim(queries[0], (1 - zlo) * group_width, group_width, 1), "zlo"
    )
    came, all_kv, near_query = lax.optimization_barrier((came, all_kv, near_query))
    back_by = jnp.remainder(y_at - jnp.arange(y_count), y_count)
    all_kv = jnp.take(all_kv, back_by, axis=0).transpose(2, 1, 0, 3, 4).reshape(2, -1, HEAD_SIZE)
    key, value = all_kv[0], all_kv[1]
    key_t, value_t = key.T, value.T
    block_heads = out_proj.shape[0] // HEAD_SIZE
    own_row = ((zlo * y_count + y_at) * tokens).astype(jnp.int32).reshape(1)
    near_row = (((1 - zlo) * y_count + y_at) * tokens).astype(jnp.int32).reshape(1)
    own_probs = softmax_probs(own_row, own_query, key_t, block_heads)
    near_probs = softmax_probs(near_row, near_query, key_t, block_heads)

    back = expert_back(came, own, other)

    proj_own = lax.all_gather(turned(out_proj), PLANE, axis=0, tiled=False)
    proj_own = proj_own.reshape(y_count, -1, *proj_own.shape[1:])
    proj_own, _ = lax.optimization_barrier((proj_own, back))
    halves = y_count // 2
    proj_other = [swapped(proj_own[i : i + 1], "core") for i in range(y_count)]
    result = to_chips(back)
    resid = mix(ids, gate_probs[0].T, out_grad[0], result)
    near_resid = swapped(resid, "zlo")

    dquery, *sums = attention_back(
        core, resid, proj_own, proj_other, own_query, own_probs, key, value_t, 0, (), False
    )
    near = (near_query, near_probs, key, value_t)
    near_first, *sums = attention_back(
        core, near_resid, proj_own, proj_other[:halves], *near, 0, sums, False
    )
    near_second, dkv = attention_back(
        core, near_resid, proj_own, proj_other[halves:], *near, halves, sums, True
    )
    far_first = swapped(near_first, "zlo")
    dkv, far_first = lax.optimization_barrier((dkv, far_first))
    far_dquery = jnp.concatenate([far_first, swapped(near_second, "zlo")], axis=1)
    dquery = jnp.where(
        zlo == 0,
        jnp.concatenate([dquery, far_dquery], axis=1),
        jnp.concatenate([far_dquery, dquery], axis=1),
    )
    sent = lax.all_to_all(
        dkv.reshape(-1, tokens, 2 * HEAD_SIZE), SEQ, split_axis=0, concat_axis=0, tiled=True
    )
    sent = sent.reshape(GROUPS, y_count, tokens, 2 * HEAD_SIZE)
    sums = jnp.sum(sent.astype(F32), axis=1).astype(BF16)
    dkey = jnp.concatenate([sums[g, :, :HEAD_SIZE] for g in range(GROUPS)], axis=1)
    dvalue = jnp.concatenate([sums[g, :, HEAD_SIZE:] for g in range(GROUPS)], axis=1)
    return resid[None], dquery[None], dkey[None], dvalue[None]


def solution(mesh):
    fine = Mesh(mesh.devices.reshape(2, 4, 2, 4, 2), ("zlo", "y", "zhi", "x", "core"))
    dp = ("zhi", "x", "core")
    token_spec = P(dp, SEQ, None)
    weight_spec = P((*SEQ, *dp), None, None)
    return jax.shard_map(
        body,
        mesh=fine,
        in_specs=(token_spec,) * 5
        + (P(SEQ, dp), token_spec, token_spec, weight_spec, weight_spec, weight_spec),
        out_specs=(token_spec,) * 4,
        check_vma=False,
    )
```

```python
import functools

import jax
import jax.numpy as jnp
import numpy as np
from jax import lax
from jax.experimental import pallas as pl
from jax.experimental.pallas import tpu as pltpu
from jax.sharding import Mesh
from jax.sharding import PartitionSpec as P

HEAD_SIZE = 128
GROUPS = 2
CAPACITY = 5
EXPERTS = 64
SLOTS = EXPERTS * CAPACITY
SEQ = ("zlo", "y")
CHIPS = ("zlo", "y", "zhi", "x")
PLANE = ("y", "zhi", "x")
BLOCK = 512
PIECES = 8
BATCH = PIECES * CAPACITY
HIDDEN_TILE = 256
VMEM_BYTES = 60 * 1024 * 1024
NT = (((1,), (1,)), ((), ()))
TN = (((0,), (0,)), ((), ()))
F32 = jnp.float32
BF16 = jnp.bfloat16


def chunk_order():
    count = PIECES * BATCH
    row = lax.broadcasted_iota(jnp.int32, (count, 1), 0)
    chip = (row * 1639) >> 16
    rest = row - chip * BATCH
    piece = (rest * 205) >> 10
    moved = piece * BATCH + chip * CAPACITY + rest - piece * CAPACITY
    return jnp.where(
        lax.broadcasted_iota(jnp.int32, (count, count), 1) == moved, 1.0, 0.0
    ).astype(BF16)


def reordered(order, rows):
    return jnp.dot(order, rows, preferred_element_type=F32)


def slot_rows(ids):
    tokens = ids.shape[1]
    expert = lax.broadcasted_iota(jnp.int32, (EXPERTS, tokens), 0)
    chosen = [ids[k : k + 1] for k in range(ids.shape[0])]
    hots = [jnp.where(expert == e, 1.0, 0.0) for e in chosen]
    before = jnp.where(
        lax.broadcasted_iota(jnp.int32, (tokens, tokens), 0)
        < lax.broadcasted_iota(jnp.int32, (tokens, tokens), 1),
        1.0,
        0.0,
    ).astype(BF16)
    earlier = jnp.dot(sum(hots).astype(BF16), before, preferred_element_type=F32)
    return [
        e * CAPACITY + jnp.sum(earlier * hot, axis=0, keepdims=True).astype(jnp.int32)
        for e, hot in zip(chosen, hots)
    ]


def pick_kernel(ids, hidden, grads, out, rows, row_grads, chunks, sems):
    slot = lax.broadcasted_iota(jnp.int32, (SLOTS, ids.shape[1]), 0)
    picking = sum(jnp.where(slot == row, 1.0, 0.0) for row in slot_rows(ids)).astype(BF16)
    for piece in range(PIECES):
        at = slice(piece * BLOCK, (piece + 1) * BLOCK)
        rows[:, at] = jnp.dot(picking, hidden[:, at], preferred_element_type=F32)
        row_grads[:, at] = jnp.dot(picking, grads[:, at], preferred_element_type=F32)
    order = chunk_order()
    leaving = []
    for g in range(SLOTS // BATCH):
        slots = slice(g * BATCH, (g + 1) * BATCH)
        at = slice(g * PIECES * BATCH, (g + 1) * PIECES * BATCH)
        for side, source in enumerate((rows, row_grads)):
            pieces = [source[slots, p * BLOCK : (p + 1) * BLOCK] for p in range(PIECES)]
            sent = reordered(order, jnp.concatenate(pieces, axis=0).astype(BF16))
            chunks[at, side * BLOCK : (side + 1) * BLOCK] = sent.astype(BF16)
        copy = pltpu.make_async_copy(chunks.at[at], out.at[at], sems.at[g])
        copy.start()
        leaving.append(copy)
    for copy in leaving:
        copy.wait()


def pick(ids, hidden, grads):
    width = hidden.shape[1]
    held = pl.BlockSpec(memory_space=pltpu.VMEM)
    return pl.pallas_call(
        pick_kernel,
        in_specs=[held] * 3,
        out_specs=pl.BlockSpec(memory_space=pl.ANY),
        out_shape=jax.ShapeDtypeStruct((EXPERTS * BATCH, 2 * BLOCK), BF16),
        scratch_shapes=[pltpu.VMEM((SLOTS, width), F32)] * 2
        + [
            pltpu.VMEM((EXPERTS * BATCH, 2 * BLOCK), BF16),
            pltpu.SemaphoreType.DMA((SLOTS // BATCH,)),
        ],
        compiler_params=pltpu.CompilerParams(vmem_limit_bytes=VMEM_BYTES),
        cost_estimate=pl.CostEstimate(
            flops=8 * SLOTS * SLOTS * width, bytes_accessed=8 * SLOTS * width, transcendentals=0
        ),
        name="pick",
    )(ids, hidden, grads)


def mix_kernel(ids, probs, grads, came, out, rows):
    order = chunk_order()
    for g in range(SLOTS // BATCH):
        batch = came[g * PIECES * BATCH : (g + 1) * PIECES * BATCH]
        batch = reordered(order, batch)
        for p in range(PIECES):
            rows[g * BATCH : (g + 1) * BATCH, p * BLOCK : (p + 1) * BLOCK] = batch[
                p * BATCH : (p + 1) * BATCH
            ]
    slot = lax.broadcasted_iota(jnp.int32, (SLOTS, ids.shape[1]), 0)
    mixing = sum(
        jnp.where(slot == row, probs[k : k + 1], 0.0) for k, row in enumerate(slot_rows(ids))
    )
    mixing = jnp.transpose(mixing)
    mixing_high = mixing.astype(BF16)
    mixing_low = (mixing - mixing_high.astype(F32)).astype(BF16)
    for p in range(PIECES):
        at = slice(p * BLOCK, (p + 1) * BLOCK)
        block = rows[:, at].astype(BF16)
        mixed = jnp.dot(mixing_high, block, preferred_element_type=F32)
        mixed += jnp.dot(mixing_low, block, preferred_element_type=F32)
        out[:, at] = (grads[:, at].astype(F32) + mixed).astype(BF16)


def mix(ids, probs, grads, came):
    held = pl.BlockSpec(memory_space=pltpu.VMEM)
    return pl.pallas_call(
        mix_kernel,
        in_specs=[held] * 4,
        out_specs=held,
        out_shape=jax.ShapeDtypeStruct(grads.shape, BF16),
        scratch_shapes=[pltpu.VMEM((SLOTS, grads.shape[1]), F32)],
        compiler_params=pltpu.CompilerParams(vmem_limit_bytes=VMEM_BYTES),
        name="mix",
    )(ids, probs, grads, came)


def turn_kernel(block, out):
    out[...] = jnp.transpose(block[...])


def turned(block):
    held = pl.BlockSpec(memory_space=pltpu.VMEM)
    return pl.pallas_call(
        turn_kernel,
        in_specs=[held],
        out_specs=held,
        out_shape=jax.ShapeDtypeStruct(block.shape[::-1], block.dtype),
        compiler_params=pltpu.CompilerParams(vmem_limit_bytes=VMEM_BYTES),
        name="turned",
    )(block)


def expert_kernel(
    g0, u0, d0, g1, u1, d1, sent, out, came, rows, grads, gate, up, down, d_gate, d_up, sems, edge_sems
):
    arrival = pltpu.make_async_copy(sent, came, edge_sems.at[0])
    arrival.start()
    halves, width, half = gate.shape
    tile = 512
    loads = []
    for h, (g, u, d) in enumerate(((g0, u0, d0), (g1, u1, d1))):
        for at in range(0, half, HIDDEN_TILE):
            part = slice(at, at + HIDDEN_TILE)
            copies = [
                pltpu.make_async_copy(g.at[0, :, part], gate.at[h, :, part], sems.at[len(loads), 0]),
                pltpu.make_async_copy(u.at[0, :, part], up.at[h, :, part], sems.at[len(loads), 1]),
                pltpu.make_async_copy(d.at[0, part, :], down.at[h, part, :], sems.at[len(loads), 2]),
            ]
            loads.append((h, part, copies))

    def load(number):
        if number < len(loads):
            for copy in loads[number][2]:
                copy.start()

    load(0)
    size = PIECES * BATCH
    order = chunk_order()
    arrival.wait()
    load(1)
    for g in range(0, SLOTS // BATCH, 2):
        batches = [reordered(order, came[(g + i) * size : (g + i + 1) * size]) for i in range(2)]
        slots = slice(g * BATCH, (g + 2) * BATCH)
        for p in range(PIECES):
            pair = [batch[p * BATCH : (p + 1) * BATCH] for batch in batches]
            pair = jnp.concatenate(pair, axis=0).astype(BF16)
            rows[slots, p * BLOCK : (p + 1) * BLOCK] = pair[:, :BLOCK]
            grads[slots, p * BLOCK : (p + 1) * BLOCK] = pair[:, BLOCK:]
    for number, (h, part, copies) in enumerate(loads):
        load(number + 2)
        for copy in copies:
            copy.wait()
        pre_gate = jnp.dot(rows[...], gate[h, :, part], preferred_element_type=F32)
        pre_up = jnp.dot(rows[...], up[h, :, part], preferred_element_type=F32)
        upstream = lax.dot_general(grads[...], down[h, part, :], NT, preferred_element_type=F32)
        sig = jax.nn.sigmoid(pre_gate)
        d_gate[h, :, part] = (upstream * pre_up * sig * (1.0 + pre_gate * (1.0 - sig))).astype(BF16)
        d_up[h, :, part] = (upstream * pre_gate * sig).astype(BF16)

    @pl.loop(0, width // tile)
    def _(i):
        at = pl.ds(pl.multiple_of(i * tile, tile), tile)
        total = lax.dot_general(d_gate[0], gate[0, at, :], NT, preferred_element_type=F32)
        total += lax.dot_general(d_up[0], up[0, at, :], NT, preferred_element_type=F32)
        for h in range(1, halves):
            total += lax.dot_general(d_gate[h], gate[h, at, :], NT, preferred_element_type=F32)
            total += lax.dot_general(d_up[h], up[h, at, :], NT, preferred_element_type=F32)
        rows[:, at] = total.astype(BF16)

    leaving = []
    for g in range(0, SLOTS // BATCH, 2):
        slots = slice(g * BATCH, (g + 2) * BATCH)
        pieces = [rows[slots, p * BLOCK : (p + 1) * BLOCK].astype(F32) for p in range(PIECES)]
        for i in range(2):
            batch = [piece[i * BATCH : (i + 1) * BATCH] for piece in pieces]
            batch = jnp.concatenate(batch, axis=0).astype(BF16)
            at = slice((g + i) * size, (g + i + 1) * size)
            came[at, :BLOCK] = reordered(order, batch).astype(BF16)
            copy = pltpu.make_async_copy(came.at[at, :BLOCK], out.at[at], edge_sems.at[1 + g + i])
            copy.start()
            leaving.append(copy)
    for copy in leaving:
        copy.wait()


def expert_back(sent, own, other):
    width, half = own[0].shape[1:]
    far = pl.BlockSpec(memory_space=pl.ANY)
    return pl.pallas_call(
        expert_kernel,
        in_specs=[far] * 7,
        out_specs=far,
        out_shape=jax.ShapeDtypeStruct((EXPERTS * BATCH, BLOCK), BF16),
        scratch_shapes=[
            pltpu.VMEM(sent.shape, BF16),
            pltpu.VMEM((SLOTS, width), BF16),
            pltpu.VMEM((SLOTS, width), BF16),
            pltpu.VMEM((2, width, half), BF16),
            pltpu.VMEM((2, width, half), BF16),
            pltpu.VMEM((2, half, width), BF16),
            pltpu.VMEM((2, SLOTS, half), BF16),
            pltpu.VMEM((2, SLOTS, half), BF16),
            pltpu.SemaphoreType.DMA((2 * half // HIDDEN_TILE, 3)),
            pltpu.SemaphoreType.DMA((1 + SLOTS // BATCH,)),
        ],
        compiler_params=pltpu.CompilerParams(vmem_limit_bytes=VMEM_BYTES),
        cost_estimate=pl.CostEstimate(
            flops=20 * SLOTS * width * half, bytes_accessed=12 * width * half, transcendentals=0
        ),
        name="expert_back",
    )(*own, *other, sent)


def stack_heads(block):
    heads = block.shape[1] // HEAD_SIZE
    return jnp.concatenate(
        [block[:, h * HEAD_SIZE : (h + 1) * HEAD_SIZE] for h in range(heads)], axis=0
    )


def softmax_kernel(first_row, query, key, probs):
    scale = HEAD_SIZE ** (-0.5)
    tokens = query.shape[0]
    scores = jnp.dot(stack_heads(query[...]), key[...], preferred_element_type=F32) * scale
    row = lax.broadcasted_iota(jnp.int32, scores.shape, 0) % tokens + first_row[0]
    col = lax.broadcasted_iota(jnp.int32, scores.shape, 1)
    scores = jnp.where(col <= row, scores, -1e30)
    weights = jnp.exp(scores - jnp.max(scores, axis=1, keepdims=True))
    probs[...] = (weights / jnp.sum(weights, axis=1, keepdims=True)).astype(BF16)


def softmax_probs(first_row, queries, key, block_heads):
    tokens, width = queries.shape
    length = key.shape[1]
    rows = block_heads * tokens
    steps = width // (block_heads * HEAD_SIZE)
    return pl.pallas_call(
        softmax_kernel,
        grid=(steps,),
        in_specs=[
            pl.BlockSpec(memory_space=pltpu.SMEM),
            pl.BlockSpec((tokens, block_heads * HEAD_SIZE), lambda i: (0, i)),
            pl.BlockSpec((HEAD_SIZE, length), lambda i: (0, 0)),
        ],
        out_specs=pl.BlockSpec((rows, length), lambda i: (i, 0)),
        out_shape=jax.ShapeDtypeStruct((steps * rows, length), BF16),
        compiler_params=pltpu.CompilerParams(vmem_limit_bytes=VMEM_BYTES),
        cost_estimate=pl.CostEstimate(
            flops=20 * steps * rows * length * HEAD_SIZE,
            bytes_accessed=2 * steps * rows * length,
            transcendentals=steps * rows * length,
        ),
        name="softmax_probs",
    )(first_row, queries, key)


def attention_kernel(begins, ends, core, resid, own, query, probs, key, value_t, *refs):
    ctx, refs = refs[-1], refs[:-1]
    steps = pl.num_programs(0)
    if not begins:
        dkey_in, dvalue_in = refs[:2]
        refs = refs[2:]
    if ends:
        *others, dquery, dkv, dkey, dvalue = refs
    else:
        *others, dquery, dkey, dvalue = refs
    step = pl.program_id(0)
    scale = HEAD_SIZE ** (-0.5)
    tokens = query.shape[0]
    pieces, depth, block_cols = own.shape[1:]

    @pl.when(step == 0)
    def _():
        if begins:
            dkey[...] = jnp.zeros_like(dkey)
            dvalue[...] = jnp.zeros_like(dvalue)
        else:
            dkey[...] = dkey_in[...]
            dvalue[...] = dvalue_in[...]

    def project(side, shard):
        total = jnp.zeros((tokens, block_cols), F32)
        for piece in range(pieces):
            at = pl.ds(pl.multiple_of((2 * piece + side) * depth, depth), depth)
            total += jnp.dot(resid[:, at], shard[0, piece], preferred_element_type=F32)
        return total

    for j, other in enumerate(others):

        @pl.when(step * len(others) // steps == j)
        def _(other=other):
            ctx[...] = project(1 - core[0], other)

    ctx = stack_heads((ctx[...] + project(core[0], own)).astype(BF16))
    query_rows = stack_heads(query[...])
    low = probs[...]
    weights = low.astype(F32)
    dprobs = jnp.dot(ctx, value_t[...], preferred_element_type=F32)
    delta = jnp.sum(weights * dprobs, axis=1, keepdims=True)
    dscores = (weights * (dprobs - delta)).astype(BF16)
    dq = jnp.dot(dscores, key[...], preferred_element_type=F32) * scale
    for h in range(query.shape[1] // HEAD_SIZE):
        dquery[:, h * HEAD_SIZE : (h + 1) * HEAD_SIZE] = dq[h * tokens : (h + 1) * tokens].astype(
            BF16
        )
    dkey[...] += lax.dot_general(query_rows, dscores, TN, preferred_element_type=F32)
    dvalue[...] += lax.dot_general(ctx, low, TN, preferred_element_type=F32)

    if ends:

        @pl.when(step == steps - 1)
        def _():
            dkv[:, :HEAD_SIZE] = jnp.transpose(dkey[...] * scale).astype(BF16)
            dkv[:, HEAD_SIZE:] = jnp.transpose(dvalue[...]).astype(BF16)


def attention_back(core, resid, own, others, queries, probs, key, value_t, first, carried, ends):
    tokens, width = resid.shape
    pieces, depth, block_cols = own.shape[1:]
    each = others[0].shape[0]
    steps = each * len(others)
    length = key.shape[0]
    rows = tokens * block_cols // HEAD_SIZE

    def whole(*shape):
        return pl.BlockSpec(shape, lambda i: (0,) * len(shape))

    shard = (1, pieces, depth, block_cols)
    in_specs = [
        pl.BlockSpec(memory_space=pltpu.SMEM),
        whole(tokens, width),
        pl.BlockSpec(shard, lambda i: (first + i, 0, 0, 0)),
        pl.BlockSpec((tokens, block_cols), lambda i: (0, first + i)),
        pl.BlockSpec((rows, length), lambda i: (first + i, 0)),
        whole(length, HEAD_SIZE),
        whole(HEAD_SIZE, length),
    ]
    in_specs += [whole(HEAD_SIZE, length)] * len(carried)
    for j in range(len(others)):
        in_specs.append(
            pl.BlockSpec(shard, lambda i, j=j: (jnp.clip(i - j * each, 0, each - 1), 0, 0, 0))
        )
    sums = jax.ShapeDtypeStruct((HEAD_SIZE, length), F32)
    out_specs = [pl.BlockSpec((tokens, block_cols), lambda i: (0, i))]
    out_shape = [jax.ShapeDtypeStruct((tokens, steps * block_cols), BF16)]
    scratch = [pltpu.VMEM((tokens, block_cols), F32)]
    if ends:
        out_specs += [whole(length, 2 * HEAD_SIZE)]
        out_shape += [jax.ShapeDtypeStruct((length, 2 * HEAD_SIZE), BF16)]
        scratch = [pltpu.VMEM((HEAD_SIZE, length), F32)] * 2 + scratch
    else:
        out_specs += [whole(HEAD_SIZE, length)] * 2
        out_shape += [sums, sums]
    return pl.pallas_call(
        functools.partial(attention_kernel, not carried, ends),
        grid=(steps,),
        in_specs=in_specs,
        out_specs=out_specs,
        scratch_shapes=scratch,
        out_shape=out_shape,
        compiler_params=pltpu.CompilerParams(vmem_limit_bytes=VMEM_BYTES),
        cost_estimate=pl.CostEstimate(
            flops=2 * steps * rows * (5 * length * HEAD_SIZE + width * HEAD_SIZE),
            bytes_accessed=steps * (2 * width * block_cols + 2 * rows * length),
            transcendentals=0,
        ),
        name="attention_back",
    )(core, resid, own, queries, probs, key, value_t, *carried, *others)


def swapped(block, axis):
    return lax.ppermute(block, axis, [(0, 1), (1, 0)])


def shifted(block, axis, by):
    count = lax.axis_size(axis)
    return lax.ppermute(block, axis, [(i, (i + by) % count) for i in range(count)])


def to_chips(chunks):
    sent = chunks.reshape(EXPERTS, BATCH, -1)
    return lax.all_to_all(sent, CHIPS, split_axis=0, concat_axis=0, tiled=True).reshape(
        chunks.shape
    )


def body(
    hidden_in,
    out_grad,
    queries,
    keys,
    values,
    out_proj,
    expert_ids,
    gate_probs,
    w_gate,
    w_up,
    w_down,
):
    tokens, width = hidden_in.shape[1:]
    zlo = lax.axis_index("zlo")
    y_at = lax.axis_index("y")
    y_count = lax.axis_size("y")
    core = lax.axis_index("core").astype(jnp.int32).reshape(1)
    own = (w_gate, w_up, w_down)
    other = tuple(swapped(w, "core") for w in own)

    ids = expert_ids[0].T

    kv = jnp.stack([keys[0], values[0]]).reshape(2, tokens, GROUPS, HEAD_SIZE)
    own_kv = lax.dynamic_index_in_dim(kv, zlo, 2, keepdims=False)
    near_kv = swapped(lax.dynamic_index_in_dim(kv, 1 - zlo, 2, keepdims=False), "zlo")
    pair_kv = jnp.where(zlo == 0, jnp.stack([own_kv, near_kv]), jnp.stack([near_kv, own_kv]))

    ids, pair_kv = lax.optimization_barrier((ids, pair_kv))
    all_kv = jnp.stack([pair_kv] + [shifted(pair_kv, "y", k) for k in range(1, y_count)])

    chunks = pick(ids, hidden_in[0], out_grad[0])
    chunks, all_kv = lax.optimization_barrier((chunks, all_kv))
    came = to_chips(chunks)

    group_width = width // GROUPS
    own_query = lax.dynamic_slice_in_dim(queries[0], zlo * group_width, group_width, 1)
    near_query = swapped(
        lax.dynamic_slice_in_dim(queries[0], (1 - zlo) * group_width, group_width, 1), "zlo"
    )
    came, near_query = lax.optimization_barrier((came, near_query))
    back_by = jnp.remainder(y_at - jnp.arange(y_count), y_count)
    all_kv = jnp.take(all_kv, back_by, axis=0).transpose(2, 1, 0, 3, 4).reshape(2, -1, HEAD_SIZE)
    key, value = all_kv[0], all_kv[1]
    key_t, value_t = key.T, value.T
    block_heads = out_proj.shape[0] // HEAD_SIZE
    own_row = ((zlo * y_count + y_at) * tokens).astype(jnp.int32).reshape(1)
    near_row = (((1 - zlo) * y_count + y_at) * tokens).astype(jnp.int32).reshape(1)
    own_probs = softmax_probs(own_row, own_query, key_t, block_heads)
    near_probs = softmax_probs(near_row, near_query, key_t, block_heads)

    back = expert_back(came, own, other)

    proj_own = lax.all_gather(turned(out_proj), PLANE, axis=0, tiled=False)
    proj_own = proj_own.reshape(y_count, -1, *proj_own.shape[1:])
    proj_own, _ = lax.optimization_barrier((proj_own, back))
    halves = y_count // 2
    proj_other = [swapped(proj_own[i : i + 1], "core") for i in range(y_count)]
    result = to_chips(back)
    result, own_probs, near_probs = lax.optimization_barrier((result, own_probs, near_probs))
    resid = mix(ids, gate_probs[0].T, out_grad[0], result)
    near_resid = swapped(resid, "zlo")

    dquery, *sums = attention_back(
        core, resid, proj_own, proj_other, own_query, own_probs, key, value_t, 0, (), False
    )
    near = (near_query, near_probs, key, value_t)
    near_first, *sums = attention_back(
        core, near_resid, proj_own, proj_other[:halves], *near, 0, sums, False
    )
    near_second, dkv = attention_back(
        core, near_resid, proj_own, proj_other[halves:], *near, halves, sums, True
    )
    far_first = swapped(near_first, "zlo")
    dkv, far_first = lax.optimization_barrier((dkv, far_first))
    far_dquery = jnp.concatenate([far_first, swapped(near_second, "zlo")], axis=1)
    dquery = jnp.where(
        zlo == 0,
        jnp.concatenate([dquery, far_dquery], axis=1),
        jnp.concatenate([far_dquery, dquery], axis=1),
    )
    sent = lax.all_to_all(
        dkv.reshape(-1, tokens, 2 * HEAD_SIZE), SEQ, split_axis=0, concat_axis=0, tiled=True
    )
    sent = sent.reshape(GROUPS, y_count, tokens, 2 * HEAD_SIZE)
    sums = jnp.sum(sent.astype(F32), axis=1).astype(BF16)
    dkey = jnp.concatenate([sums[g, :, :HEAD_SIZE] for g in range(GROUPS)], axis=1)
    dvalue = jnp.concatenate([sums[g, :, HEAD_SIZE:] for g in range(GROUPS)], axis=1)
    return resid[None], dquery[None], dkey[None], dvalue[None]


def solution(mesh):
    fine = Mesh(mesh.devices.reshape(2, 4, 2, 4, 2), ("zlo", "y", "zhi", "x", "core"))
    dp = ("zhi", "x", "core")
    token_spec = P(dp, SEQ, None)
    weight_spec = P((*SEQ, *dp), None, None)
    return jax.shard_map(
        body,
        mesh=fine,
        in_specs=(token_spec,) * 5
        + (P(SEQ, dp), token_spec, token_spec, weight_spec, weight_spec, weight_spec),
        out_specs=(token_spec,) * 4,
        check_vma=False,
    )
```

```python
import functools

import jax
import jax.numpy as jnp
import numpy as np
from jax import lax
from jax.experimental import pallas as pl
from jax.experimental.pallas import tpu as pltpu
from jax.sharding import Mesh
from jax.sharding import PartitionSpec as P

HEAD_SIZE = 128
GROUPS = 2
CAPACITY = 5
EXPERTS = 64
SLOTS = EXPERTS * CAPACITY
SEQ = ("zlo", "y")
CHIPS = ("zlo", "y", "zhi", "x")
PLANE = ("y", "zhi", "x")
BLOCK = 512
PIECES = 8
BATCH = PIECES * CAPACITY
HIDDEN_TILE = 256
VMEM_BYTES = 60 * 1024 * 1024
NT = (((1,), (1,)), ((), ()))
TN = (((0,), (0,)), ((), ()))
F32 = jnp.float32
BF16 = jnp.bfloat16


def chunk_order():
    count = PIECES * BATCH
    row = lax.broadcasted_iota(jnp.int32, (count, 1), 0)
    chip = (row * 1639) >> 16
    rest = row - chip * BATCH
    piece = (rest * 205) >> 10
    moved = piece * BATCH + chip * CAPACITY + rest - piece * CAPACITY
    return jnp.where(
        lax.broadcasted_iota(jnp.int32, (count, count), 1) == moved, 1.0, 0.0
    ).astype(BF16)


def reordered(order, rows):
    return jnp.dot(order, rows, preferred_element_type=F32)


def slot_rows(ids):
    tokens = ids.shape[1]
    expert = lax.broadcasted_iota(jnp.int32, (EXPERTS, tokens), 0)
    chosen = [ids[k : k + 1] for k in range(ids.shape[0])]
    hots = [jnp.where(expert == e, 1.0, 0.0) for e in chosen]
    before = jnp.where(
        lax.broadcasted_iota(jnp.int32, (tokens, tokens), 0)
        < lax.broadcasted_iota(jnp.int32, (tokens, tokens), 1),
        1.0,
        0.0,
    ).astype(BF16)
    earlier = jnp.dot(sum(hots).astype(BF16), before, preferred_element_type=F32)
    return [
        e * CAPACITY + jnp.sum(earlier * hot, axis=0, keepdims=True).astype(jnp.int32)
        for e, hot in zip(chosen, hots)
    ]


def pick_kernel(ids, hidden, grads, out, rows, row_grads, chunks, sems):
    slot = lax.broadcasted_iota(jnp.int32, (SLOTS, ids.shape[1]), 0)
    picking = sum(jnp.where(slot == row, 1.0, 0.0) for row in slot_rows(ids)).astype(BF16)
    for piece in range(PIECES):
        at = slice(piece * BLOCK, (piece + 1) * BLOCK)
        rows[:, at] = jnp.dot(picking, hidden[:, at], preferred_element_type=F32)
        row_grads[:, at] = jnp.dot(picking, grads[:, at], preferred_element_type=F32)
    order = chunk_order()
    leaving = []
    for g in range(SLOTS // BATCH):
        slots = slice(g * BATCH, (g + 1) * BATCH)
        at = slice(g * PIECES * BATCH, (g + 1) * PIECES * BATCH)
        for side, source in enumerate((rows, row_grads)):
            pieces = [source[slots, p * BLOCK : (p + 1) * BLOCK] for p in range(PIECES)]
            sent = reordered(order, jnp.concatenate(pieces, axis=0).astype(BF16))
            chunks[at, side * BLOCK : (side + 1) * BLOCK] = sent.astype(BF16)
        copy = pltpu.make_async_copy(chunks.at[at], out.at[at], sems.at[g])
        copy.start()
        leaving.append(copy)
    for copy in leaving:
        copy.wait()


def pick(ids, hidden, grads):
    width = hidden.shape[1]
    held = pl.BlockSpec(memory_space=pltpu.VMEM)
    return pl.pallas_call(
        pick_kernel,
        in_specs=[held] * 3,
        out_specs=pl.BlockSpec(memory_space=pl.ANY),
        out_shape=jax.ShapeDtypeStruct((EXPERTS * BATCH, 2 * BLOCK), BF16),
        scratch_shapes=[pltpu.VMEM((SLOTS, width), F32)] * 2
        + [
            pltpu.VMEM((EXPERTS * BATCH, 2 * BLOCK), BF16),
            pltpu.SemaphoreType.DMA((SLOTS // BATCH,)),
        ],
        compiler_params=pltpu.CompilerParams(vmem_limit_bytes=VMEM_BYTES),
        cost_estimate=pl.CostEstimate(
            flops=8 * SLOTS * SLOTS * width, bytes_accessed=8 * SLOTS * width, transcendentals=0
        ),
        name="pick",
    )(ids, hidden, grads)


def mix_kernel(ids, probs, grads, came, out, rows):
    order = chunk_order()
    for g in range(SLOTS // BATCH):
        batch = came[g * PIECES * BATCH : (g + 1) * PIECES * BATCH]
        batch = reordered(order, batch)
        for p in range(PIECES):
            rows[g * BATCH : (g + 1) * BATCH, p * BLOCK : (p + 1) * BLOCK] = batch[
                p * BATCH : (p + 1) * BATCH
            ]
    slot = lax.broadcasted_iota(jnp.int32, (SLOTS, ids.shape[1]), 0)
    mixing = sum(
        jnp.where(slot == row, probs[k : k + 1], 0.0) for k, row in enumerate(slot_rows(ids))
    )
    mixing = jnp.transpose(mixing)
    mixing_high = mixing.astype(BF16)
    mixing_low = (mixing - mixing_high.astype(F32)).astype(BF16)
    for p in range(PIECES):
        at = slice(p * BLOCK, (p + 1) * BLOCK)
        block = rows[:, at].astype(BF16)
        mixed = jnp.dot(mixing_high, block, preferred_element_type=F32)
        mixed += jnp.dot(mixing_low, block, preferred_element_type=F32)
        out[:, at] = (grads[:, at].astype(F32) + mixed).astype(BF16)


def mix(ids, probs, grads, came):
    held = pl.BlockSpec(memory_space=pltpu.VMEM)
    return pl.pallas_call(
        mix_kernel,
        in_specs=[held] * 4,
        out_specs=held,
        out_shape=jax.ShapeDtypeStruct(grads.shape, BF16),
        scratch_shapes=[pltpu.VMEM((SLOTS, grads.shape[1]), F32)],
        compiler_params=pltpu.CompilerParams(vmem_limit_bytes=VMEM_BYTES),
        name="mix",
    )(ids, probs, grads, came)


def turn_kernel(block, out):
    out[...] = jnp.transpose(block[...])


def turned(block):
    held = pl.BlockSpec(memory_space=pltpu.VMEM)
    return pl.pallas_call(
        turn_kernel,
        in_specs=[held],
        out_specs=held,
        out_shape=jax.ShapeDtypeStruct(block.shape[::-1], block.dtype),
        compiler_params=pltpu.CompilerParams(vmem_limit_bytes=VMEM_BYTES),
        name="turned",
    )(block)


def expert_kernel(
    g0, u0, d0, g1, u1, d1, sent, out, came, rows, grads, gate, up, down, d_gate, d_up, sems, edge_sems
):
    arrival = pltpu.make_async_copy(sent, came, edge_sems.at[0])
    arrival.start()
    halves, width, half = gate.shape
    tile = 512
    loads = []
    for h, (g, u, d) in enumerate(((g0, u0, d0), (g1, u1, d1))):
        for at in range(0, half, HIDDEN_TILE):
            part = slice(at, at + HIDDEN_TILE)
            copies = [
                pltpu.make_async_copy(g.at[0, :, part], gate.at[h, :, part], sems.at[len(loads), 0]),
                pltpu.make_async_copy(u.at[0, :, part], up.at[h, :, part], sems.at[len(loads), 1]),
                pltpu.make_async_copy(d.at[0, part, :], down.at[h, part, :], sems.at[len(loads), 2]),
            ]
            loads.append((h, part, copies))

    def load(number):
        if number < len(loads):
            for copy in loads[number][2]:
                copy.start()

    load(0)
    size = PIECES * BATCH
    order = chunk_order()
    arrival.wait()
    load(1)
    for g in range(0, SLOTS // BATCH, 2):
        batches = [reordered(order, came[(g + i) * size : (g + i + 1) * size]) for i in range(2)]
        slots = slice(g * BATCH, (g + 2) * BATCH)
        for p in range(PIECES):
            pair = [batch[p * BATCH : (p + 1) * BATCH] for batch in batches]
            pair = jnp.concatenate(pair, axis=0).astype(BF16)
            rows[slots, p * BLOCK : (p + 1) * BLOCK] = pair[:, :BLOCK]
            grads[slots, p * BLOCK : (p + 1) * BLOCK] = pair[:, BLOCK:]
    for number, (h, part, copies) in enumerate(loads):
        load(number + 2)
        for copy in copies:
            copy.wait()
        pre_gate = jnp.dot(rows[...], gate[h, :, part], preferred_element_type=F32)
        pre_up = jnp.dot(rows[...], up[h, :, part], preferred_element_type=F32)
        upstream = lax.dot_general(grads[...], down[h, part, :], NT, preferred_element_type=F32)
        sig = jax.nn.sigmoid(pre_gate)
        d_gate[h, :, part] = (upstream * pre_up * sig * (1.0 + pre_gate * (1.0 - sig))).astype(BF16)
        d_up[h, :, part] = (upstream * pre_gate * sig).astype(BF16)

    @pl.loop(0, width // tile)
    def _(i):
        at = pl.ds(pl.multiple_of(i * tile, tile), tile)
        total = lax.dot_general(d_gate[0], gate[0, at, :], NT, preferred_element_type=F32)
        total += lax.dot_general(d_up[0], up[0, at, :], NT, preferred_element_type=F32)
        for h in range(1, halves):
            total += lax.dot_general(d_gate[h], gate[h, at, :], NT, preferred_element_type=F32)
            total += lax.dot_general(d_up[h], up[h, at, :], NT, preferred_element_type=F32)
        rows[:, at] = total.astype(BF16)

    leaving = []
    for g in range(0, SLOTS // BATCH, 2):
        slots = slice(g * BATCH, (g + 2) * BATCH)
        pieces = [rows[slots, p * BLOCK : (p + 1) * BLOCK].astype(F32) for p in range(PIECES)]
        for i in range(2):
            batch = [piece[i * BATCH : (i + 1) * BATCH] for piece in pieces]
            batch = jnp.concatenate(batch, axis=0).astype(BF16)
            at = slice((g + i) * size, (g + i + 1) * size)
            came[at, :BLOCK] = reordered(order, batch).astype(BF16)
            copy = pltpu.make_async_copy(came.at[at, :BLOCK], out.at[at], edge_sems.at[1 + g + i])
            copy.start()
            leaving.append(copy)
    for copy in leaving:
        copy.wait()


def expert_back(sent, own, other):
    width, half = own[0].shape[1:]
    far = pl.BlockSpec(memory_space=pl.ANY)
    return pl.pallas_call(
        expert_kernel,
        in_specs=[far] * 7,
        out_specs=far,
        out_shape=jax.ShapeDtypeStruct((EXPERTS * BATCH, BLOCK), BF16),
        scratch_shapes=[
            pltpu.VMEM(sent.shape, BF16),
            pltpu.VMEM((SLOTS, width), BF16),
            pltpu.VMEM((SLOTS, width), BF16),
            pltpu.VMEM((2, width, half), BF16),
            pltpu.VMEM((2, width, half), BF16),
            pltpu.VMEM((2, half, width), BF16),
            pltpu.VMEM((2, SLOTS, half), BF16),
            pltpu.VMEM((2, SLOTS, half), BF16),
            pltpu.SemaphoreType.DMA((2 * half // HIDDEN_TILE, 3)),
            pltpu.SemaphoreType.DMA((1 + SLOTS // BATCH,)),
        ],
        compiler_params=pltpu.CompilerParams(vmem_limit_bytes=VMEM_BYTES),
        cost_estimate=pl.CostEstimate(
            flops=20 * SLOTS * width * half, bytes_accessed=12 * width * half, transcendentals=0
        ),
        name="expert_back",
    )(*own, *other, sent)


def stack_heads(block):
    heads = block.shape[1] // HEAD_SIZE
    return jnp.concatenate(
        [block[:, h * HEAD_SIZE : (h + 1) * HEAD_SIZE] for h in range(heads)], axis=0
    )


def softmax_kernel(first_row, query, key, probs):
    scale = HEAD_SIZE ** (-0.5)
    tokens = query.shape[0]
    scores = jnp.dot(stack_heads(query[...]), key[...], preferred_element_type=F32) * scale
    row = lax.broadcasted_iota(jnp.int32, scores.shape, 0) % tokens + first_row[0]
    col = lax.broadcasted_iota(jnp.int32, scores.shape, 1)
    scores = jnp.where(col <= row, scores, -1e30)
    weights = jnp.exp(scores - jnp.max(scores, axis=1, keepdims=True))
    probs[...] = (weights / jnp.sum(weights, axis=1, keepdims=True)).astype(BF16)


def softmax_probs(first_row, queries, key, block_heads):
    tokens, width = queries.shape
    length = key.shape[1]
    rows = block_heads * tokens
    steps = width // (block_heads * HEAD_SIZE)
    return pl.pallas_call(
        softmax_kernel,
        grid=(steps,),
        in_specs=[
            pl.BlockSpec(memory_space=pltpu.SMEM),
            pl.BlockSpec((tokens, block_heads * HEAD_SIZE), lambda i: (0, i)),
            pl.BlockSpec((HEAD_SIZE, length), lambda i: (0, 0)),
        ],
        out_specs=pl.BlockSpec((rows, length), lambda i: (i, 0)),
        out_shape=jax.ShapeDtypeStruct((steps * rows, length), BF16),
        compiler_params=pltpu.CompilerParams(vmem_limit_bytes=VMEM_BYTES),
        cost_estimate=pl.CostEstimate(
            flops=20 * steps * rows * length * HEAD_SIZE,
            bytes_accessed=2 * steps * rows * length,
            transcendentals=steps * rows * length,
        ),
        name="softmax_probs",
    )(first_row, queries, key)


def attention_kernel(begins, ends, core, resid, own, query, probs, key, value_t, *refs):
    ctx, refs = refs[-1], refs[:-1]
    steps = pl.num_programs(0)
    if not begins:
        dkey_in, dvalue_in = refs[:2]
        refs = refs[2:]
    if ends:
        *others, dquery, dkv, dkey, dvalue = refs
    else:
        *others, dquery, dkey, dvalue = refs
    step = pl.program_id(0)
    scale = HEAD_SIZE ** (-0.5)
    tokens = query.shape[0]
    pieces, depth, block_cols = own.shape[1:]

    @pl.when(step == 0)
    def _():
        if begins:
            dkey[...] = jnp.zeros_like(dkey)
            dvalue[...] = jnp.zeros_like(dvalue)
        else:
            dkey[...] = dkey_in[...]
            dvalue[...] = dvalue_in[...]

    def project(side, shard):
        total = jnp.zeros((tokens, block_cols), F32)
        for piece in range(pieces):
            at = pl.ds(pl.multiple_of((2 * piece + side) * depth, depth), depth)
            total += jnp.dot(resid[:, at], shard[0, piece], preferred_element_type=F32)
        return total

    for j, other in enumerate(others):

        @pl.when(step * len(others) // steps == j)
        def _(other=other):
            ctx[...] = project(1 - core[0], other)

    ctx = stack_heads((ctx[...] + project(core[0], own)).astype(BF16))
    query_rows = stack_heads(query[...])
    low = probs[...]
    weights = low.astype(F32)
    dprobs = jnp.dot(ctx, value_t[...], preferred_element_type=F32)
    delta = jnp.sum(weights * dprobs, axis=1, keepdims=True)
    dscores = (weights * (dprobs - delta)).astype(BF16)
    dq = jnp.dot(dscores, key[...], preferred_element_type=F32) * scale
    for h in range(query.shape[1] // HEAD_SIZE):
        dquery[:, h * HEAD_SIZE : (h + 1) * HEAD_SIZE] = dq[h * tokens : (h + 1) * tokens].astype(
            BF16
        )
    dkey[...] += lax.dot_general(query_rows, dscores, TN, preferred_element_type=F32)
    dvalue[...] += lax.dot_general(ctx, low, TN, preferred_element_type=F32)

    if ends:

        @pl.when(step == steps - 1)
        def _():
            dkv[:, :HEAD_SIZE] = jnp.transpose(dkey[...] * scale).astype(BF16)
            dkv[:, HEAD_SIZE:] = jnp.transpose(dvalue[...]).astype(BF16)


def attention_back(core, resid, own, others, queries, probs, key, value_t, first, carried, ends):
    tokens, width = resid.shape
    pieces, depth, block_cols = own.shape[1:]
    each = others[0].shape[0]
    steps = each * len(others)
    length = key.shape[0]
    rows = tokens * block_cols // HEAD_SIZE

    def whole(*shape):
        return pl.BlockSpec(shape, lambda i: (0,) * len(shape))

    shard = (1, pieces, depth, block_cols)
    in_specs = [
        pl.BlockSpec(memory_space=pltpu.SMEM),
        whole(tokens, width),
        pl.BlockSpec(shard, lambda i: (first + i, 0, 0, 0)),
        pl.BlockSpec((tokens, block_cols), lambda i: (0, first + i)),
        pl.BlockSpec((rows, length), lambda i: (first + i, 0)),
        whole(length, HEAD_SIZE),
        whole(HEAD_SIZE, length),
    ]
    in_specs += [whole(HEAD_SIZE, length)] * len(carried)
    for j in range(len(others)):
        in_specs.append(
            pl.BlockSpec(shard, lambda i, j=j: (jnp.clip(i - j * each, 0, each - 1), 0, 0, 0))
        )
    sums = jax.ShapeDtypeStruct((HEAD_SIZE, length), F32)
    out_specs = [pl.BlockSpec((tokens, block_cols), lambda i: (0, i))]
    out_shape = [jax.ShapeDtypeStruct((tokens, steps * block_cols), BF16)]
    scratch = [pltpu.VMEM((tokens, block_cols), F32)]
    if ends:
        out_specs += [whole(length, 2 * HEAD_SIZE)]
        out_shape += [jax.ShapeDtypeStruct((length, 2 * HEAD_SIZE), BF16)]
        scratch = [pltpu.VMEM((HEAD_SIZE, length), F32)] * 2 + scratch
    else:
        out_specs += [whole(HEAD_SIZE, length)] * 2
        out_shape += [sums, sums]
    return pl.pallas_call(
        functools.partial(attention_kernel, not carried, ends),
        grid=(steps,),
        in_specs=in_specs,
        out_specs=out_specs,
        scratch_shapes=scratch,
        out_shape=out_shape,
        compiler_params=pltpu.CompilerParams(vmem_limit_bytes=VMEM_BYTES),
        cost_estimate=pl.CostEstimate(
            flops=2 * steps * rows * (5 * length * HEAD_SIZE + width * HEAD_SIZE),
            bytes_accessed=steps * (2 * width * block_cols + 2 * rows * length),
            transcendentals=0,
        ),
        name="attention_back",
    )(core, resid, own, queries, probs, key, value_t, *carried, *others)


def swapped(block, axis):
    return lax.ppermute(block, axis, [(0, 1), (1, 0)])


def exchanged(block, axis, mask):
    return lax.ppermute(block, axis, [(i, i ^ mask) for i in range(lax.axis_size(axis))])


def in_order(own, other, place):
    return jnp.where(
        place == 0,
        jnp.concatenate([own, other], axis=0),
        jnp.concatenate([other, own], axis=0),
    )


def to_chips(chunks):
    sent = chunks.reshape(EXPERTS, BATCH, -1)
    return lax.all_to_all(sent, CHIPS, split_axis=0, concat_axis=0, tiled=True).reshape(
        chunks.shape
    )


def body(
    hidden_in,
    out_grad,
    queries,
    keys,
    values,
    out_proj,
    expert_ids,
    gate_probs,
    w_gate,
    w_up,
    w_down,
):
    tokens, width = hidden_in.shape[1:]
    zlo = lax.axis_index("zlo")
    y_at = lax.axis_index("y")
    y_count = lax.axis_size("y")
    core = lax.axis_index("core").astype(jnp.int32).reshape(1)
    own = (w_gate, w_up, w_down)
    other = tuple(swapped(w, "core") for w in own)

    ids = expert_ids[0].T

    kv = jnp.concatenate([keys[0], values[0]], axis=1)
    kv = in_order(kv, exchanged(kv, "y", 1), y_at & 1)
    ids, kv = lax.optimization_barrier((ids, kv))
    far_kv = exchanged(kv, "y", 2)

    chunks = pick(ids, hidden_in[0], out_grad[0])
    chunks, far_kv = lax.optimization_barrier((chunks, far_kv))
    came = to_chips(chunks)

    kv = in_order(kv, far_kv, y_at >> 1).reshape(-1, 2, GROUPS, HEAD_SIZE)
    own_kv = lax.dynamic_index_in_dim(kv, zlo, 2, keepdims=False)
    near_kv = lax.dynamic_index_in_dim(kv, 1 - zlo, 2, keepdims=False)
    group_width = width // GROUPS
    own_query = lax.dynamic_slice_in_dim(queries[0], zlo * group_width, group_width, 1)
    near_query = lax.dynamic_slice_in_dim(queries[0], (1 - zlo) * group_width, group_width, 1)
    crossing = swapped(
        jnp.concatenate([near_query, near_kv.reshape(-1, group_width)], axis=0), "zlo"
    )
    came, crossing = lax.optimization_barrier((came, crossing))
    near_query = crossing[:tokens]
    near_kv = crossing[tokens:].reshape(own_kv.shape)
    all_kv = in_order(own_kv, near_kv, zlo).reshape(-1, 2, HEAD_SIZE)
    key, value = all_kv[:, 0], all_kv[:, 1]
    key_t, value_t = key.T, value.T
    block_heads = out_proj.shape[0] // HEAD_SIZE
    own_row = ((zlo * y_count + y_at) * tokens).astype(jnp.int32).reshape(1)
    near_row = (((1 - zlo) * y_count + y_at) * tokens).astype(jnp.int32).reshape(1)
    back = expert_back(came, own, other)

    own_query, near_query, _ = lax.optimization_barrier((own_query, near_query, back))
    own_probs = softmax_probs(own_row, own_query, key_t, block_heads)
    near_probs = softmax_probs(near_row, near_query, key_t, block_heads)

    proj_own = lax.all_gather(turned(out_proj), PLANE, axis=0, tiled=False)
    proj_own = proj_own.reshape(y_count, -1, *proj_own.shape[1:])
    proj_own, own_probs, near_probs = lax.optimization_barrier((proj_own, own_probs, near_probs))
    halves = y_count // 2
    proj_other = [swapped(proj_own[i : i + 1], "core") for i in range(y_count)]
    result = to_chips(back)
    resid = mix(ids, gate_probs[0].T, out_grad[0], result)
    near_resid = swapped(resid, "zlo")

    dquery, *sums = attention_back(
        core, resid, proj_own, proj_other, own_query, own_probs, key, value_t, 0, (), False
    )
    near = (near_query, near_probs, key, value_t)
    near_first, *sums = attention_back(
        core, near_resid, proj_own, proj_other[:halves], *near, 0, sums, False
    )
    near_second, dkv = attention_back(
        core, near_resid, proj_own, proj_other[halves:], *near, halves, sums, True
    )
    far_first = swapped(near_first, "zlo")
    dkv, far_first = lax.optimization_barrier((dkv, far_first))
    far_dquery = jnp.concatenate([far_first, swapped(near_second, "zlo")], axis=1)
    dquery = jnp.where(
        zlo == 0,
        jnp.concatenate([dquery, far_dquery], axis=1),
        jnp.concatenate([far_dquery, dquery], axis=1),
    )
    sent = lax.all_to_all(
        dkv.reshape(-1, tokens, 2 * HEAD_SIZE), SEQ, split_axis=0, concat_axis=0, tiled=True
    )
    sent = sent.reshape(GROUPS, y_count, tokens, 2 * HEAD_SIZE)
    sums = jnp.sum(sent.astype(F32), axis=1).astype(BF16)
    dkey = jnp.concatenate([sums[g, :, :HEAD_SIZE] for g in range(GROUPS)], axis=1)
    dvalue = jnp.concatenate([sums[g, :, HEAD_SIZE:] for g in range(GROUPS)], axis=1)
    return resid[None], dquery[None], dkey[None], dvalue[None]


def solution(mesh):
    fine = Mesh(mesh.devices.reshape(2, 4, 2, 4, 2), ("zlo", "y", "zhi", "x", "core"))
    dp = ("zhi", "x", "core")
    token_spec = P(dp, SEQ, None)
    weight_spec = P((*SEQ, *dp), None, None)
    return jax.shard_map(
        body,
        mesh=fine,
        in_specs=(token_spec,) * 5
        + (P(SEQ, dp), token_spec, token_spec, weight_spec, weight_spec, weight_spec),
        out_specs=(token_spec,) * 4,
        check_vma=False,
    )
```

```python
import functools

import jax
import jax.numpy as jnp
import numpy as np
from jax import lax
from jax.experimental import pallas as pl
from jax.experimental.pallas import tpu as pltpu
from jax.sharding import Mesh
from jax.sharding import PartitionSpec as P

HEAD_SIZE = 128
GROUPS = 2
CAPACITY = 5
EXPERTS = 64
SLOTS = EXPERTS * CAPACITY
SEQ = ("zlo", "y")
CHIPS = ("zlo", "y", "zhi", "x")
PLANE = ("y", "zhi", "x")
BLOCK = 512
PIECES = 8
BATCH = PIECES * CAPACITY
HIDDEN_TILE = 256
VMEM_BYTES = 60 * 1024 * 1024
NT = (((1,), (1,)), ((), ()))
TN = (((0,), (0,)), ((), ()))
F32 = jnp.float32
BF16 = jnp.bfloat16


def chunk_order():
    count = PIECES * BATCH
    row = lax.broadcasted_iota(jnp.int32, (count, 1), 0)
    chip = (row * 1639) >> 16
    rest = row - chip * BATCH
    piece = (rest * 205) >> 10
    moved = piece * BATCH + chip * CAPACITY + rest - piece * CAPACITY
    return jnp.where(
        lax.broadcasted_iota(jnp.int32, (count, count), 1) == moved, 1.0, 0.0
    ).astype(BF16)


def reordered(order, rows):
    return jnp.dot(order, rows, preferred_element_type=F32)


def slot_rows(ids):
    tokens = ids.shape[1]
    expert = lax.broadcasted_iota(jnp.int32, (EXPERTS, tokens), 0)
    chosen = [ids[k : k + 1] for k in range(ids.shape[0])]
    hots = [jnp.where(expert == e, 1.0, 0.0) for e in chosen]
    before = jnp.where(
        lax.broadcasted_iota(jnp.int32, (tokens, tokens), 0)
        < lax.broadcasted_iota(jnp.int32, (tokens, tokens), 1),
        1.0,
        0.0,
    ).astype(BF16)
    earlier = jnp.dot(sum(hots).astype(BF16), before, preferred_element_type=F32)
    return [
        e * CAPACITY + jnp.sum(earlier * hot, axis=0, keepdims=True).astype(jnp.int32)
        for e, hot in zip(chosen, hots)
    ]


def pick_kernel(ids, hidden, grads, out, rows, row_grads, chunks, sems):
    slot = lax.broadcasted_iota(jnp.int32, (SLOTS, ids.shape[1]), 0)
    picking = sum(jnp.where(slot == row, 1.0, 0.0) for row in slot_rows(ids)).astype(BF16)
    for piece in range(PIECES):
        at = slice(piece * BLOCK, (piece + 1) * BLOCK)
        rows[:, at] = jnp.dot(picking, hidden[:, at], preferred_element_type=F32)
        row_grads[:, at] = jnp.dot(picking, grads[:, at], preferred_element_type=F32)
    order = chunk_order()
    leaving = []
    for g in range(SLOTS // BATCH):
        slots = slice(g * BATCH, (g + 1) * BATCH)
        at = slice(g * PIECES * BATCH, (g + 1) * PIECES * BATCH)
        for side, source in enumerate((rows, row_grads)):
            pieces = [source[slots, p * BLOCK : (p + 1) * BLOCK] for p in range(PIECES)]
            sent = reordered(order, jnp.concatenate(pieces, axis=0).astype(BF16))
            chunks[at, side * BLOCK : (side + 1) * BLOCK] = sent.astype(BF16)
        copy = pltpu.make_async_copy(chunks.at[at], out.at[at], sems.at[g])
        copy.start()
        leaving.append(copy)
    for copy in leaving:
        copy.wait()


def pick(ids, hidden, grads):
    width = hidden.shape[1]
    held = pl.BlockSpec(memory_space=pltpu.VMEM)
    return pl.pallas_call(
        pick_kernel,
        in_specs=[held] * 3,
        out_specs=pl.BlockSpec(memory_space=pl.ANY),
        out_shape=jax.ShapeDtypeStruct((EXPERTS * BATCH, 2 * BLOCK), BF16),
        scratch_shapes=[pltpu.VMEM((SLOTS, width), F32)] * 2
        + [
            pltpu.VMEM((EXPERTS * BATCH, 2 * BLOCK), BF16),
            pltpu.SemaphoreType.DMA((SLOTS // BATCH,)),
        ],
        compiler_params=pltpu.CompilerParams(vmem_limit_bytes=VMEM_BYTES),
        cost_estimate=pl.CostEstimate(
            flops=8 * SLOTS * SLOTS * width, bytes_accessed=8 * SLOTS * width, transcendentals=0
        ),
        name="pick",
    )(ids, hidden, grads)


def mixing_kernel(ids, probs, out):
    slot = lax.broadcasted_iota(jnp.int32, (SLOTS, ids.shape[1]), 0)
    mixing = sum(
        jnp.where(slot == row, probs[k : k + 1], 0.0) for k, row in enumerate(slot_rows(ids))
    )
    mixing = jnp.transpose(mixing)
    mixing_high = mixing.astype(BF16)
    out[0] = mixing_high
    out[1] = (mixing - mixing_high.astype(F32)).astype(BF16)


def mixing_parts(ids, probs):
    held = pl.BlockSpec(memory_space=pltpu.VMEM)
    return pl.pallas_call(
        mixing_kernel,
        in_specs=[held] * 2,
        out_specs=held,
        out_shape=jax.ShapeDtypeStruct((2, ids.shape[1], SLOTS), BF16),
        compiler_params=pltpu.CompilerParams(vmem_limit_bytes=VMEM_BYTES),
        name="mixing_parts",
    )(ids, probs)


def mix_kernel(mixing, grads, sent, out, came, rows, sems):
    size = PIECES * BATCH
    arrivals = []
    for g in range(SLOTS // BATCH):
        at = slice(g * size, (g + 1) * size)
        copy = pltpu.make_async_copy(sent.at[at], came.at[at], sems.at[g])
        copy.start()
        arrivals.append(copy)
    order = chunk_order()
    for g in range(SLOTS // BATCH):
        arrivals[g].wait()
        batch = reordered(order, came[g * size : (g + 1) * size])
        for p in range(PIECES):
            rows[g * BATCH : (g + 1) * BATCH, p * BLOCK : (p + 1) * BLOCK] = batch[
                p * BATCH : (p + 1) * BATCH
            ]
    for p in range(PIECES):
        at = slice(p * BLOCK, (p + 1) * BLOCK)
        block = rows[:, at].astype(BF16)
        mixed = jnp.dot(mixing[0], block, preferred_element_type=F32)
        mixed += jnp.dot(mixing[1], block, preferred_element_type=F32)
        out[:, at] = (grads[:, at].astype(F32) + mixed).astype(BF16)


def mix(mixing, grads, sent):
    held = pl.BlockSpec(memory_space=pltpu.VMEM)
    return pl.pallas_call(
        mix_kernel,
        in_specs=[held] * 2 + [pl.BlockSpec(memory_space=pl.ANY)],
        out_specs=held,
        out_shape=jax.ShapeDtypeStruct(grads.shape, BF16),
        scratch_shapes=[
            pltpu.VMEM(sent.shape, BF16),
            pltpu.VMEM((SLOTS, grads.shape[1]), F32),
            pltpu.SemaphoreType.DMA((SLOTS // BATCH,)),
        ],
        compiler_params=pltpu.CompilerParams(vmem_limit_bytes=VMEM_BYTES // 2),
        name="mix",
    )(mixing, grads, sent)


def turn_kernel(block, out):
    out[...] = jnp.transpose(block[...])


def turned(block):
    held = pl.BlockSpec(memory_space=pltpu.VMEM)
    return pl.pallas_call(
        turn_kernel,
        in_specs=[held],
        out_specs=held,
        out_shape=jax.ShapeDtypeStruct(block.shape[::-1], block.dtype),
        compiler_params=pltpu.CompilerParams(vmem_limit_bytes=VMEM_BYTES),
        name="turned",
    )(block)


def expert_kernel(
    g0, u0, d0, g1, u1, d1, sent, out, came, rows, grads, gate, up, down, d_gate, d_up, sems, edge_sems
):
    arrival = pltpu.make_async_copy(sent, came, edge_sems.at[0])
    arrival.start()
    halves, width, half = gate.shape
    tile = 512
    loads = []
    for h, (g, u, d) in enumerate(((g0, u0, d0), (g1, u1, d1))):
        for at in range(0, half, HIDDEN_TILE):
            part = slice(at, at + HIDDEN_TILE)
            copies = [
                pltpu.make_async_copy(g.at[0, :, part], gate.at[h, :, part], sems.at[len(loads), 0]),
                pltpu.make_async_copy(u.at[0, :, part], up.at[h, :, part], sems.at[len(loads), 1]),
                pltpu.make_async_copy(d.at[0, part, :], down.at[h, part, :], sems.at[len(loads), 2]),
            ]
            loads.append((h, part, copies))

    def load(number):
        if number < len(loads):
            for copy in loads[number][2]:
                copy.start()

    load(0)
    size = PIECES * BATCH
    order = chunk_order()
    arrival.wait()
    load(1)
    for g in range(0, SLOTS // BATCH, 2):
        batches = [reordered(order, came[(g + i) * size : (g + i + 1) * size]) for i in range(2)]
        slots = slice(g * BATCH, (g + 2) * BATCH)
        for p in range(PIECES):
            pair = [batch[p * BATCH : (p + 1) * BATCH] for batch in batches]
            pair = jnp.concatenate(pair, axis=0).astype(BF16)
            rows[slots, p * BLOCK : (p + 1) * BLOCK] = pair[:, :BLOCK]
            grads[slots, p * BLOCK : (p + 1) * BLOCK] = pair[:, BLOCK:]
    for number, (h, part, copies) in enumerate(loads):
        load(number + 2)
        for copy in copies:
            copy.wait()
        pre_gate = jnp.dot(rows[...], gate[h, :, part], preferred_element_type=F32)
        pre_up = jnp.dot(rows[...], up[h, :, part], preferred_element_type=F32)
        upstream = lax.dot_general(grads[...], down[h, part, :], NT, preferred_element_type=F32)
        sig = jax.nn.sigmoid(pre_gate)
        d_gate[h, :, part] = (upstream * pre_up * sig * (1.0 + pre_gate * (1.0 - sig))).astype(BF16)
        d_up[h, :, part] = (upstream * pre_gate * sig).astype(BF16)

    @pl.loop(0, width // tile)
    def _(i):
        at = pl.ds(pl.multiple_of(i * tile, tile), tile)
        total = lax.dot_general(d_gate[0], gate[0, at, :], NT, preferred_element_type=F32)
        total += lax.dot_general(d_up[0], up[0, at, :], NT, preferred_element_type=F32)
        for h in range(1, halves):
            total += lax.dot_general(d_gate[h], gate[h, at, :], NT, preferred_element_type=F32)
            total += lax.dot_general(d_up[h], up[h, at, :], NT, preferred_element_type=F32)
        rows[:, at] = total.astype(BF16)

    leaving = []
    for g in range(0, SLOTS // BATCH, 2):
        slots = slice(g * BATCH, (g + 2) * BATCH)
        pieces = [rows[slots, p * BLOCK : (p + 1) * BLOCK].astype(F32) for p in range(PIECES)]
        for i in range(2):
            batch = [piece[i * BATCH : (i + 1) * BATCH] for piece in pieces]
            batch = jnp.concatenate(batch, axis=0).astype(BF16)
            at = slice((g + i) * size, (g + i + 1) * size)
            came[at, :BLOCK] = reordered(order, batch).astype(BF16)
            copy = pltpu.make_async_copy(came.at[at, :BLOCK], out.at[at], edge_sems.at[1 + g + i])
            copy.start()
            leaving.append(copy)
    for copy in leaving:
        copy.wait()


def expert_back(sent, own, other):
    width, half = own[0].shape[1:]
    far = pl.BlockSpec(memory_space=pl.ANY)
    return pl.pallas_call(
        expert_kernel,
        in_specs=[far] * 7,
        out_specs=far,
        out_shape=jax.ShapeDtypeStruct((EXPERTS * BATCH, BLOCK), BF16),
        scratch_shapes=[
            pltpu.VMEM(sent.shape, BF16),
            pltpu.VMEM((SLOTS, width), BF16),
            pltpu.VMEM((SLOTS, width), BF16),
            pltpu.VMEM((2, width, half), BF16),
            pltpu.VMEM((2, width, half), BF16),
            pltpu.VMEM((2, half, width), BF16),
            pltpu.VMEM((2, SLOTS, half), BF16),
            pltpu.VMEM((2, SLOTS, half), BF16),
            pltpu.SemaphoreType.DMA((2 * half // HIDDEN_TILE, 3)),
            pltpu.SemaphoreType.DMA((1 + SLOTS // BATCH,)),
        ],
        compiler_params=pltpu.CompilerParams(vmem_limit_bytes=VMEM_BYTES),
        cost_estimate=pl.CostEstimate(
            flops=20 * SLOTS * width * half, bytes_accessed=12 * width * half, transcendentals=0
        ),
        name="expert_back",
    )(*own, *other, sent)


def stack_heads(block):
    heads = block.shape[1] // HEAD_SIZE
    return jnp.concatenate(
        [block[:, h * HEAD_SIZE : (h + 1) * HEAD_SIZE] for h in range(heads)], axis=0
    )


def softmax_kernel(first_row, query, key, probs):
    scale = HEAD_SIZE ** (-0.5)
    tokens = query.shape[0]
    scores = jnp.dot(stack_heads(query[...]), key[...], preferred_element_type=F32) * scale
    row = lax.broadcasted_iota(jnp.int32, scores.shape, 0) % tokens + first_row[0]
    col = lax.broadcasted_iota(jnp.int32, scores.shape, 1)
    scores = jnp.where(col <= row, scores, -1e30)
    weights = jnp.exp(scores - jnp.max(scores, axis=1, keepdims=True))
    probs[...] = (weights / jnp.sum(weights, axis=1, keepdims=True)).astype(BF16)


def softmax_probs(first_row, queries, key, block_heads):
    tokens, width = queries.shape
    length = key.shape[1]
    rows = block_heads * tokens
    steps = width // (block_heads * HEAD_SIZE)
    return pl.pallas_call(
        softmax_kernel,
        grid=(steps,),
        in_specs=[
            pl.BlockSpec(memory_space=pltpu.SMEM),
            pl.BlockSpec((tokens, block_heads * HEAD_SIZE), lambda i: (0, i)),
            pl.BlockSpec((HEAD_SIZE, length), lambda i: (0, 0)),
        ],
        out_specs=pl.BlockSpec((rows, length), lambda i: (i, 0)),
        out_shape=jax.ShapeDtypeStruct((steps * rows, length), BF16),
        compiler_params=pltpu.CompilerParams(vmem_limit_bytes=VMEM_BYTES),
        cost_estimate=pl.CostEstimate(
            flops=20 * steps * rows * length * HEAD_SIZE,
            bytes_accessed=2 * steps * rows * length,
            transcendentals=steps * rows * length,
        ),
        name="softmax_probs",
    )(first_row, queries, key)


def attention_kernel(begins, ends, core, resid, own, query, probs, key, value_t, *refs):
    ctx, refs = refs[-1], refs[:-1]
    steps = pl.num_programs(0)
    if not begins:
        dkey_in, dvalue_in = refs[:2]
        refs = refs[2:]
    if ends:
        *others, dquery, dkv, dkey, dvalue = refs
    else:
        *others, dquery, dkey, dvalue = refs
    step = pl.program_id(0)
    scale = HEAD_SIZE ** (-0.5)
    tokens = query.shape[0]
    pieces, depth, block_cols = own.shape[1:]

    @pl.when(step == 0)
    def _():
        if begins:
            dkey[...] = jnp.zeros_like(dkey)
            dvalue[...] = jnp.zeros_like(dvalue)
        else:
            dkey[...] = dkey_in[...]
            dvalue[...] = dvalue_in[...]

    def project(side, shard):
        total = jnp.zeros((tokens, block_cols), F32)
        for piece in range(pieces):
            at = pl.ds(pl.multiple_of((2 * piece + side) * depth, depth), depth)
            total += jnp.dot(resid[:, at], shard[0, piece], preferred_element_type=F32)
        return total

    for j, other in enumerate(others):

        @pl.when(step * len(others) // steps == j)
        def _(other=other):
            ctx[...] = project(1 - core[0], other)

    ctx = stack_heads((ctx[...] + project(core[0], own)).astype(BF16))
    query_rows = stack_heads(query[...])
    low = probs[...]
    weights = low.astype(F32)
    dprobs = jnp.dot(ctx, value_t[...], preferred_element_type=F32)
    delta = jnp.sum(weights * dprobs, axis=1, keepdims=True)
    dscores = (weights * (dprobs - delta)).astype(BF16)
    dq = jnp.dot(dscores, key[...], preferred_element_type=F32) * scale
    for h in range(query.shape[1] // HEAD_SIZE):
        dquery[:, h * HEAD_SIZE : (h + 1) * HEAD_SIZE] = dq[h * tokens : (h + 1) * tokens].astype(
            BF16
        )
    dkey[...] += lax.dot_general(query_rows, dscores, TN, preferred_element_type=F32)
    dvalue[...] += lax.dot_general(ctx, low, TN, preferred_element_type=F32)

    if ends:

        @pl.when(step == steps - 1)
        def _():
            dkv[:, :HEAD_SIZE] = jnp.transpose(dkey[...] * scale).astype(BF16)
            dkv[:, HEAD_SIZE:] = jnp.transpose(dvalue[...]).astype(BF16)


def attention_back(core, resid, own, others, queries, probs, key, value_t, first, carried, ends):
    tokens, width = resid.shape
    pieces, depth, block_cols = own.shape[1:]
    each = others[0].shape[0]
    steps = each * len(others)
    length = key.shape[0]
    rows = tokens * block_cols // HEAD_SIZE

    def whole(*shape):
        return pl.BlockSpec(shape, lambda i: (0,) * len(shape))

    shard = (1, pieces, depth, block_cols)
    in_specs = [
        pl.BlockSpec(memory_space=pltpu.SMEM),
        whole(tokens, width),
        pl.BlockSpec(shard, lambda i: (first + i, 0, 0, 0)),
        pl.BlockSpec((tokens, block_cols), lambda i: (0, first + i)),
        pl.BlockSpec((rows, length), lambda i: (first + i, 0)),
        whole(length, HEAD_SIZE),
        whole(HEAD_SIZE, length),
    ]
    in_specs += [whole(HEAD_SIZE, length)] * len(carried)
    for j in range(len(others)):
        in_specs.append(
            pl.BlockSpec(shard, lambda i, j=j: (jnp.clip(i - j * each, 0, each - 1), 0, 0, 0))
        )
    sums = jax.ShapeDtypeStruct((HEAD_SIZE, length), F32)
    out_specs = [pl.BlockSpec((tokens, block_cols), lambda i: (0, i))]
    out_shape = [jax.ShapeDtypeStruct((tokens, steps * block_cols), BF16)]
    scratch = [pltpu.VMEM((tokens, block_cols), F32)]
    if ends:
        out_specs += [whole(length, 2 * HEAD_SIZE)]
        out_shape += [jax.ShapeDtypeStruct((length, 2 * HEAD_SIZE), BF16)]
        scratch = [pltpu.VMEM((HEAD_SIZE, length), F32)] * 2 + scratch
    else:
        out_specs += [whole(HEAD_SIZE, length)] * 2
        out_shape += [sums, sums]
    return pl.pallas_call(
        functools.partial(attention_kernel, not carried, ends),
        grid=(steps,),
        in_specs=in_specs,
        out_specs=out_specs,
        scratch_shapes=scratch,
        out_shape=out_shape,
        compiler_params=pltpu.CompilerParams(vmem_limit_bytes=VMEM_BYTES),
        cost_estimate=pl.CostEstimate(
            flops=2 * steps * rows * (5 * length * HEAD_SIZE + width * HEAD_SIZE),
            bytes_accessed=steps * (2 * width * block_cols + 2 * rows * length),
            transcendentals=0,
        ),
        name="attention_back",
    )(core, resid, own, queries, probs, key, value_t, *carried, *others)


def swapped(block, axis):
    return lax.ppermute(block, axis, [(0, 1), (1, 0)])


def exchanged(block, axis, mask):
    return lax.ppermute(block, axis, [(i, i ^ mask) for i in range(lax.axis_size(axis))])


def in_order(own, other, place):
    return jnp.where(
        place == 0,
        jnp.concatenate([own, other], axis=0),
        jnp.concatenate([other, own], axis=0),
    )


def to_chips(chunks):
    sent = chunks.reshape(EXPERTS, BATCH, -1)
    return lax.all_to_all(sent, CHIPS, split_axis=0, concat_axis=0, tiled=True).reshape(
        chunks.shape
    )


def body(
    hidden_in,
    out_grad,
    queries,
    keys,
    values,
    out_proj,
    expert_ids,
    gate_probs,
    w_gate,
    w_up,
    w_down,
):
    tokens, width = hidden_in.shape[1:]
    zlo = lax.axis_index("zlo")
    y_at = lax.axis_index("y")
    y_count = lax.axis_size("y")
    core = lax.axis_index("core").astype(jnp.int32).reshape(1)
    own = (w_gate, w_up, w_down)
    other = tuple(swapped(w, "core") for w in own)

    ids = expert_ids[0].T

    kv = jnp.concatenate([keys[0], values[0]], axis=1)
    far_kv = exchanged(kv, "y", 1)

    chunks = pick(ids, hidden_in[0], out_grad[0])
    chunks, far_kv = lax.optimization_barrier((chunks, far_kv))
    came = to_chips(chunks)

    kv = in_order(kv, far_kv, y_at & 1)
    far_kv = exchanged(kv, "y", 2)
    mixing = mixing_parts(ids, gate_probs[0].T)
    group_width = width // GROUPS
    own_query = lax.dynamic_slice_in_dim(queries[0], zlo * group_width, group_width, 1)
    near_query = swapped(
        lax.dynamic_slice_in_dim(queries[0], (1 - zlo) * group_width, group_width, 1), "zlo"
    )
    came, far_kv, mixing = lax.optimization_barrier((came, far_kv, mixing))
    kv = in_order(kv, far_kv, y_at >> 1).reshape(-1, 2, GROUPS, HEAD_SIZE)
    near_kv = swapped(lax.dynamic_index_in_dim(kv, 1 - zlo, 2, keepdims=False), "zlo")
    back = expert_back(came, own, other)
    near_kv, own_query, near_query, _ = lax.optimization_barrier(
        (near_kv, own_query, near_query, back)
    )
    own_kv = lax.dynamic_index_in_dim(kv, zlo, 2, keepdims=False)
    all_kv = in_order(own_kv, near_kv, zlo)
    key, value = all_kv[:, 0], all_kv[:, 1]
    key_t, value_t = key.T, value.T
    block_heads = out_proj.shape[0] // HEAD_SIZE
    own_row = ((zlo * y_count + y_at) * tokens).astype(jnp.int32).reshape(1)
    near_row = (((1 - zlo) * y_count + y_at) * tokens).astype(jnp.int32).reshape(1)
    own_probs = softmax_probs(own_row, own_query, key_t, block_heads)
    near_probs = softmax_probs(near_row, near_query, key_t, block_heads)

    proj_own = lax.all_gather(turned(out_proj), PLANE, axis=0, tiled=False)
    proj_own = proj_own.reshape(y_count, -1, *proj_own.shape[1:])
    proj_own, own_probs, near_probs = lax.optimization_barrier((proj_own, own_probs, near_probs))
    halves = y_count // 2
    proj_other = [swapped(proj_own[i : i + 1], "core") for i in range(y_count)]
    result = to_chips(back)
    resid = mix(mixing, out_grad[0], result)
    near_resid = swapped(resid, "zlo")

    dquery, *sums = attention_back(
        core, resid, proj_own, proj_other, own_query, own_probs, key, value_t, 0, (), False
    )
    near = (near_query, near_probs, key, value_t)
    near_first, *sums = attention_back(
        core, near_resid, proj_own, proj_other[:halves], *near, 0, sums, False
    )
    near_second, dkv = attention_back(
        core, near_resid, proj_own, proj_other[halves:], *near, halves, sums, True
    )
    far_first = swapped(near_first, "zlo")
    dkv, far_first = lax.optimization_barrier((dkv, far_first))
    far_dquery = jnp.concatenate([far_first, swapped(near_second, "zlo")], axis=1)
    dquery = jnp.where(
        zlo == 0,
        jnp.concatenate([dquery, far_dquery], axis=1),
        jnp.concatenate([far_dquery, dquery], axis=1),
    )
    sent = lax.all_to_all(
        dkv.reshape(-1, tokens, 2 * HEAD_SIZE), SEQ, split_axis=0, concat_axis=0, tiled=True
    )
    sent = sent.reshape(GROUPS, y_count, tokens, 2 * HEAD_SIZE)
    sums = jnp.sum(sent.astype(F32), axis=1).astype(BF16)
    dkey = jnp.concatenate([sums[g, :, :HEAD_SIZE] for g in range(GROUPS)], axis=1)
    dvalue = jnp.concatenate([sums[g, :, HEAD_SIZE:] for g in range(GROUPS)], axis=1)
    return resid[None], dquery[None], dkey[None], dvalue[None]


def solution(mesh):
    fine = Mesh(mesh.devices.reshape(2, 4, 2, 4, 2), ("zlo", "y", "zhi", "x", "core"))
    dp = ("zhi", "x", "core")
    token_spec = P(dp, SEQ, None)
    weight_spec = P((*SEQ, *dp), None, None)
    return jax.shard_map(
        body,
        mesh=fine,
        in_specs=(token_spec,) * 5
        + (P(SEQ, dp), token_spec, token_spec, weight_spec, weight_spec, weight_spec),
        out_specs=(token_spec,) * 4,
        check_vma=False,
    )
```

```python
import functools

import jax
import jax.numpy as jnp
import numpy as np
from jax import lax
from jax.experimental import pallas as pl
from jax.experimental.pallas import tpu as pltpu
from jax.sharding import Mesh
from jax.sharding import PartitionSpec as P

HEAD_SIZE = 128
GROUPS = 2
CAPACITY = 5
EXPERTS = 64
SLOTS = EXPERTS * CAPACITY
SEQ = ("zlo", "y")
CHIPS = ("zlo", "y", "zhi", "x")
PLANE = ("y", "x", "core")
BLOCK = 512
PIECES = 8
BATCH = PIECES * CAPACITY
HIDDEN_TILE = 256
VMEM_BYTES = 60 * 1024 * 1024
NT = (((1,), (1,)), ((), ()))
TN = (((0,), (0,)), ((), ()))
F32 = jnp.float32
BF16 = jnp.bfloat16


def chunk_order():
    count = PIECES * BATCH
    row = lax.broadcasted_iota(jnp.int32, (count, 1), 0)
    chip = (row * 1639) >> 16
    rest = row - chip * BATCH
    piece = (rest * 205) >> 10
    moved = piece * BATCH + chip * CAPACITY + rest - piece * CAPACITY
    return jnp.where(
        lax.broadcasted_iota(jnp.int32, (count, count), 1) == moved, 1.0, 0.0
    ).astype(BF16)


def reordered(order, rows):
    return jnp.dot(order, rows, preferred_element_type=F32)


def slot_rows(ids):
    tokens = ids.shape[1]
    expert = lax.broadcasted_iota(jnp.int32, (EXPERTS, tokens), 0)
    chosen = [ids[k : k + 1] for k in range(ids.shape[0])]
    hots = [jnp.where(expert == e, 1.0, 0.0) for e in chosen]
    before = jnp.where(
        lax.broadcasted_iota(jnp.int32, (tokens, tokens), 0)
        < lax.broadcasted_iota(jnp.int32, (tokens, tokens), 1),
        1.0,
        0.0,
    ).astype(BF16)
    earlier = jnp.dot(sum(hots).astype(BF16), before, preferred_element_type=F32)
    return [
        e * CAPACITY + jnp.sum(earlier * hot, axis=0, keepdims=True).astype(jnp.int32)
        for e, hot in zip(chosen, hots)
    ]


def pick_kernel(ids, hidden, grads, out, rows, row_grads, chunks, sems):
    slot = lax.broadcasted_iota(jnp.int32, (SLOTS, ids.shape[1]), 0)
    picking = sum(jnp.where(slot == row, 1.0, 0.0) for row in slot_rows(ids)).astype(BF16)
    for piece in range(PIECES):
        at = slice(piece * BLOCK, (piece + 1) * BLOCK)
        rows[:, at] = jnp.dot(picking, hidden[:, at], preferred_element_type=F32)
        row_grads[:, at] = jnp.dot(picking, grads[:, at], preferred_element_type=F32)
    order = chunk_order()
    leaving = []
    for g in range(SLOTS // BATCH):
        slots = slice(g * BATCH, (g + 1) * BATCH)
        at = slice(g * PIECES * BATCH, (g + 1) * PIECES * BATCH)
        for side, source in enumerate((rows, row_grads)):
            pieces = [source[slots, p * BLOCK : (p + 1) * BLOCK] for p in range(PIECES)]
            sent = reordered(order, jnp.concatenate(pieces, axis=0).astype(BF16))
            chunks[at, side * BLOCK : (side + 1) * BLOCK] = sent.astype(BF16)
        copy = pltpu.make_async_copy(chunks.at[at], out.at[at], sems.at[g])
        copy.start()
        leaving.append(copy)
    for copy in leaving:
        copy.wait()


def pick(ids, hidden, grads):
    width = hidden.shape[1]
    held = pl.BlockSpec(memory_space=pltpu.VMEM)
    return pl.pallas_call(
        pick_kernel,
        in_specs=[held] * 3,
        out_specs=pl.BlockSpec(memory_space=pl.ANY),
        out_shape=jax.ShapeDtypeStruct((EXPERTS * BATCH, 2 * BLOCK), BF16),
        scratch_shapes=[pltpu.VMEM((SLOTS, width), F32)] * 2
        + [
            pltpu.VMEM((EXPERTS * BATCH, 2 * BLOCK), BF16),
            pltpu.SemaphoreType.DMA((SLOTS // BATCH,)),
        ],
        compiler_params=pltpu.CompilerParams(vmem_limit_bytes=VMEM_BYTES),
        cost_estimate=pl.CostEstimate(
            flops=8 * SLOTS * SLOTS * width, bytes_accessed=8 * SLOTS * width, transcendentals=0
        ),
        name="pick",
    )(ids, hidden, grads)


def mixing_kernel(ids, probs, out):
    slot = lax.broadcasted_iota(jnp.int32, (SLOTS, ids.shape[1]), 0)
    mixing = sum(
        jnp.where(slot == row, probs[k : k + 1], 0.0) for k, row in enumerate(slot_rows(ids))
    )
    mixing = jnp.transpose(mixing)
    mixing_high = mixing.astype(BF16)
    out[0] = mixing_high
    out[1] = (mixing - mixing_high.astype(F32)).astype(BF16)


def mixing_parts(ids, probs):
    held = pl.BlockSpec(memory_space=pltpu.VMEM)
    return pl.pallas_call(
        mixing_kernel,
        in_specs=[held] * 2,
        out_specs=held,
        out_shape=jax.ShapeDtypeStruct((2, ids.shape[1], SLOTS), BF16),
        compiler_params=pltpu.CompilerParams(vmem_limit_bytes=VMEM_BYTES),
        name="mixing_parts",
    )(ids, probs)


def mix_kernel(mixing, grads, sent, out, came, rows, sems):
    size = PIECES * BATCH
    arrivals = []
    for g in range(SLOTS // BATCH):
        at = slice(g * size, (g + 1) * size)
        copy = pltpu.make_async_copy(sent.at[at], came.at[at], sems.at[g])
        copy.start()
        arrivals.append(copy)
    order = chunk_order()
    for g in range(SLOTS // BATCH):
        arrivals[g].wait()
        batch = reordered(order, came[g * size : (g + 1) * size])
        for p in range(PIECES):
            rows[g * BATCH : (g + 1) * BATCH, p * BLOCK : (p + 1) * BLOCK] = batch[
                p * BATCH : (p + 1) * BATCH
            ]
    for p in range(PIECES):
        at = slice(p * BLOCK, (p + 1) * BLOCK)
        block = rows[:, at].astype(BF16)
        mixed = jnp.dot(mixing[0], block, preferred_element_type=F32)
        mixed += jnp.dot(mixing[1], block, preferred_element_type=F32)
        out[:, at] = (grads[:, at].astype(F32) + mixed).astype(BF16)


def mix(mixing, grads, sent):
    held = pl.BlockSpec(memory_space=pltpu.VMEM)
    return pl.pallas_call(
        mix_kernel,
        in_specs=[held] * 2 + [pl.BlockSpec(memory_space=pl.ANY)],
        out_specs=held,
        out_shape=jax.ShapeDtypeStruct(grads.shape, BF16),
        scratch_shapes=[
            pltpu.VMEM(sent.shape, BF16),
            pltpu.VMEM((SLOTS, grads.shape[1]), F32),
            pltpu.SemaphoreType.DMA((SLOTS // BATCH,)),
        ],
        compiler_params=pltpu.CompilerParams(vmem_limit_bytes=VMEM_BYTES // 2),
        name="mix",
    )(mixing, grads, sent)


def turn_kernel(block, out):
    out[...] = jnp.transpose(block[...])


def turned(block):
    held = pl.BlockSpec(memory_space=pltpu.VMEM)
    return pl.pallas_call(
        turn_kernel,
        in_specs=[held],
        out_specs=held,
        out_shape=jax.ShapeDtypeStruct(block.shape[::-1], block.dtype),
        compiler_params=pltpu.CompilerParams(vmem_limit_bytes=VMEM_BYTES),
        name="turned",
    )(block)


def expert_kernel(
    g0, u0, d0, g1, u1, d1, sent, out, came, rows, grads, gate, up, down, d_gate, d_up, sems, edge_sems
):
    arrival = pltpu.make_async_copy(sent, came, edge_sems.at[0])
    arrival.start()
    halves, width, half = gate.shape
    tile = 512
    loads = []
    for h, (g, u, d) in enumerate(((g0, u0, d0), (g1, u1, d1))):
        for at in range(0, half, HIDDEN_TILE):
            part = slice(at, at + HIDDEN_TILE)
            copies = [
                pltpu.make_async_copy(g.at[0, :, part], gate.at[h, :, part], sems.at[len(loads), 0]),
                pltpu.make_async_copy(u.at[0, :, part], up.at[h, :, part], sems.at[len(loads), 1]),
                pltpu.make_async_copy(d.at[0, part, :], down.at[h, part, :], sems.at[len(loads), 2]),
            ]
            loads.append((h, part, copies))

    def load(number):
        if number < len(loads):
            for copy in loads[number][2]:
                copy.start()

    load(0)
    size = PIECES * BATCH
    order = chunk_order()
    arrival.wait()
    load(1)
    for g in range(0, SLOTS // BATCH, 2):
        batches = [reordered(order, came[(g + i) * size : (g + i + 1) * size]) for i in range(2)]
        slots = slice(g * BATCH, (g + 2) * BATCH)
        for p in range(PIECES):
            pair = [batch[p * BATCH : (p + 1) * BATCH] for batch in batches]
            pair = jnp.concatenate(pair, axis=0).astype(BF16)
            rows[slots, p * BLOCK : (p + 1) * BLOCK] = pair[:, :BLOCK]
            grads[slots, p * BLOCK : (p + 1) * BLOCK] = pair[:, BLOCK:]
    for number, (h, part, copies) in enumerate(loads):
        load(number + 2)
        for copy in copies:
            copy.wait()
        pre_gate = jnp.dot(rows[...], gate[h, :, part], preferred_element_type=F32)
        pre_up = jnp.dot(rows[...], up[h, :, part], preferred_element_type=F32)
        upstream = lax.dot_general(grads[...], down[h, part, :], NT, preferred_element_type=F32)
        sig = jax.nn.sigmoid(pre_gate)
        d_gate[h, :, part] = (upstream * pre_up * sig * (1.0 + pre_gate * (1.0 - sig))).astype(BF16)
        d_up[h, :, part] = (upstream * pre_gate * sig).astype(BF16)

    @pl.loop(0, width // tile)
    def _(i):
        at = pl.ds(pl.multiple_of(i * tile, tile), tile)
        total = lax.dot_general(d_gate[0], gate[0, at, :], NT, preferred_element_type=F32)
        total += lax.dot_general(d_up[0], up[0, at, :], NT, preferred_element_type=F32)
        for h in range(1, halves):
            total += lax.dot_general(d_gate[h], gate[h, at, :], NT, preferred_element_type=F32)
            total += lax.dot_general(d_up[h], up[h, at, :], NT, preferred_element_type=F32)
        rows[:, at] = total.astype(BF16)

    leaving = []
    for g in range(0, SLOTS // BATCH, 2):
        slots = slice(g * BATCH, (g + 2) * BATCH)
        pieces = [rows[slots, p * BLOCK : (p + 1) * BLOCK].astype(F32) for p in range(PIECES)]
        for i in range(2):
            batch = [piece[i * BATCH : (i + 1) * BATCH] for piece in pieces]
            batch = jnp.concatenate(batch, axis=0).astype(BF16)
            at = slice((g + i) * size, (g + i + 1) * size)
            came[at, :BLOCK] = reordered(order, batch).astype(BF16)
            copy = pltpu.make_async_copy(came.at[at, :BLOCK], out.at[at], edge_sems.at[1 + g + i])
            copy.start()
            leaving.append(copy)
    for copy in leaving:
        copy.wait()


def expert_back(sent, own, other):
    width, half = own[0].shape[1:]
    far = pl.BlockSpec(memory_space=pl.ANY)
    return pl.pallas_call(
        expert_kernel,
        in_specs=[far] * 7,
        out_specs=far,
        out_shape=jax.ShapeDtypeStruct((EXPERTS * BATCH, BLOCK), BF16),
        scratch_shapes=[
            pltpu.VMEM(sent.shape, BF16),
            pltpu.VMEM((SLOTS, width), BF16),
            pltpu.VMEM((SLOTS, width), BF16),
            pltpu.VMEM((2, width, half), BF16),
            pltpu.VMEM((2, width, half), BF16),
            pltpu.VMEM((2, half, width), BF16),
            pltpu.VMEM((2, SLOTS, half), BF16),
            pltpu.VMEM((2, SLOTS, half), BF16),
            pltpu.SemaphoreType.DMA((2 * half // HIDDEN_TILE, 3)),
            pltpu.SemaphoreType.DMA((1 + SLOTS // BATCH,)),
        ],
        compiler_params=pltpu.CompilerParams(vmem_limit_bytes=VMEM_BYTES),
        cost_estimate=pl.CostEstimate(
            flops=20 * SLOTS * width * half, bytes_accessed=12 * width * half, transcendentals=0
        ),
        name="expert_back",
    )(*own, *other, sent)


def stack_heads(block):
    heads = block.shape[1] // HEAD_SIZE
    return jnp.concatenate(
        [block[:, h * HEAD_SIZE : (h + 1) * HEAD_SIZE] for h in range(heads)], axis=0
    )


def softmax_kernel(first_row, query, key, probs):
    scale = HEAD_SIZE ** (-0.5)
    tokens = query.shape[0]
    scores = jnp.dot(stack_heads(query[...]), key[...], preferred_element_type=F32) * scale
    row = lax.broadcasted_iota(jnp.int32, scores.shape, 0) % tokens + first_row[0]
    col = lax.broadcasted_iota(jnp.int32, scores.shape, 1)
    scores = jnp.where(col <= row, scores, -1e30)
    weights = jnp.exp(scores - jnp.max(scores, axis=1, keepdims=True))
    probs[...] = (weights / jnp.sum(weights, axis=1, keepdims=True)).astype(BF16)


def softmax_probs(first_row, queries, key, block_heads):
    tokens, width = queries.shape
    length = key.shape[1]
    rows = block_heads * tokens
    steps = width // (block_heads * HEAD_SIZE)
    return pl.pallas_call(
        softmax_kernel,
        grid=(steps,),
        in_specs=[
            pl.BlockSpec(memory_space=pltpu.SMEM),
            pl.BlockSpec((tokens, block_heads * HEAD_SIZE), lambda i: (0, i)),
            pl.BlockSpec((HEAD_SIZE, length), lambda i: (0, 0)),
        ],
        out_specs=pl.BlockSpec((rows, length), lambda i: (i, 0)),
        out_shape=jax.ShapeDtypeStruct((steps * rows, length), BF16),
        compiler_params=pltpu.CompilerParams(vmem_limit_bytes=VMEM_BYTES),
        cost_estimate=pl.CostEstimate(
            flops=20 * steps * rows * length * HEAD_SIZE,
            bytes_accessed=2 * steps * rows * length,
            transcendentals=steps * rows * length,
        ),
        name="softmax_probs",
    )(first_row, queries, key)


def attention_kernel(begins, ends, resid, proj, query, probs, key, value_t, *refs):
    steps = pl.num_programs(0)
    if not begins:
        dkey_in, dvalue_in = refs[:2]
        refs = refs[2:]
    if ends:
        dquery, dkv, dkey, dvalue = refs
    else:
        dquery, dkey, dvalue = refs
    step = pl.program_id(0)
    scale = HEAD_SIZE ** (-0.5)
    tokens = query.shape[0]
    x_count, core_count, zhi_count, depth, block_cols = proj.shape[1:]

    @pl.when(step == 0)
    def _():
        if begins:
            dkey[...] = jnp.zeros_like(dkey)
            dvalue[...] = jnp.zeros_like(dvalue)
        else:
            dkey[...] = dkey_in[...]
            dvalue[...] = dvalue_in[...]

    ctx = jnp.zeros((tokens, block_cols), F32)
    for x in range(x_count):
        for core in range(core_count):
            for zhi in range(zhi_count):
                at = ((zhi * x_count + x) * core_count + core) * depth
                ctx += jnp.dot(
                    resid[:, at : at + depth], proj[0, x, core, zhi], preferred_element_type=F32
                )
    ctx = stack_heads(ctx.astype(BF16))
    query_rows = stack_heads(query[...])
    low = probs[...]
    weights = low.astype(F32)
    dprobs = jnp.dot(ctx, value_t[...], preferred_element_type=F32)
    delta = jnp.sum(weights * dprobs, axis=1, keepdims=True)
    dscores = (weights * (dprobs - delta)).astype(BF16)
    dq = jnp.dot(dscores, key[...], preferred_element_type=F32) * scale
    for h in range(query.shape[1] // HEAD_SIZE):
        dquery[:, h * HEAD_SIZE : (h + 1) * HEAD_SIZE] = dq[h * tokens : (h + 1) * tokens].astype(
            BF16
        )
    dkey[...] += lax.dot_general(query_rows, dscores, TN, preferred_element_type=F32)
    dvalue[...] += lax.dot_general(ctx, low, TN, preferred_element_type=F32)

    if ends:

        @pl.when(step == steps - 1)
        def _():
            dkv[:, :HEAD_SIZE] = jnp.transpose(dkey[...] * scale).astype(BF16)
            dkv[:, HEAD_SIZE:] = jnp.transpose(dvalue[...]).astype(BF16)


def attention_back(resid, proj, queries, probs, key, value_t, first, steps, carried, ends):
    tokens, width = resid.shape
    block_cols = proj.shape[-1]
    length = key.shape[0]
    rows = tokens * block_cols // HEAD_SIZE

    def whole(*shape):
        return pl.BlockSpec(shape, lambda i: (0,) * len(shape))

    in_specs = [
        whole(tokens, width),
        pl.BlockSpec((1, *proj.shape[1:]), lambda i: (first + i, 0, 0, 0, 0, 0)),
        pl.BlockSpec((tokens, block_cols), lambda i: (0, first + i)),
        pl.BlockSpec((rows, length), lambda i: (first + i, 0)),
        whole(length, HEAD_SIZE),
        whole(HEAD_SIZE, length),
    ]
    in_specs += [whole(HEAD_SIZE, length)] * len(carried)
    sums = jax.ShapeDtypeStruct((HEAD_SIZE, length), F32)
    out_specs = [pl.BlockSpec((tokens, block_cols), lambda i: (0, i))]
    out_shape = [jax.ShapeDtypeStruct((tokens, steps * block_cols), BF16)]
    scratch = []
    if ends:
        out_specs += [whole(length, 2 * HEAD_SIZE)]
        out_shape += [jax.ShapeDtypeStruct((length, 2 * HEAD_SIZE), BF16)]
        scratch = [pltpu.VMEM((HEAD_SIZE, length), F32)] * 2
    else:
        out_specs += [whole(HEAD_SIZE, length)] * 2
        out_shape += [sums, sums]
    return pl.pallas_call(
        functools.partial(attention_kernel, not carried, ends),
        grid=(steps,),
        in_specs=in_specs,
        out_specs=out_specs,
        scratch_shapes=scratch,
        out_shape=out_shape,
        compiler_params=pltpu.CompilerParams(vmem_limit_bytes=VMEM_BYTES),
        cost_estimate=pl.CostEstimate(
            flops=2 * steps * rows * (5 * length * HEAD_SIZE + width * HEAD_SIZE),
            bytes_accessed=steps * (2 * width * block_cols + 2 * rows * length),
            transcendentals=0,
        ),
        name="attention_back",
    )(resid, proj, queries, probs, key, value_t, *carried)


def swapped(block, axis):
    return lax.ppermute(block, axis, [(0, 1), (1, 0)])


def exchanged(block, axis, mask):
    return lax.ppermute(block, axis, [(i, i ^ mask) for i in range(lax.axis_size(axis))])


def in_order(own, other, place):
    return jnp.where(
        place == 0,
        jnp.concatenate([own, other], axis=0),
        jnp.concatenate([other, own], axis=0),
    )


def to_chips(chunks):
    sent = chunks.reshape(EXPERTS, BATCH, -1)
    return lax.all_to_all(sent, CHIPS, split_axis=0, concat_axis=0, tiled=True).reshape(
        chunks.shape
    )


def body(
    hidden_in,
    out_grad,
    queries,
    keys,
    values,
    out_proj,
    expert_ids,
    gate_probs,
    w_gate,
    w_up,
    w_down,
):
    tokens, width = hidden_in.shape[1:]
    zlo = lax.axis_index("zlo")
    y_at = lax.axis_index("y")
    y_count = lax.axis_size("y")
    zhi_at = lax.axis_index("zhi")
    own = (w_gate, w_up, w_down)
    other = tuple(swapped(w, "core") for w in own)

    ids = expert_ids[0].T

    proj = turned(out_proj)
    far_proj = exchanged(proj, "zhi", 1)

    kv = jnp.concatenate([keys[0], values[0]], axis=1)
    far_kv = exchanged(kv, "y", 1)

    chunks = pick(ids, hidden_in[0], out_grad[0])
    chunks, far_kv, far_proj = lax.optimization_barrier((chunks, far_kv, far_proj))
    came = to_chips(chunks)

    proj = in_order(proj, far_proj, zhi_at)
    proj = lax.all_gather(proj, PLANE, axis=0, tiled=False)
    proj = proj.reshape(*(lax.axis_size(a) for a in (*PLANE, "zhi")), -1, proj.shape[-1])

    kv = in_order(kv, far_kv, y_at & 1)
    far_kv = exchanged(kv, "y", 2)
    mixing = mixing_parts(ids, gate_probs[0].T)
    group_width = width // GROUPS
    own_query = lax.dynamic_slice_in_dim(queries[0], zlo * group_width, group_width, 1)
    near_query = swapped(
        lax.dynamic_slice_in_dim(queries[0], (1 - zlo) * group_width, group_width, 1), "zlo"
    )
    came, far_kv, mixing = lax.optimization_barrier((came, far_kv, mixing))
    kv = in_order(kv, far_kv, y_at >> 1).reshape(-1, 2, GROUPS, HEAD_SIZE)
    near_kv = swapped(lax.dynamic_index_in_dim(kv, 1 - zlo, 2, keepdims=False), "zlo")
    back = expert_back(came, own, other)
    near_kv, own_query, near_query, back = lax.optimization_barrier(
        (near_kv, own_query, near_query, back)
    )
    own_kv = lax.dynamic_index_in_dim(kv, zlo, 2, keepdims=False)
    all_kv = in_order(own_kv, near_kv, zlo)
    key, value = all_kv[:, 0], all_kv[:, 1]
    key_t, value_t = key.T, value.T
    block_heads = out_proj.shape[0] // HEAD_SIZE
    own_row = ((zlo * y_count + y_at) * tokens).astype(jnp.int32).reshape(1)
    near_row = (((1 - zlo) * y_count + y_at) * tokens).astype(jnp.int32).reshape(1)
    own_probs = softmax_probs(own_row, own_query, key_t, block_heads)
    near_probs = softmax_probs(near_row, near_query, key_t, block_heads)

    result = to_chips(back)
    result, own_probs, near_probs = lax.optimization_barrier((result, own_probs, near_probs))
    resid = mix(mixing, out_grad[0], result)
    near_resid = swapped(resid, "zlo")

    proj, _ = lax.optimization_barrier((proj, resid))
    halves = y_count // 2
    dquery, *sums = attention_back(
        resid, proj, own_query, own_probs, key, value_t, 0, y_count, (), False
    )
    near = (near_resid, proj, near_query, near_probs, key, value_t)
    near_first, *sums = attention_back(*near, 0, halves, sums, False)
    near_second, dkv = attention_back(*near, halves, halves, sums, True)
    far_first = swapped(near_first, "zlo")
    dkv, far_first = lax.optimization_barrier((dkv, far_first))
    far_dquery = jnp.concatenate([far_first, swapped(near_second, "zlo")], axis=1)
    dquery = jnp.where(
        zlo == 0,
        jnp.concatenate([dquery, far_dquery], axis=1),
        jnp.concatenate([far_dquery, dquery], axis=1),
    )
    sent = lax.all_to_all(
        dkv.reshape(-1, tokens, 2 * HEAD_SIZE), SEQ, split_axis=0, concat_axis=0, tiled=True
    )
    sent = sent.reshape(GROUPS, y_count, tokens, 2 * HEAD_SIZE)
    sums = jnp.sum(sent.astype(F32), axis=1).astype(BF16)
    dkey = jnp.concatenate([sums[g, :, :HEAD_SIZE] for g in range(GROUPS)], axis=1)
    dvalue = jnp.concatenate([sums[g, :, HEAD_SIZE:] for g in range(GROUPS)], axis=1)
    return resid[None], dquery[None], dkey[None], dvalue[None]


def solution(mesh):
    fine = Mesh(mesh.devices.reshape(2, 4, 2, 4, 2), ("zlo", "y", "zhi", "x", "core"))
    dp = ("zhi", "x", "core")
    token_spec = P(dp, SEQ, None)
    weight_spec = P((*SEQ, *dp), None, None)
    return jax.shard_map(
        body,
        mesh=fine,
        in_specs=(token_spec,) * 5
        + (P(SEQ, dp), token_spec, token_spec, weight_spec, weight_spec, weight_spec),
        out_specs=(token_spec,) * 4,
        check_vma=False,
    )
```

```python
import functools

import jax
import jax.numpy as jnp
import numpy as np
from jax import lax
from jax.experimental import pallas as pl
from jax.experimental.pallas import tpu as pltpu
from jax.sharding import Mesh
from jax.sharding import PartitionSpec as P

HEAD_SIZE = 128
GROUPS = 2
CAPACITY = 5
EXPERTS = 64
SLOTS = EXPERTS * CAPACITY
SEQ = ("zlo", "y")
CHIPS = ("zlo", "y", "zhi", "x")
PLANE = ("y", "x", "core")
BLOCK = 512
PIECES = 8
BATCH = PIECES * CAPACITY
HIDDEN_TILE = 256
VMEM_BYTES = 60 * 1024 * 1024
NT = (((1,), (1,)), ((), ()))
TN = (((0,), (0,)), ((), ()))
F32 = jnp.float32
BF16 = jnp.bfloat16


def chunk_order():
    count = PIECES * BATCH
    row = lax.broadcasted_iota(jnp.int32, (count, 1), 0)
    chip = (row * 1639) >> 16
    rest = row - chip * BATCH
    piece = (rest * 205) >> 10
    moved = piece * BATCH + chip * CAPACITY + rest - piece * CAPACITY
    return jnp.where(
        lax.broadcasted_iota(jnp.int32, (count, count), 1) == moved, 1.0, 0.0
    ).astype(BF16)


def reordered(order, rows):
    return jnp.dot(order, rows, preferred_element_type=F32)


def slot_rows(ids):
    tokens = ids.shape[1]
    expert = lax.broadcasted_iota(jnp.int32, (EXPERTS, tokens), 0)
    chosen = [ids[k : k + 1] for k in range(ids.shape[0])]
    hots = [jnp.where(expert == e, 1.0, 0.0) for e in chosen]
    before = jnp.where(
        lax.broadcasted_iota(jnp.int32, (tokens, tokens), 0)
        < lax.broadcasted_iota(jnp.int32, (tokens, tokens), 1),
        1.0,
        0.0,
    ).astype(BF16)
    earlier = jnp.dot(sum(hots).astype(BF16), before, preferred_element_type=F32)
    return [
        e * CAPACITY + jnp.sum(earlier * hot, axis=0, keepdims=True).astype(jnp.int32)
        for e, hot in zip(chosen, hots)
    ]


def pick_kernel(ids, hidden, grads, out, rows, row_grads, chunks, sems):
    slot = lax.broadcasted_iota(jnp.int32, (SLOTS, ids.shape[1]), 0)
    picking = sum(jnp.where(slot == row, 1.0, 0.0) for row in slot_rows(ids)).astype(BF16)
    for piece in range(PIECES):
        at = slice(piece * BLOCK, (piece + 1) * BLOCK)
        rows[:, at] = jnp.dot(picking, hidden[:, at], preferred_element_type=F32)
        row_grads[:, at] = jnp.dot(picking, grads[:, at], preferred_element_type=F32)
    order = chunk_order()
    leaving = []
    for g in range(SLOTS // BATCH):
        slots = slice(g * BATCH, (g + 1) * BATCH)
        at = slice(g * PIECES * BATCH, (g + 1) * PIECES * BATCH)
        for side, source in enumerate((rows, row_grads)):
            pieces = [source[slots, p * BLOCK : (p + 1) * BLOCK] for p in range(PIECES)]
            sent = reordered(order, jnp.concatenate(pieces, axis=0).astype(BF16))
            chunks[at, side * BLOCK : (side + 1) * BLOCK] = sent.astype(BF16)
        copy = pltpu.make_async_copy(chunks.at[at], out.at[at], sems.at[g])
        copy.start()
        leaving.append(copy)
    for copy in leaving:
        copy.wait()


def pick(ids, hidden, grads):
    width = hidden.shape[1]
    held = pl.BlockSpec(memory_space=pltpu.VMEM)
    return pl.pallas_call(
        pick_kernel,
        in_specs=[held] * 3,
        out_specs=pl.BlockSpec(memory_space=pl.ANY),
        out_shape=jax.ShapeDtypeStruct((EXPERTS * BATCH, 2 * BLOCK), BF16),
        scratch_shapes=[pltpu.VMEM((SLOTS, width), F32)] * 2
        + [
            pltpu.VMEM((EXPERTS * BATCH, 2 * BLOCK), BF16),
            pltpu.SemaphoreType.DMA((SLOTS // BATCH,)),
        ],
        compiler_params=pltpu.CompilerParams(vmem_limit_bytes=VMEM_BYTES),
        cost_estimate=pl.CostEstimate(
            flops=8 * SLOTS * SLOTS * width, bytes_accessed=8 * SLOTS * width, transcendentals=0
        ),
        name="pick",
    )(ids, hidden, grads)


def mixing_kernel(ids, probs, out):
    slot = lax.broadcasted_iota(jnp.int32, (SLOTS, ids.shape[1]), 0)
    mixing = sum(
        jnp.where(slot == row, probs[k : k + 1], 0.0) for k, row in enumerate(slot_rows(ids))
    )
    mixing = jnp.transpose(mixing)
    mixing_high = mixing.astype(BF16)
    out[: ids.shape[1]] = mixing_high
    out[ids.shape[1] :] = (mixing - mixing_high.astype(F32)).astype(BF16)


def mixing_parts(ids, probs):
    held = pl.BlockSpec(memory_space=pltpu.VMEM)
    return pl.pallas_call(
        mixing_kernel,
        in_specs=[held] * 2,
        out_specs=held,
        out_shape=jax.ShapeDtypeStruct((2 * ids.shape[1], SLOTS), BF16),
        compiler_params=pltpu.CompilerParams(vmem_limit_bytes=VMEM_BYTES),
        name="mixing_parts",
    )(ids, probs)


def mix_kernel(mixing, grads, sent, out, came, rows, sems):
    size = PIECES * BATCH
    tokens = out.shape[0]
    arrivals = []
    for g in range(SLOTS // BATCH):
        at = slice(g * size, (g + 1) * size)
        copy = pltpu.make_async_copy(sent.at[at], came.at[at], sems.at[g])
        copy.start()
        arrivals.append(copy)
    order = chunk_order()
    for g in range(SLOTS // BATCH):
        arrivals[g].wait()
        batch = reordered(order, came[g * size : (g + 1) * size])
        for p in range(PIECES):
            rows[g * BATCH : (g + 1) * BATCH, p * BLOCK : (p + 1) * BLOCK] = batch[
                p * BATCH : (p + 1) * BATCH
            ]
    for p in range(PIECES):
        at = slice(p * BLOCK, (p + 1) * BLOCK)
        mixed = jnp.dot(mixing[...], rows[:, at].astype(BF16), preferred_element_type=F32)
        mixed = mixed[:tokens] + mixed[tokens:]
        out[:, at] = (grads[:, at].astype(F32) + mixed).astype(BF16)


def mix(mixing, grads, sent):
    held = pl.BlockSpec(memory_space=pltpu.VMEM)
    return pl.pallas_call(
        mix_kernel,
        in_specs=[held] * 2 + [pl.BlockSpec(memory_space=pl.ANY)],
        out_specs=held,
        out_shape=jax.ShapeDtypeStruct(grads.shape, BF16),
        scratch_shapes=[
            pltpu.VMEM(sent.shape, BF16),
            pltpu.VMEM((SLOTS, grads.shape[1]), F32),
            pltpu.SemaphoreType.DMA((SLOTS // BATCH,)),
        ],
        compiler_params=pltpu.CompilerParams(vmem_limit_bytes=VMEM_BYTES // 2),
        name="mix",
    )(mixing, grads, sent)


def turn_kernel(block, out):
    out[...] = jnp.transpose(block[...])


def turned(block):
    held = pl.BlockSpec(memory_space=pltpu.VMEM)
    return pl.pallas_call(
        turn_kernel,
        in_specs=[held],
        out_specs=held,
        out_shape=jax.ShapeDtypeStruct(block.shape[::-1], block.dtype),
        compiler_params=pltpu.CompilerParams(vmem_limit_bytes=VMEM_BYTES),
        name="turned",
    )(block)


def expert_kernel(
    g0, u0, d0, g1, u1, d1, sent, out, came, rows, grads, gate, up, down, d_gate, d_up, sems, edge_sems
):
    arrival = pltpu.make_async_copy(sent, came, edge_sems.at[0])
    arrival.start()
    halves, width, half = gate.shape
    tile = 512
    loads = []
    for h, (g, u, d) in enumerate(((g0, u0, d0), (g1, u1, d1))):
        for at in range(0, half, HIDDEN_TILE):
            part = slice(at, at + HIDDEN_TILE)
            copies = [
                pltpu.make_async_copy(g.at[0, :, part], gate.at[h, :, part], sems.at[len(loads), 0]),
                pltpu.make_async_copy(u.at[0, :, part], up.at[h, :, part], sems.at[len(loads), 1]),
                pltpu.make_async_copy(d.at[0, part, :], down.at[h, part, :], sems.at[len(loads), 2]),
            ]
            loads.append((h, part, copies))

    def load(number):
        if number < len(loads):
            for copy in loads[number][2]:
                copy.start()

    size = PIECES * BATCH
    order = chunk_order()
    arrival.wait()
    load(0)
    load(1)
    for g in range(0, SLOTS // BATCH, 2):
        batches = [reordered(order, came[(g + i) * size : (g + i + 1) * size]) for i in range(2)]
        slots = slice(g * BATCH, (g + 2) * BATCH)
        for p in range(PIECES):
            pair = [batch[p * BATCH : (p + 1) * BATCH] for batch in batches]
            pair = jnp.concatenate(pair, axis=0).astype(BF16)
            rows[slots, p * BLOCK : (p + 1) * BLOCK] = pair[:, :BLOCK]
            grads[slots, p * BLOCK : (p + 1) * BLOCK] = pair[:, BLOCK:]
    for number, (h, part, copies) in enumerate(loads):
        load(number + 2)
        for copy in copies:
            copy.wait()
        pre_gate = jnp.dot(rows[...], gate[h, :, part], preferred_element_type=F32)
        pre_up = jnp.dot(rows[...], up[h, :, part], preferred_element_type=F32)
        upstream = lax.dot_general(grads[...], down[h, part, :], NT, preferred_element_type=F32)
        sig = jax.nn.sigmoid(pre_gate)
        d_gate[h, :, part] = (upstream * pre_up * sig * (1.0 + pre_gate * (1.0 - sig))).astype(BF16)
        d_up[h, :, part] = (upstream * pre_gate * sig).astype(BF16)

    @pl.loop(0, width // tile)
    def _(i):
        at = pl.ds(pl.multiple_of(i * tile, tile), tile)
        total = lax.dot_general(d_gate[0], gate[0, at, :], NT, preferred_element_type=F32)
        total += lax.dot_general(d_up[0], up[0, at, :], NT, preferred_element_type=F32)
        for h in range(1, halves):
            total += lax.dot_general(d_gate[h], gate[h, at, :], NT, preferred_element_type=F32)
            total += lax.dot_general(d_up[h], up[h, at, :], NT, preferred_element_type=F32)
        rows[:, at] = total.astype(BF16)

    leaving = []
    for g in range(0, SLOTS // BATCH, 2):
        slots = slice(g * BATCH, (g + 2) * BATCH)
        pieces = [rows[slots, p * BLOCK : (p + 1) * BLOCK].astype(F32) for p in range(PIECES)]
        for i in range(2):
            batch = [piece[i * BATCH : (i + 1) * BATCH] for piece in pieces]
            batch = jnp.concatenate(batch, axis=0).astype(BF16)
            at = slice((g + i) * size, (g + i + 1) * size)
            came[at, :BLOCK] = reordered(order, batch).astype(BF16)
            copy = pltpu.make_async_copy(came.at[at, :BLOCK], out.at[at], edge_sems.at[1 + g + i])
            copy.start()
            leaving.append(copy)
    for copy in leaving:
        copy.wait()


def expert_back(sent, own, other):
    width, half = own[0].shape[1:]
    far = pl.BlockSpec(memory_space=pl.ANY)
    return pl.pallas_call(
        expert_kernel,
        in_specs=[far] * 7,
        out_specs=far,
        out_shape=jax.ShapeDtypeStruct((EXPERTS * BATCH, BLOCK), BF16),
        scratch_shapes=[
            pltpu.VMEM(sent.shape, BF16),
            pltpu.VMEM((SLOTS, width), BF16),
            pltpu.VMEM((SLOTS, width), BF16),
            pltpu.VMEM((2, width, half), BF16),
            pltpu.VMEM((2, width, half), BF16),
            pltpu.VMEM((2, half, width), BF16),
            pltpu.VMEM((2, SLOTS, half), BF16),
            pltpu.VMEM((2, SLOTS, half), BF16),
            pltpu.SemaphoreType.DMA((2 * half // HIDDEN_TILE, 3)),
            pltpu.SemaphoreType.DMA((1 + SLOTS // BATCH,)),
        ],
        compiler_params=pltpu.CompilerParams(vmem_limit_bytes=VMEM_BYTES),
        cost_estimate=pl.CostEstimate(
            flops=20 * SLOTS * width * half, bytes_accessed=12 * width * half, transcendentals=0
        ),
        name="expert_back",
    )(*own, *other, sent)


def stack_heads(block):
    heads = block.shape[1] // HEAD_SIZE
    return jnp.concatenate(
        [block[:, h * HEAD_SIZE : (h + 1) * HEAD_SIZE] for h in range(heads)], axis=0
    )


def softmax_kernel(first_row, query, key, probs):
    scale = HEAD_SIZE ** (-0.5)
    tokens = query.shape[0]
    scores = jnp.dot(stack_heads(query[...]), key[...], preferred_element_type=F32) * scale
    row = lax.broadcasted_iota(jnp.int32, scores.shape, 0) % tokens + first_row[0]
    col = lax.broadcasted_iota(jnp.int32, scores.shape, 1)
    scores = jnp.where(col <= row, scores, -1e30)
    weights = jnp.exp(scores - jnp.max(scores, axis=1, keepdims=True))
    probs[...] = (weights / jnp.sum(weights, axis=1, keepdims=True)).astype(BF16)


def softmax_probs(first_row, queries, key, block_heads):
    tokens, width = queries.shape
    length = key.shape[1]
    rows = block_heads * tokens
    steps = width // (block_heads * HEAD_SIZE)
    return pl.pallas_call(
        softmax_kernel,
        grid=(steps,),
        in_specs=[
            pl.BlockSpec(memory_space=pltpu.SMEM),
            pl.BlockSpec((tokens, block_heads * HEAD_SIZE), lambda i: (0, i)),
            pl.BlockSpec((HEAD_SIZE, length), lambda i: (0, 0)),
        ],
        out_specs=pl.BlockSpec((rows, length), lambda i: (i, 0)),
        out_shape=jax.ShapeDtypeStruct((steps * rows, length), BF16),
        compiler_params=pltpu.CompilerParams(vmem_limit_bytes=VMEM_BYTES),
        cost_estimate=pl.CostEstimate(
            flops=20 * steps * rows * length * HEAD_SIZE,
            bytes_accessed=2 * steps * rows * length,
            transcendentals=steps * rows * length,
        ),
        name="softmax_probs",
    )(first_row, queries, key)


def attention_kernel(begins, ends, resid, proj, query, probs, key, value_t, *refs):
    steps = pl.num_programs(0)
    if not begins:
        dkey_in, dvalue_in = refs[:2]
        refs = refs[2:]
    if ends:
        dquery, dkv, dkey, dvalue = refs
    else:
        dquery, dkey, dvalue = refs
    step = pl.program_id(0)
    scale = HEAD_SIZE ** (-0.5)
    tokens = query.shape[0]
    x_count, core_count, zhi_count, depth, block_cols = proj.shape[1:]

    @pl.when(step == 0)
    def _():
        if begins:
            dkey[...] = jnp.zeros_like(dkey)
            dvalue[...] = jnp.zeros_like(dvalue)
        else:
            dkey[...] = dkey_in[...]
            dvalue[...] = dvalue_in[...]

    ctx = jnp.zeros((tokens, block_cols), F32)
    for x in range(x_count):
        for core in range(core_count):
            for zhi in range(zhi_count):
                at = ((zhi * x_count + x) * core_count + core) * depth
                ctx += jnp.dot(
                    resid[:, at : at + depth], proj[0, x, core, zhi], preferred_element_type=F32
                )
    ctx = stack_heads(ctx.astype(BF16))
    query_rows = stack_heads(query[...])
    low = probs[...]
    weights = low.astype(F32)
    dprobs = jnp.dot(ctx, value_t[...], preferred_element_type=F32)
    delta = jnp.sum(weights * dprobs, axis=1, keepdims=True)
    dscores = (weights * (dprobs - delta)).astype(BF16)
    dq = jnp.dot(dscores, key[...], preferred_element_type=F32) * scale
    for h in range(query.shape[1] // HEAD_SIZE):
        dquery[:, h * HEAD_SIZE : (h + 1) * HEAD_SIZE] = dq[h * tokens : (h + 1) * tokens].astype(
            BF16
        )
    dkey[...] += lax.dot_general(query_rows, dscores, TN, preferred_element_type=F32)
    dvalue[...] += lax.dot_general(ctx, low, TN, preferred_element_type=F32)

    if ends:

        @pl.when(step == steps - 1)
        def _():
            dkv[:, :HEAD_SIZE] = jnp.transpose(dkey[...] * scale).astype(BF16)
            dkv[:, HEAD_SIZE:] = jnp.transpose(dvalue[...]).astype(BF16)


def attention_back(resid, proj, queries, probs, key, value_t, first, steps, carried, ends):
    tokens, width = resid.shape
    block_cols = proj.shape[-1]
    length = key.shape[0]
    rows = tokens * block_cols // HEAD_SIZE

    def whole(*shape):
        return pl.BlockSpec(shape, lambda i: (0,) * len(shape))

    in_specs = [
        whole(tokens, width),
        pl.BlockSpec((1, *proj.shape[1:]), lambda i: (first + i, 0, 0, 0, 0, 0)),
        pl.BlockSpec((tokens, block_cols), lambda i: (0, first + i)),
        pl.BlockSpec((rows, length), lambda i: (first + i, 0)),
        whole(length, HEAD_SIZE),
        whole(HEAD_SIZE, length),
    ]
    in_specs += [whole(HEAD_SIZE, length)] * len(carried)
    sums = jax.ShapeDtypeStruct((HEAD_SIZE, length), F32)
    out_specs = [pl.BlockSpec((tokens, block_cols), lambda i: (0, i))]
    out_shape = [jax.ShapeDtypeStruct((tokens, steps * block_cols), BF16)]
    scratch = []
    if ends:
        out_specs += [whole(length, 2 * HEAD_SIZE)]
        out_shape += [jax.ShapeDtypeStruct((length, 2 * HEAD_SIZE), BF16)]
        scratch = [pltpu.VMEM((HEAD_SIZE, length), F32)] * 2
    else:
        out_specs += [whole(HEAD_SIZE, length)] * 2
        out_shape += [sums, sums]
    return pl.pallas_call(
        functools.partial(attention_kernel, not carried, ends),
        grid=(steps,),
        in_specs=in_specs,
        out_specs=out_specs,
        scratch_shapes=scratch,
        out_shape=out_shape,
        compiler_params=pltpu.CompilerParams(vmem_limit_bytes=VMEM_BYTES * 3 // 4),
        cost_estimate=pl.CostEstimate(
            flops=2 * steps * rows * (5 * length * HEAD_SIZE + width * HEAD_SIZE),
            bytes_accessed=steps * (2 * width * block_cols + 2 * rows * length),
            transcendentals=0,
        ),
        name="attention_back",
    )(resid, proj, queries, probs, key, value_t, *carried)


def swapped(block, axis):
    return lax.ppermute(block, axis, [(0, 1), (1, 0)])


def exchanged(block, axis, mask):
    return lax.ppermute(block, axis, [(i, i ^ mask) for i in range(lax.axis_size(axis))])


def in_order(own, other, place):
    return jnp.where(
        place == 0,
        jnp.concatenate([own, other], axis=0),
        jnp.concatenate([other, own], axis=0),
    )


def to_chips(chunks):
    sent = chunks.reshape(EXPERTS, BATCH, -1)
    return lax.all_to_all(sent, CHIPS, split_axis=0, concat_axis=0, tiled=True).reshape(
        chunks.shape
    )


def body(
    hidden_in,
    out_grad,
    queries,
    keys,
    values,
    out_proj,
    expert_ids,
    gate_probs,
    w_gate,
    w_up,
    w_down,
):
    tokens, width = hidden_in.shape[1:]
    zlo = lax.axis_index("zlo")
    y_at = lax.axis_index("y")
    y_count = lax.axis_size("y")
    zhi_at = lax.axis_index("zhi")
    own = (w_gate, w_up, w_down)
    other = tuple(swapped(w, "core") for w in own)

    ids = expert_ids[0].T

    proj = turned(out_proj)
    far_proj = exchanged(proj, "zhi", 1)

    kv = jnp.concatenate([keys[0], values[0]], axis=1)
    far_kv = exchanged(kv, "y", 1)

    chunks = pick(ids, hidden_in[0], out_grad[0])
    chunks, far_kv, far_proj = lax.optimization_barrier((chunks, far_kv, far_proj))
    came = to_chips(chunks)

    proj = in_order(proj, far_proj, zhi_at)
    proj = lax.all_gather(proj, PLANE, axis=0, tiled=False)
    proj = proj.reshape(*(lax.axis_size(a) for a in (*PLANE, "zhi")), -1, proj.shape[-1])

    kv = in_order(kv, far_kv, y_at & 1)
    far_kv = exchanged(kv, "y", 2)
    mixing = mixing_parts(ids, gate_probs[0].T)
    group_width = width // GROUPS
    own_query = lax.dynamic_slice_in_dim(queries[0], zlo * group_width, group_width, 1)
    near_query = swapped(
        lax.dynamic_slice_in_dim(queries[0], (1 - zlo) * group_width, group_width, 1), "zlo"
    )
    came, far_kv, mixing = lax.optimization_barrier((came, far_kv, mixing))
    kv = in_order(kv, far_kv, y_at >> 1).reshape(-1, 2, GROUPS, HEAD_SIZE)
    near_kv = swapped(lax.dynamic_index_in_dim(kv, 1 - zlo, 2, keepdims=False), "zlo")
    back = expert_back(came, own, other)
    near_kv, own_query, near_query, back = lax.optimization_barrier(
        (near_kv, own_query, near_query, back)
    )
    own_kv = lax.dynamic_index_in_dim(kv, zlo, 2, keepdims=False)
    all_kv = in_order(own_kv, near_kv, zlo)
    key, value = all_kv[:, 0], all_kv[:, 1]
    key_t, value_t = key.T, value.T
    block_heads = out_proj.shape[0] // HEAD_SIZE
    own_row = ((zlo * y_count + y_at) * tokens).astype(jnp.int32).reshape(1)
    near_row = (((1 - zlo) * y_count + y_at) * tokens).astype(jnp.int32).reshape(1)
    own_probs = softmax_probs(own_row, own_query, key_t, block_heads)
    near_probs = softmax_probs(near_row, near_query, key_t, block_heads)

    result = to_chips(back)
    result, own_probs, near_probs = lax.optimization_barrier((result, own_probs, near_probs))
    resid = mix(mixing, out_grad[0], result)
    near_resid = swapped(resid, "zlo")

    proj, _ = lax.optimization_barrier((proj, resid))
    halves = y_count // 2
    dquery, *sums = attention_back(
        resid, proj, own_query, own_probs, key, value_t, 0, y_count, (), False
    )
    near = (near_resid, proj, near_query, near_probs, key, value_t)
    near_first, *sums = attention_back(*near, 0, halves, sums, False)
    near_second, dkv = attention_back(*near, halves, halves, sums, True)
    far_first = swapped(near_first, "zlo")
    dkv, far_first = lax.optimization_barrier((dkv, far_first))
    far_dquery = jnp.concatenate([far_first, swapped(near_second, "zlo")], axis=1)
    dquery = jnp.where(
        zlo == 0,
        jnp.concatenate([dquery, far_dquery], axis=1),
        jnp.concatenate([far_dquery, dquery], axis=1),
    )
    sent = lax.all_to_all(
        dkv.reshape(-1, tokens, 2 * HEAD_SIZE), SEQ, split_axis=0, concat_axis=0, tiled=True
    )
    sent = sent.reshape(GROUPS, y_count, tokens, 2 * HEAD_SIZE)
    sums = jnp.sum(sent.astype(F32), axis=1).astype(BF16)
    dkey = jnp.concatenate([sums[g, :, :HEAD_SIZE] for g in range(GROUPS)], axis=1)
    dvalue = jnp.concatenate([sums[g, :, HEAD_SIZE:] for g in range(GROUPS)], axis=1)
    return resid[None], dquery[None], dkey[None], dvalue[None]


def solution(mesh):
    fine = Mesh(mesh.devices.reshape(2, 4, 2, 4, 2), ("zlo", "y", "zhi", "x", "core"))
    dp = ("zhi", "x", "core")
    token_spec = P(dp, SEQ, None)
    weight_spec = P((*SEQ, *dp), None, None)
    return jax.shard_map(
        body,
        mesh=fine,
        in_specs=(token_spec,) * 5
        + (P(SEQ, dp), token_spec, token_spec, weight_spec, weight_spec, weight_spec),
        out_specs=(token_spec,) * 4,
        check_vma=False,
    )
```

```python
import functools

import jax
import jax.numpy as jnp
import numpy as np
from jax import lax
from jax.experimental import pallas as pl
from jax.experimental.pallas import tpu as pltpu
from jax.sharding import Mesh
from jax.sharding import PartitionSpec as P

HEAD_SIZE = 128
GROUPS = 2
CAPACITY = 5
EXPERTS = 64
SLOTS = EXPERTS * CAPACITY
SEQ = ("zlo", "y")
CHIPS = ("zlo", "y", "zhi", "x")
PLANE = ("y", "x", "core")
BLOCK = 512
PIECES = 8
BATCH = PIECES * CAPACITY
HIDDEN_TILE = 256
VMEM_BYTES = 60 * 1024 * 1024
NT = (((1,), (1,)), ((), ()))
TN = (((0,), (0,)), ((), ()))
F32 = jnp.float32
BF16 = jnp.bfloat16


def chunk_order():
    count = PIECES * BATCH
    row = lax.broadcasted_iota(jnp.int32, (count, 1), 0)
    chip = (row * 1639) >> 16
    rest = row - chip * BATCH
    piece = (rest * 205) >> 10
    moved = piece * BATCH + chip * CAPACITY + rest - piece * CAPACITY
    return jnp.where(
        lax.broadcasted_iota(jnp.int32, (count, count), 1) == moved, 1.0, 0.0
    ).astype(BF16)


def reordered(order, rows):
    return jnp.dot(order, rows, preferred_element_type=F32)


def slot_rows(ids):
    tokens = ids.shape[1]
    expert = lax.broadcasted_iota(jnp.int32, (EXPERTS, tokens), 0)
    chosen = [ids[k : k + 1] for k in range(ids.shape[0])]
    hots = [jnp.where(expert == e, 1.0, 0.0) for e in chosen]
    before = jnp.where(
        lax.broadcasted_iota(jnp.int32, (tokens, tokens), 0)
        < lax.broadcasted_iota(jnp.int32, (tokens, tokens), 1),
        1.0,
        0.0,
    ).astype(BF16)
    earlier = jnp.dot(sum(hots).astype(BF16), before, preferred_element_type=F32)
    return [
        e * CAPACITY + jnp.sum(earlier * hot, axis=0, keepdims=True).astype(jnp.int32)
        for e, hot in zip(chosen, hots)
    ]


def pick_kernel(ids, hidden, grads, out, rows, row_grads, chunks, sems):
    slot = lax.broadcasted_iota(jnp.int32, (SLOTS, ids.shape[1]), 0)
    picking = sum(jnp.where(slot == row, 1.0, 0.0) for row in slot_rows(ids)).astype(BF16)
    for piece in range(PIECES):
        at = slice(piece * BLOCK, (piece + 1) * BLOCK)
        rows[:, at] = jnp.dot(picking, hidden[:, at], preferred_element_type=F32)
        row_grads[:, at] = jnp.dot(picking, grads[:, at], preferred_element_type=F32)
    order = chunk_order()
    leaving = []
    for g in range(SLOTS // BATCH):
        slots = slice(g * BATCH, (g + 1) * BATCH)
        at = slice(g * PIECES * BATCH, (g + 1) * PIECES * BATCH)
        for side, source in enumerate((rows, row_grads)):
            pieces = [source[slots, p * BLOCK : (p + 1) * BLOCK] for p in range(PIECES)]
            sent = reordered(order, jnp.concatenate(pieces, axis=0).astype(BF16))
            chunks[at, side * BLOCK : (side + 1) * BLOCK] = sent.astype(BF16)
        copy = pltpu.make_async_copy(chunks.at[at], out.at[at], sems.at[g])
        copy.start()
        leaving.append(copy)
    for copy in leaving:
        copy.wait()


def pick(ids, hidden, grads):
    width = hidden.shape[1]
    held = pl.BlockSpec(memory_space=pltpu.VMEM)
    return pl.pallas_call(
        pick_kernel,
        in_specs=[held] * 3,
        out_specs=pl.BlockSpec(memory_space=pl.ANY),
        out_shape=jax.ShapeDtypeStruct((EXPERTS * BATCH, 2 * BLOCK), BF16),
        scratch_shapes=[pltpu.VMEM((SLOTS, width), F32)] * 2
        + [
            pltpu.VMEM((EXPERTS * BATCH, 2 * BLOCK), BF16),
            pltpu.SemaphoreType.DMA((SLOTS // BATCH,)),
        ],
        compiler_params=pltpu.CompilerParams(vmem_limit_bytes=VMEM_BYTES),
        cost_estimate=pl.CostEstimate(
            flops=8 * SLOTS * SLOTS * width, bytes_accessed=8 * SLOTS * width, transcendentals=0
        ),
        name="pick",
    )(ids, hidden, grads)


def mixing_kernel(ids, probs, out):
    slot = lax.broadcasted_iota(jnp.int32, (SLOTS, ids.shape[1]), 0)
    mixing = sum(
        jnp.where(slot == row, probs[k : k + 1], 0.0) for k, row in enumerate(slot_rows(ids))
    )
    mixing = jnp.transpose(mixing)
    mixing_high = mixing.astype(BF16)
    out[: ids.shape[1]] = mixing_high
    out[ids.shape[1] :] = (mixing - mixing_high.astype(F32)).astype(BF16)


def mixing_parts(ids, probs):
    held = pl.BlockSpec(memory_space=pltpu.VMEM)
    return pl.pallas_call(
        mixing_kernel,
        in_specs=[held] * 2,
        out_specs=held,
        out_shape=jax.ShapeDtypeStruct((2 * ids.shape[1], SLOTS), BF16),
        compiler_params=pltpu.CompilerParams(vmem_limit_bytes=VMEM_BYTES),
        name="mixing_parts",
    )(ids, probs)


def mix_kernel(mixing, grads, sent, out, came, rows, sems):
    size = PIECES * BATCH
    tokens = out.shape[0]
    arrivals = []
    for g in range(SLOTS // BATCH):
        at = slice(g * size, (g + 1) * size)
        copy = pltpu.make_async_copy(sent.at[at], came.at[at], sems.at[g])
        copy.start()
        arrivals.append(copy)
    order = chunk_order()
    for g in range(SLOTS // BATCH):
        arrivals[g].wait()
        batch = reordered(order, came[g * size : (g + 1) * size])
        for p in range(PIECES):
            rows[g * BATCH : (g + 1) * BATCH, p * BLOCK : (p + 1) * BLOCK] = batch[
                p * BATCH : (p + 1) * BATCH
            ]
    for p in range(PIECES):
        at = slice(p * BLOCK, (p + 1) * BLOCK)
        mixed = jnp.dot(mixing[...], rows[:, at].astype(BF16), preferred_element_type=F32)
        mixed = mixed[:tokens] + mixed[tokens:]
        out[:, at] = (grads[:, at].astype(F32) + mixed).astype(BF16)


def mix(mixing, grads, sent):
    held = pl.BlockSpec(memory_space=pltpu.VMEM)
    return pl.pallas_call(
        mix_kernel,
        in_specs=[held] * 2 + [pl.BlockSpec(memory_space=pl.ANY)],
        out_specs=held,
        out_shape=jax.ShapeDtypeStruct(grads.shape, BF16),
        scratch_shapes=[
            pltpu.VMEM(sent.shape, BF16),
            pltpu.VMEM((SLOTS, grads.shape[1]), F32),
            pltpu.SemaphoreType.DMA((SLOTS // BATCH,)),
        ],
        compiler_params=pltpu.CompilerParams(vmem_limit_bytes=VMEM_BYTES // 2),
        name="mix",
    )(mixing, grads, sent)


def turn_kernel(block, out):
    out[...] = jnp.transpose(block[...])


def turned(block):
    held = pl.BlockSpec(memory_space=pltpu.VMEM)
    return pl.pallas_call(
        turn_kernel,
        in_specs=[held],
        out_specs=held,
        out_shape=jax.ShapeDtypeStruct(block.shape[::-1], block.dtype),
        compiler_params=pltpu.CompilerParams(vmem_limit_bytes=VMEM_BYTES),
        name="turned",
    )(block)


def expert_kernel(
    g0, u0, d0, g1, u1, d1, sent, out, came, rows, grads, gate, up, down, d_gate, d_up, sems, edge_sems
):
    arrival = pltpu.make_async_copy(sent, came, edge_sems.at[0])
    arrival.start()
    halves, width, half = gate.shape
    tile = 1024
    loads = []
    for h, (g, u, d) in enumerate(((g0, u0, d0), (g1, u1, d1))):
        for at in range(0, half, HIDDEN_TILE):
            part = slice(at, at + HIDDEN_TILE)
            copies = [
                pltpu.make_async_copy(g.at[0, :, part], gate.at[h, :, part], sems.at[len(loads), 0]),
                pltpu.make_async_copy(u.at[0, :, part], up.at[h, :, part], sems.at[len(loads), 1]),
                pltpu.make_async_copy(d.at[0, part, :], down.at[h, part, :], sems.at[len(loads), 2]),
            ]
            loads.append((h, part, copies))

    def load(number):
        if number < len(loads):
            for copy in loads[number][2]:
                copy.start()

    size = PIECES * BATCH
    order = chunk_order()
    arrival.wait()
    load(0)
    load(1)
    for g in range(0, SLOTS // BATCH, 2):
        batches = [reordered(order, came[(g + i) * size : (g + i + 1) * size]) for i in range(2)]
        slots = slice(g * BATCH, (g + 2) * BATCH)
        for p in range(PIECES):
            pair = [batch[p * BATCH : (p + 1) * BATCH] for batch in batches]
            pair = jnp.concatenate(pair, axis=0).astype(BF16)
            rows[slots, p * BLOCK : (p + 1) * BLOCK] = pair[:, :BLOCK]
            grads[slots, p * BLOCK : (p + 1) * BLOCK] = pair[:, BLOCK:]
    for number, (h, part, copies) in enumerate(loads):
        load(number + 2)
        for copy in copies:
            copy.wait()
        pre_gate = jnp.dot(rows[...], gate[h, :, part], preferred_element_type=F32)
        pre_up = jnp.dot(rows[...], up[h, :, part], preferred_element_type=F32)
        upstream = lax.dot_general(grads[...], down[h, part, :], NT, preferred_element_type=F32)
        sig = jax.nn.sigmoid(pre_gate)
        d_gate[h, :, part] = (upstream * pre_up * sig * (1.0 + pre_gate * (1.0 - sig))).astype(BF16)
        d_up[h, :, part] = (upstream * pre_gate * sig).astype(BF16)

    @pl.loop(0, width // tile)
    def _(i):
        at = pl.ds(pl.multiple_of(i * tile, tile), tile)
        total = lax.dot_general(d_gate[0], gate[0, at, :], NT, preferred_element_type=F32)
        total += lax.dot_general(d_up[0], up[0, at, :], NT, preferred_element_type=F32)
        for h in range(1, halves):
            total += lax.dot_general(d_gate[h], gate[h, at, :], NT, preferred_element_type=F32)
            total += lax.dot_general(d_up[h], up[h, at, :], NT, preferred_element_type=F32)
        rows[:, at] = total.astype(BF16)

    leaving = []
    for g in range(0, SLOTS // BATCH, 2):
        slots = slice(g * BATCH, (g + 2) * BATCH)
        pieces = [rows[slots, p * BLOCK : (p + 1) * BLOCK].astype(F32) for p in range(PIECES)]
        for i in range(2):
            batch = [piece[i * BATCH : (i + 1) * BATCH] for piece in pieces]
            batch = jnp.concatenate(batch, axis=0).astype(BF16)
            at = slice((g + i) * size, (g + i + 1) * size)
            came[at, :BLOCK] = reordered(order, batch).astype(BF16)
            copy = pltpu.make_async_copy(came.at[at, :BLOCK], out.at[at], edge_sems.at[1 + g + i])
            copy.start()
            leaving.append(copy)
    for copy in leaving:
        copy.wait()


def expert_back(sent, own, other):
    width, half = own[0].shape[1:]
    far = pl.BlockSpec(memory_space=pl.ANY)
    return pl.pallas_call(
        expert_kernel,
        in_specs=[far] * 7,
        out_specs=far,
        out_shape=jax.ShapeDtypeStruct((EXPERTS * BATCH, BLOCK), BF16),
        scratch_shapes=[
            pltpu.VMEM(sent.shape, BF16),
            pltpu.VMEM((SLOTS, width), BF16),
            pltpu.VMEM((SLOTS, width), BF16),
            pltpu.VMEM((2, width, half), BF16),
            pltpu.VMEM((2, width, half), BF16),
            pltpu.VMEM((2, half, width), BF16),
            pltpu.VMEM((2, SLOTS, half), BF16),
            pltpu.VMEM((2, SLOTS, half), BF16),
            pltpu.SemaphoreType.DMA((2 * half // HIDDEN_TILE, 3)),
            pltpu.SemaphoreType.DMA((1 + SLOTS // BATCH,)),
        ],
        compiler_params=pltpu.CompilerParams(vmem_limit_bytes=VMEM_BYTES),
        cost_estimate=pl.CostEstimate(
            flops=20 * SLOTS * width * half, bytes_accessed=12 * width * half, transcendentals=0
        ),
        name="expert_back",
    )(*own, *other, sent)


def stack_heads(block):
    heads = block.shape[1] // HEAD_SIZE
    return jnp.concatenate(
        [block[:, h * HEAD_SIZE : (h + 1) * HEAD_SIZE] for h in range(heads)], axis=0
    )


def softmax_kernel(first_row, query, key, probs):
    scale = HEAD_SIZE ** (-0.5)
    tokens = query.shape[0]
    scores = jnp.dot(stack_heads(query[...]), key[...], preferred_element_type=F32) * scale
    row = lax.broadcasted_iota(jnp.int32, scores.shape, 0) % tokens + first_row[0]
    col = lax.broadcasted_iota(jnp.int32, scores.shape, 1)
    scores = jnp.where(col <= row, scores, -1e30)
    weights = jnp.exp(scores - jnp.max(scores, axis=1, keepdims=True))
    probs[...] = (weights / jnp.sum(weights, axis=1, keepdims=True)).astype(BF16)


def softmax_probs(first_row, queries, key, block_heads):
    tokens, width = queries.shape
    length = key.shape[1]
    rows = block_heads * tokens
    steps = width // (block_heads * HEAD_SIZE)
    return pl.pallas_call(
        softmax_kernel,
        grid=(steps,),
        in_specs=[
            pl.BlockSpec(memory_space=pltpu.SMEM),
            pl.BlockSpec((tokens, block_heads * HEAD_SIZE), lambda i: (0, i)),
            pl.BlockSpec((HEAD_SIZE, length), lambda i: (0, 0)),
        ],
        out_specs=pl.BlockSpec((rows, length), lambda i: (i, 0)),
        out_shape=jax.ShapeDtypeStruct((steps * rows, length), BF16),
        compiler_params=pltpu.CompilerParams(vmem_limit_bytes=VMEM_BYTES),
        cost_estimate=pl.CostEstimate(
            flops=20 * steps * rows * length * HEAD_SIZE,
            bytes_accessed=2 * steps * rows * length,
            transcendentals=steps * rows * length,
        ),
        name="softmax_probs",
    )(first_row, queries, key)


def attention_kernel(begins, ends, resid, proj, query, probs, key, value_t, *refs):
    steps = pl.num_programs(0)
    if not begins:
        dkey_in, dvalue_in = refs[:2]
        refs = refs[2:]
    if ends:
        dquery, dkv, dkey, dvalue = refs
    else:
        dquery, dkey, dvalue = refs
    step = pl.program_id(0)
    scale = HEAD_SIZE ** (-0.5)
    tokens = query.shape[0]
    x_count, core_count, zhi_count, depth, block_cols = proj.shape[1:]

    @pl.when(step == 0)
    def _():
        if begins:
            dkey[...] = jnp.zeros_like(dkey)
            dvalue[...] = jnp.zeros_like(dvalue)
        else:
            dkey[...] = dkey_in[...]
            dvalue[...] = dvalue_in[...]

    ctx = jnp.zeros((tokens, block_cols), F32)
    for x in range(x_count):
        for core in range(core_count):
            for zhi in range(zhi_count):
                at = ((zhi * x_count + x) * core_count + core) * depth
                ctx += jnp.dot(
                    resid[:, at : at + depth], proj[0, x, core, zhi], preferred_element_type=F32
                )
    ctx = stack_heads(ctx.astype(BF16))
    query_rows = stack_heads(query[...])
    low = probs[...]
    weights = low.astype(F32)
    dprobs = jnp.dot(ctx, value_t[...], preferred_element_type=F32)
    delta = jnp.sum(weights * dprobs, axis=1, keepdims=True)
    dscores = (weights * (dprobs - delta)).astype(BF16)
    dq = jnp.dot(dscores, key[...], preferred_element_type=F32) * scale
    for h in range(query.shape[1] // HEAD_SIZE):
        dquery[:, h * HEAD_SIZE : (h + 1) * HEAD_SIZE] = dq[h * tokens : (h + 1) * tokens].astype(
            BF16
        )
    dkey[...] += lax.dot_general(query_rows, dscores, TN, preferred_element_type=F32)
    dvalue[...] += lax.dot_general(ctx, low, TN, preferred_element_type=F32)

    if ends:

        @pl.when(step == steps - 1)
        def _():
            dkv[:, :HEAD_SIZE] = jnp.transpose(dkey[...] * scale).astype(BF16)
            dkv[:, HEAD_SIZE:] = jnp.transpose(dvalue[...]).astype(BF16)


def attention_back(resid, proj, queries, probs, key, value_t, first, steps, carried, ends):
    tokens, width = resid.shape
    block_cols = proj.shape[-1]
    length = key.shape[0]
    rows = tokens * block_cols // HEAD_SIZE

    def whole(*shape):
        return pl.BlockSpec(shape, lambda i: (0,) * len(shape))

    in_specs = [
        whole(tokens, width),
        pl.BlockSpec((1, *proj.shape[1:]), lambda i: (first + i, 0, 0, 0, 0, 0)),
        pl.BlockSpec((tokens, block_cols), lambda i: (0, first + i)),
        pl.BlockSpec((rows, length), lambda i: (first + i, 0)),
        whole(length, HEAD_SIZE),
        whole(HEAD_SIZE, length),
    ]
    in_specs += [whole(HEAD_SIZE, length)] * len(carried)
    sums = jax.ShapeDtypeStruct((HEAD_SIZE, length), F32)
    out_specs = [pl.BlockSpec((tokens, block_cols), lambda i: (0, i))]
    out_shape = [jax.ShapeDtypeStruct((tokens, steps * block_cols), BF16)]
    scratch = []
    if ends:
        out_specs += [whole(length, 2 * HEAD_SIZE)]
        out_shape += [jax.ShapeDtypeStruct((length, 2 * HEAD_SIZE), BF16)]
        scratch = [pltpu.VMEM((HEAD_SIZE, length), F32)] * 2
    else:
        out_specs += [whole(HEAD_SIZE, length)] * 2
        out_shape += [sums, sums]
    return pl.pallas_call(
        functools.partial(attention_kernel, not carried, ends),
        grid=(steps,),
        in_specs=in_specs,
        out_specs=out_specs,
        scratch_shapes=scratch,
        out_shape=out_shape,
        compiler_params=pltpu.CompilerParams(vmem_limit_bytes=VMEM_BYTES * 3 // 4),
        cost_estimate=pl.CostEstimate(
            flops=2 * steps * rows * (5 * length * HEAD_SIZE + width * HEAD_SIZE),
            bytes_accessed=steps * (2 * width * block_cols + 2 * rows * length),
            transcendentals=0,
        ),
        name="attention_back",
    )(resid, proj, queries, probs, key, value_t, *carried)


def swapped(block, axis):
    return lax.ppermute(block, axis, [(0, 1), (1, 0)])


def exchanged(block, axis, mask):
    return lax.ppermute(block, axis, [(i, i ^ mask) for i in range(lax.axis_size(axis))])


def in_order(own, other, place):
    return jnp.where(
        place == 0,
        jnp.concatenate([own, other], axis=0),
        jnp.concatenate([other, own], axis=0),
    )


def to_chips(chunks):
    sent = chunks.reshape(EXPERTS, BATCH, -1)
    return lax.all_to_all(sent, CHIPS, split_axis=0, concat_axis=0, tiled=True).reshape(
        chunks.shape
    )


def body(
    hidden_in,
    out_grad,
    queries,
    keys,
    values,
    out_proj,
    expert_ids,
    gate_probs,
    w_gate,
    w_up,
    w_down,
):
    tokens, width = hidden_in.shape[1:]
    zlo = lax.axis_index("zlo")
    y_at = lax.axis_index("y")
    y_count = lax.axis_size("y")
    zhi_at = lax.axis_index("zhi")
    own = (w_gate, w_up, w_down)
    other = tuple(swapped(w, "core") for w in own)

    ids = expert_ids[0].T

    proj = turned(out_proj)
    far_proj = exchanged(proj, "zhi", 1)

    kv = jnp.concatenate([keys[0], values[0]], axis=1)
    far_kv = exchanged(kv, "y", 1)

    chunks = pick(ids, hidden_in[0], out_grad[0])
    chunks, far_kv, far_proj = lax.optimization_barrier((chunks, far_kv, far_proj))
    came = to_chips(chunks)

    proj = in_order(proj, far_proj, zhi_at)
    proj = lax.all_gather(proj, PLANE, axis=0, tiled=False)
    proj = proj.reshape(*(lax.axis_size(a) for a in (*PLANE, "zhi")), -1, proj.shape[-1])

    kv = in_order(kv, far_kv, y_at & 1)
    far_kv = exchanged(kv, "y", 2)
    mixing = mixing_parts(ids, gate_probs[0].T)
    group_width = width // GROUPS
    own_query = lax.dynamic_slice_in_dim(queries[0], zlo * group_width, group_width, 1)
    near_query = swapped(
        lax.dynamic_slice_in_dim(queries[0], (1 - zlo) * group_width, group_width, 1), "zlo"
    )
    came, far_kv, mixing = lax.optimization_barrier((came, far_kv, mixing))
    kv = in_order(kv, far_kv, y_at >> 1).reshape(-1, 2, GROUPS, HEAD_SIZE)
    near_kv = swapped(lax.dynamic_index_in_dim(kv, 1 - zlo, 2, keepdims=False), "zlo")
    back = expert_back(came, own, other)
    near_kv, own_query, near_query, back = lax.optimization_barrier(
        (near_kv, own_query, near_query, back)
    )
    own_kv = lax.dynamic_index_in_dim(kv, zlo, 2, keepdims=False)
    all_kv = in_order(own_kv, near_kv, zlo)
    key, value = all_kv[:, 0], all_kv[:, 1]
    key_t, value_t = key.T, value.T
    block_heads = out_proj.shape[0] // HEAD_SIZE
    own_row = ((zlo * y_count + y_at) * tokens).astype(jnp.int32).reshape(1)
    near_row = (((1 - zlo) * y_count + y_at) * tokens).astype(jnp.int32).reshape(1)
    own_probs = softmax_probs(own_row, own_query, key_t, block_heads)
    near_probs = softmax_probs(near_row, near_query, key_t, block_heads)

    result = to_chips(back)
    result, own_probs, near_probs = lax.optimization_barrier((result, own_probs, near_probs))
    resid = mix(mixing, out_grad[0], result)
    near_resid = swapped(resid, "zlo")

    proj, _ = lax.optimization_barrier((proj, resid))
    halves = y_count // 2
    dquery, *sums = attention_back(
        resid, proj, own_query, own_probs, key, value_t, 0, y_count, (), False
    )
    near = (near_resid, proj, near_query, near_probs, key, value_t)
    near_first, *sums = attention_back(*near, 0, halves, sums, False)
    near_second, dkv = attention_back(*near, halves, halves, sums, True)
    far_first = swapped(near_first, "zlo")
    dkv, far_first = lax.optimization_barrier((dkv, far_first))
    far_dquery = jnp.concatenate([far_first, swapped(near_second, "zlo")], axis=1)
    dquery = jnp.where(
        zlo == 0,
        jnp.concatenate([dquery, far_dquery], axis=1),
        jnp.concatenate([far_dquery, dquery], axis=1),
    )
    sent = lax.all_to_all(
        dkv.reshape(-1, tokens, 2 * HEAD_SIZE), SEQ, split_axis=0, concat_axis=0, tiled=True
    )
    sent = sent.reshape(GROUPS, y_count, tokens, 2 * HEAD_SIZE)
    sums = jnp.sum(sent.astype(F32), axis=1).astype(BF16)
    dkey = jnp.concatenate([sums[g, :, :HEAD_SIZE] for g in range(GROUPS)], axis=1)
    dvalue = jnp.concatenate([sums[g, :, HEAD_SIZE:] for g in range(GROUPS)], axis=1)
    return resid[None], dquery[None], dkey[None], dvalue[None]


def solution(mesh):
    fine = Mesh(mesh.devices.reshape(2, 4, 2, 4, 2), ("zlo", "y", "zhi", "x", "core"))
    dp = ("zhi", "x", "core")
    token_spec = P(dp, SEQ, None)
    weight_spec = P((*SEQ, *dp), None, None)
    return jax.shard_map(
        body,
        mesh=fine,
        in_specs=(token_spec,) * 5
        + (P(SEQ, dp), token_spec, token_spec, weight_spec, weight_spec, weight_spec),
        out_specs=(token_spec,) * 4,
        check_vma=False,
    )
```
